32 devices in a mesh: batch: 16 (over z, y, core), seq: 2 (over x).
Axes of the slice: x: 2, y: 2, z: 4, core: 2. Of those that a mesh axis runs over, the one named last changes fastest.
Arguments:
- tokens: bfloat16 [48, 1024, 1024], P('batch', 'seq'), may hold values from -6 to 6
- cotangent: bfloat16 [48, 1024, 1024], P('batch', 'seq'), may hold values from -6 to 6
- layout: int32 [4], replicated, may hold values from 0 to 3, each once
- attention_norm_gain: float32 [1024], replicated, may hold values from 0.1 to 1.9
- feedforward_norm_gain: float32 [1024], replicated, may hold values from 0.1 to 1.9
- query_weight: bfloat16 [1024, 1024], P('batch'), may hold values from -0.25 to 0.25
- key_weight: bfloat16 [1024, 1024], P('batch'), may hold values from -0.25 to 0.25
- value_weight: bfloat16 [1024, 1024], P('batch'), may hold values from -0.1875 to 0.1875
- attention_output_weight: bfloat16 [1024, 1024], P('batch'), may hold values from -0.5 to 0.5
- up_weight: bfloat16 [1024, 4096], P('batch'), may hold values from -0.1875 to 0.1875
- down_weight: bfloat16 [4096, 1024], P('batch'), may hold values from -0.09375 to 0.09375
- query_down_adapter: bfloat16 [1024, 4], replicated, may hold values from -0.1875 to 0.1875
- query_up_adapter: bfloat16 [4, 1024], replicated, may hold values from -0.1796875 to 0.1796875
- value_down_adapter: bfloat16 [1024, 4], replicated, may hold values from -0.1875 to 0.1875
- value_up_adapter: bfloat16 [4, 1024], replicated, may hold values from -0.1796875 to 0.1796875
Outputs:
- layer_out: bfloat16 [48, 1024, 1024], P('batch', 'seq')
- input_grad: bfloat16 [48, 1024, 1024], P('batch', 'seq')
- grad_qa: float32 [1024, 4], replicated
- query_up_gradient: float32 [4, 1024], replicated
- grad_va: float32 [1024, 4], replicated
- value_up_gradient: float32 [4, 1024], replicated
The draws below stay inside these ranges and needn't reach their ends.
Inputs may be any that keep to these rules, and one draw needn't show every extreme that they name: `layout`: a permutation: each position block of a document is held by exactly one stored block, the same for all documents.
All inputs are finite; a program needn't handle non-finite values.
Results may differ from the reference program's by a relative error of at most 0.018.
Values may be sent and summed in bfloat16 or wider, within the bound.
A program may use at most 384 MiB of HBM per device.

```python
import jax
import jax.numpy as jnp
from jax import lax

MODEL_DIM = 1024
FF = 4096
HEADS = 16
HEAD_DIM = 64
ADAPTER_RANK = 4
SEQ_LEN = 1024
HALF = 256
DOCS = 48
N_SEQ = 2


def steps_of(key, extent, split, low, largest):
    gain, own = 1.0, jax.random.fold_in(key, 6)
    for position, shards_of in split:
        draws = jnp.exp(jax.random.uniform(jax.random.fold_in(own, position), (shards_of,), jnp.float32, low / len(split), largest / len(split)))
        gain = gain * jnp.repeat(draws, extent[position] // shards_of).reshape([-1 if axis == position else 1 for axis in range(len(extent))])
    return gain


def scatter_about(stream_key, shape, deviation, limit, split=(), held_as=jnp.bfloat16):
    entries = deviation * jax.random.normal(stream_key, shape, jnp.float32)
    if split:
        entries = entries * steps_of(stream_key, shape, split, -0.22, 0.18)
    return jnp.clip(entries, -limit, limit).astype(held_as)


def setup_inputs(seed: int = 0) -> dict:
    arg_keys = jax.random.split(jax.random.key(seed), 16)
    tokens = scatter_about(arg_keys[0], (DOCS, SEQ_LEN, MODEL_DIM), 1.0, 6.0, ((0, 16), (1, 2)))
    cotangent = scatter_about(arg_keys[1], (DOCS, SEQ_LEN, MODEL_DIM), 1.0, 6.0, ((0, 16), (1, 2)))
    layout = jax.random.permutation(arg_keys[2], 2 * N_SEQ).astype(jnp.int32)
    attention_norm_gain = jnp.clip(1.0 + 0.18 * jax.random.normal(arg_keys[3], (MODEL_DIM,), jnp.float32), 0.1, 1.9)
    feedforward_norm_gain = jnp.clip(1.0 + 0.18 * jax.random.normal(arg_keys[4], (MODEL_DIM,), jnp.float32), 0.1, 1.9)
    query_weight = scatter_about(arg_keys[5], (MODEL_DIM, MODEL_DIM), (MODEL_DIM // 2) ** -0.5, 0.25, ((0, 16),))
    key_weight = scatter_about(arg_keys[6], (MODEL_DIM, MODEL_DIM), (MODEL_DIM // 2) ** -0.5, 0.25, ((0, 16),))
    value_weight = scatter_about(arg_keys[7], (MODEL_DIM, MODEL_DIM), MODEL_DIM ** -0.5, 0.1875, ((0, 16),))
    attention_output_weight = scatter_about(arg_keys[8], (MODEL_DIM, MODEL_DIM), (MODEL_DIM // 8) ** -0.5, 0.5, ((0, 16),))
    up_weight = scatter_about(arg_keys[9], (MODEL_DIM, FF), MODEL_DIM ** -0.5, 0.1875, ((0, 16),))
    down_weight = scatter_about(arg_keys[10], (FF, MODEL_DIM), FF ** -0.5, 0.09375, ((0, 16),))
    query_down_adapter = scatter_about(arg_keys[11], (MODEL_DIM, ADAPTER_RANK), MODEL_DIM ** -0.5, 0.1875)
    query_up_adapter = scatter_about(arg_keys[12], (ADAPTER_RANK, MODEL_DIM), 0.03, 0.1796875)
    value_down_adapter = scatter_about(arg_keys[13], (MODEL_DIM, ADAPTER_RANK), MODEL_DIM ** -0.5, 0.1875)
    value_up_adapter = scatter_about(arg_keys[14], (ADAPTER_RANK, MODEL_DIM), 0.03, 0.1796875)
    return {"tokens": tokens, "cotangent": cotangent, "layout": layout, "attention_norm_gain": attention_norm_gain, "feedforward_norm_gain": feedforward_norm_gain, "query_weight": query_weight, "key_weight": key_weight, "value_weight": value_weight, "attention_output_weight": attention_output_weight, "up_weight": up_weight, "down_weight": down_weight, "query_down_adapter": query_down_adapter, "query_up_adapter": query_up_adapter, "value_down_adapter": value_down_adapter, "value_up_adapter": value_up_adapter}


PRECISE = lax.Precision.HIGHEST
EPSILON = 1e-05
ADAPTER_SCALE = 8.0
SCORE_SCALE = 0.125
NEG_FILL = -1e+30
GELU_C = 0.7978845608028654

@jax.custom_vjp
def reduced_rank(v):
    return lax.optimization_barrier(v.astype(jnp.bfloat16)).astype(jnp.float32)

@jax.custom_vjp
def reduced_backward(v):
    return v

def low_keep(v):
    return (reduced_rank(v), None)

def low_pass(kept, grad):
    return (grad,)

def back_keep(v):
    return (v, None)

def back_low(kept, grad):
    return (reduced_rank(grad),)
reduced_rank.defvjp(low_keep, low_pass)
reduced_backward.defvjp(back_keep, back_low)

def matrix_multiply(left_op, right_op):
    return jnp.dot(left_op, right_op, precision=PRECISE)

def norm_rows(values, gain_vec):
    row_mean = lax.optimization_barrier(jnp.mean(values, axis=-1, keepdims=True))
    centred = values - row_mean
    spread = lax.optimization_barrier(jnp.mean(centred * centred, axis=-1, keepdims=True))
    return centred * lax.rsqrt(spread + EPSILON) * gain_vec

def gelu_tanh(values):
    return 0.5 * values * (1.0 + jnp.tanh(GELU_C * (values + 0.044715 * values * values * values)))

def positions(layout):
    stored = jnp.arange(SEQ_LEN, dtype=jnp.int32)
    return layout[stored // HALF] * HALF + stored % HALF

def forward(inputs, adapter_weights, frozen, allowed):
    adapt_qa, adapted_query_up, adapt_va, adapted_value_up = adapter_weights
    attention_norm_gain, feedforward_norm_gain, query_weight, key_weight, value_weight, attention_output_weight, up_weight, down_weight = frozen
    length = inputs.shape[0]
    first_normalized = reduced_rank(norm_rows(inputs, attention_norm_gain))
    reduced_query = reduced_backward(reduced_rank(matrix_multiply(first_normalized, adapt_qa)))
    reduced_value = reduced_backward(reduced_rank(matrix_multiply(first_normalized, adapt_va)))
    query_rows = reduced_backward(reduced_rank(matrix_multiply(first_normalized, query_weight) + ADAPTER_SCALE * matrix_multiply(reduced_query, adapted_query_up)))
    key_rows = reduced_backward(reduced_rank(matrix_multiply(first_normalized, key_weight)))
    value_rows = reduced_backward(reduced_rank(matrix_multiply(first_normalized, value_weight) + ADAPTER_SCALE * matrix_multiply(reduced_value, adapted_value_up)))
    query_heads = query_rows.reshape(length, HEADS, HEAD_DIM)
    key_heads = key_rows.reshape(length, HEADS, HEAD_DIM)
    value_heads = value_rows.reshape(length, HEADS, HEAD_DIM)
    scores = reduced_backward(jnp.einsum('qhd,khd->qhk', query_heads, key_heads, precision=PRECISE) * SCORE_SCALE)
    scores = jnp.where(allowed[:, None, :], scores, NEG_FILL)
    shifted = scores - lax.optimization_barrier(jnp.max(scores, axis=-1, keepdims=True))
    expo = jnp.exp(shifted)
    chances = expo / lax.optimization_barrier(jnp.sum(expo, axis=-1, keepdims=True))
    mixed_out = jnp.einsum('qhk,khd->qhd', reduced_rank(chances), value_heads, precision=PRECISE)
    attended = reduced_backward(reduced_rank(mixed_out.reshape(length, MODEL_DIM)))
    residual = inputs + reduced_backward(matrix_multiply(attended, attention_output_weight))
    normed_second = reduced_rank(norm_rows(residual, feedforward_norm_gain))
    pre_act = reduced_backward(matrix_multiply(normed_second, up_weight))
    return residual + reduced_backward(matrix_multiply(reduced_rank(gelu_tanh(pre_act)), down_weight))

def reference(tokens, cotangent, layout, attention_norm_gain, feedforward_norm_gain, query_weight, key_weight, value_weight, attention_output_weight, up_weight, down_weight, query_down_adapter, query_up_adapter, value_down_adapter, value_up_adapter):
    pos_all = positions(layout)
    allowed = pos_all[None, :] <= pos_all[:, None]
    frozen = tuple((input_array.astype(jnp.float32) for input_array in (attention_norm_gain, feedforward_norm_gain, query_weight, key_weight, value_weight, attention_output_weight, up_weight, down_weight)))
    adapter_weights = tuple((input_array.astype(jnp.float32) for input_array in (query_down_adapter, query_up_adapter, value_down_adapter, value_up_adapter)))

    def one_doc(totals, pair):
        doc_tokens, doc_cot = pair
        result, pull = jax.vjp(lambda inputs, weights_in: forward(inputs, weights_in, frozen, allowed), doc_tokens.astype(jnp.float32), adapter_weights)
        token_grad, adapter_grad = pull(doc_cot.astype(jnp.float32))
        totals = tuple((running + addition for running, addition in zip(totals, adapter_grad)))
        return (totals, (result.astype(jnp.bfloat16), token_grad.astype(jnp.bfloat16)))
    zero_filled = tuple((jnp.zeros(input_array.shape, jnp.float32) for input_array in adapter_weights))
    totals, (layer_out, input_grad) = lax.scan(one_doc, zero_filled, (tokens, cotangent))
    return (layer_out, input_grad, totals[0], totals[1], totals[2], totals[3])
```

```python
import functools
import math

import jax
import jax.numpy as jnp
from jax import lax
from jax.experimental import pallas as pl
from jax.experimental.pallas import tpu as pltpu
from jax.sharding import PartitionSpec as P


LOG2E = math.log2(math.e)
SCALE = 0.125
NT = (((1,), (1,)), ((), ()))
NN = (((1,), (0,)), ((), ()))
F32 = jnp.float32
BF = jnp.bfloat16

def dot(a, b, dims=NN):
    return lax.dot_general(a, b, dims, preferred_element_type=F32)

def in_order(ref, where, blocks, size):
    halves, rows = ref.shape[0], ref.shape[2]
    per = rows // size
    out = []
    for p in range(blocks):
        s = where[p]
        out.append(ref[s // per, 0, pl.ds(pl.multiple_of((s % per) * size, size), size), :])
    return jnp.concatenate(out, axis=0)

def att_fwd_kernel(where, q_ref, k_ref, v_ref, o_ref, lse_ref, *, blocks, size, tile):
    q = in_order(q_ref, where, blocks, size)
    k = in_order(k_ref, where, blocks, size)
    v = in_order(v_ref, where, blocks, size)
    n = blocks * size
    vt = v.T
    lane = lax.broadcasted_iota(jnp.int32, (1, 128), 1)
    c = SCALE * LOG2E
    tri = lax.broadcasted_iota(jnp.int32, (tile, tile), 0) <= lax.broadcasted_iota(jnp.int32, (tile, tile), 1)
    work = [(i, h) for i in range(n // tile) for h in range(2)]
    lses = [[], []]
    ots = {}

    def scores(i, h):
        qm = jnp.where((lane < 64) == (h == 0), q[i * tile:(i + 1) * tile], jnp.zeros((), BF))
        return dot(k[:(i + 1) * tile], qm, NT)

    ahead = scores(*work[0])
    for t, (i, h) in enumerate(work):
        st = ahead
        if t + 1 < len(work):
            ahead = scores(*work[t + 1])
        kk = (i + 1) * tile
        diag = jnp.where(tri, st[i * tile:], -1e30)
        st = diag if i == 0 else jnp.concatenate([st[: i * tile], diag], axis=0)
        m = jnp.max(st, axis=0, keepdims=True) * c
        e = jnp.exp2(st * c - m)
        l = jnp.sum(e, axis=0, keepdims=True)
        o = dot(vt[64 * h:64 * h + 64, :kk], e.astype(BF))
        ots[i, h] = o * (1.0 / l)
        lses[h].append(m + jnp.log2(l))
    outs = [jnp.concatenate([ots[i, 0], ots[i, 1]], axis=0).T.astype(BF) for i in range(n // tile)]
    o = jnp.concatenate(outs, axis=0)
    halves, rows = o_ref.shape[0], o_ref.shape[2]
    per = rows // size
    for p in range(blocks):
        s = where[p]
        o_ref[s // per, 0, pl.ds(pl.multiple_of((s % per) * size, size), size), :] = o[p * size:(p + 1) * size]
    for h in range(2):
        lse_ref[0, 0, h:h + 1, :] = jnp.concatenate(lses[h], axis=1)

def att_fwd(where, qkv, size, tile=256):
    halves, docs, rows, w3 = qkv.shape
    w = w3 // 3
    pairs = w // 128
    n = halves * rows
    blocks = n // size
    def spec(part):
        return pl.BlockSpec((halves, 1, rows, 128), lambda d, p, s, part=part: (0, d, 0, part * pairs + p))
    return pl.pallas_call(
        functools.partial(att_fwd_kernel, blocks=blocks, size=size, tile=tile),
        grid_spec=pltpu.PrefetchScalarGridSpec(
            num_scalar_prefetch=1, grid=(docs, pairs),
            in_specs=[spec(0), spec(1), spec(2)],
            out_specs=[pl.BlockSpec((halves, 1, rows, 128), lambda d, p, s: (0, d, 0, p)),
                       pl.BlockSpec((1, 1, 2, n), lambda d, p, s: (d, p, 0, 0))]),
        out_shape=[jax.ShapeDtypeStruct((halves, docs, rows, w), BF),
                   jax.ShapeDtypeStruct((docs, pairs, 2, n), F32)],
        compiler_params=pltpu.CompilerParams(vmem_limit_bytes=60 << 20),
        name="attention_forward",
    )(where, qkv, qkv, qkv)

def att_bwd_kernel(where, q_ref, k_ref, v_ref, o_ref, g_ref, lse_ref, dq_ref, dk_ref, dv_ref, dqt, *, blocks, size, tile):
    q = in_order(q_ref, where, blocks, size)
    k = in_order(k_ref, where, blocks, size)
    v = in_order(v_ref, where, blocks, size)
    o = in_order(o_ref, where, blocks, size)
    g = in_order(g_ref, where, blocks, size)
    n = blocks * size
    kt = k.T
    lane = lax.broadcasted_iota(jnp.int32, (1, 128), 1)
    c = SCALE * LOG2E
    tri = lax.broadcasted_iota(jnp.int32, (tile, tile), 0) <= lax.broadcasted_iota(jnp.int32, (tile, tile), 1)
    prod = (o.astype(F32) * g.astype(F32)).astype(BF)
    sel = (lax.broadcasted_iota(jnp.int32, (8, 128), 1) // 64 == lax.broadcasted_iota(jnp.int32, (8, 128), 0)).astype(BF)
    delta = dot(sel, prod, NT)
    zero = jnp.zeros((), BF)
    masks = [(lane < 64) == (h == 0) for h in range(2)]
    qms = [jnp.where(mk, q, zero) for mk in masks]
    gms = [jnp.where(mk, g, zero) for mk in masks]
    lse = lse_ref[0, 0]
    halves, rows = o_ref.shape[0], o_ref.shape[2]
    per = rows // size
    dks, dvs = [], []
    work = [(j, h) for j in range(n // tile) for h in range(2)]

    def products(j, h):
        lo, hi = j * tile, (j + 1) * tile
        return dot(k[lo:hi], qms[h][lo:], NT), dot(v[lo:hi], gms[h][lo:], NT)

    ahead = products(*work[0])
    for t, (j, h) in enumerate(work):
        st, dp = ahead
        if t + 1 < len(work):
            ahead = products(*work[t + 1])
        lo, hi = j * tile, (j + 1) * tile
        p = jnp.exp2(st * c - lse[h:h + 1, lo:])
        dg = jnp.where(tri, p[:, :tile], 0.0)
        p = dg if hi == n else jnp.concatenate([dg, p[:, tile:]], axis=1)
        ds = (p * (dp - delta[h:h + 1, lo:])).astype(BF)
        dvh = dot(p.astype(BF), gms[h][lo:])
        dkh = dot(ds, qms[h][lo:])
        dv = dvh if h == 0 else dv + dvh
        dk = dkh if h == 0 else dk + dkh
        dqh = dot(kt[64 * h:64 * h + 64, lo:hi], ds)
        if j == 0:
            dqt[64 * h:64 * h + 64, :] = dqh
        else:
            dqt[64 * h:64 * h + 64, lo:] += dqh
        if h == 1:
            dks.append((dk * SCALE).astype(BF))
            dvs.append(dv.astype(BF))
    dk = jnp.concatenate(dks, axis=0)
    dv = jnp.concatenate(dvs, axis=0)
    dq = (dqt[...] * SCALE).T.astype(BF)
    for p in range(blocks):
        s = where[p]
        at = (s // per, 0, pl.ds(pl.multiple_of((s % per) * size, size), size), slice(None))
        piece = slice(p * size, (p + 1) * size)
        dq_ref[at] = dq[piece]
        dk_ref[at] = dk[piece]
        dv_ref[at] = dv[piece]

def att_bwd(where, qkv, o, g, lse, size, tile=256):
    halves, docs, rows, w3 = qkv.shape
    w = w3 // 3
    pairs = w // 128
    n = halves * rows
    blocks = n // size
    def spec(part):
        return pl.BlockSpec((halves, 1, rows, 128), lambda d, p, s, part=part: (0, d, 0, part * pairs + p))
    return pl.pallas_call(
        functools.partial(att_bwd_kernel, blocks=blocks, size=size, tile=tile),
        grid_spec=pltpu.PrefetchScalarGridSpec(
            num_scalar_prefetch=1, grid=(docs, pairs),
            in_specs=[spec(0), spec(1), spec(2), spec(0), spec(0),
                      pl.BlockSpec((1, 1, 2, n), lambda d, p, s: (d, p, 0, 0))],
            out_specs=[spec(0)] * 3,
            scratch_shapes=[pltpu.VMEM((128, n), F32)]),
        out_shape=[jax.ShapeDtypeStruct((halves, docs, rows, w), BF)] * 3,
        compiler_params=pltpu.CompilerParams(vmem_limit_bytes=60 << 20),
        name="attention_backward",
    )(where, qkv, qkv, qkv, o, g, lse)
EPS = 1e-5
GELU_C = 0.7978845608028654
TN = (((0,), (0,)), ((), ()))

def normalise(x):
    mean = jnp.mean(x, axis=-1, keepdims=True)
    cen = x - mean
    inv = lax.rsqrt(jnp.mean(cen * cen, axis=-1, keepdims=True) + EPS)
    return cen * inv, inv

def norm_back(xh, inv, gain, up):
    t = up * gain
    return inv * (t - jnp.mean(t, axis=-1, keepdims=True) - xh * jnp.mean(t * xh, axis=-1, keepdims=True))

def gelu_parts(u):
    cubic = 0.044715 * u * u
    th = jnp.tanh(GELU_C * (u + cubic * u))
    half = 0.5 * (1.0 + th)
    return half * u, half + (0.5 * GELU_C) * u * (1.0 - th * th) * (1.0 + 3.0 * cubic)

def project_kernel(x_ref, gain_ref, w_ref, down_ref, up_ref, out_ref, low_ref):
    groups, w3 = out_ref.shape[0], out_ref.shape[3]
    w = w3 // 3
    xh, _ = normalise(x_ref[0].astype(F32))
    n1 = (xh * gain_ref[...]).astype(BF)
    low = dot(n1, down_ref[...]).astype(BF)
    low_ref[0] = low
    for g in range(groups):
        for part in range(3):
            cols = slice(g * w3 + part * w, g * w3 + (part + 1) * w)
            y = dot(n1, w_ref[:, cols])
            if part != 1:
                y = y + dot(low, up_ref[:, cols])
            out_ref[g, 0, :, part * w:(part + 1) * w] = y.astype(BF)

def project(x, gain, w, down, up, groups):
    docs, rows, d = x.shape
    n = w.shape[1]
    full = lambda a: pl.BlockSpec(a.shape, lambda i: (0,) * a.ndim)
    return pl.pallas_call(
        project_kernel,
        grid=(docs,),
        in_specs=[pl.BlockSpec((1, rows, d), lambda i: (i, 0, 0)), full(gain), full(w), full(down), full(up)],
        out_specs=[pl.BlockSpec((groups, 1, rows, n // groups), lambda i: (0, i, 0, 0)),
                   pl.BlockSpec((1, rows, 128), lambda i: (i, 0, 0))],
        out_shape=[jax.ShapeDtypeStruct((groups, docs, rows, n // groups), BF),
                   jax.ShapeDtypeStruct((docs, rows, 128), BF)],
        compiler_params=pltpu.CompilerParams(vmem_limit_bytes=60 << 20),
        name="projections",
    )(x, gain, w, down, up)

def middle_kernel(x_ref, att_ref, cot_ref, gain_ref, wo_ref, up_ref, down_ref, out_ref, res_ref, mix_ref,
                  acc, xhs, dn, n2s, invs, *, tile):
    f = pl.program_id(0)
    last = pl.num_programs(0) - 1
    docs, rows, d = x_ref.shape
    groups, w = att_ref.shape[0], att_ref.shape[3]
    tiles = [(i, r) for i in range(docs) for r in range(0, rows, tile)]

    @pl.when(f == 0)
    def _():
        for i, r in tiles:
            at = slice(i * rows + r, i * rows + r + tile)
            res = x_ref[i, r:r + tile, :].astype(F32)
            for g in range(groups):
                res = res + dot(att_ref[g, i, r:r + tile, :], wo_ref[g * w:(g + 1) * w, :])
            acc[at, :] = res
            xh, inv = normalise(res)
            xhs[at, :] = xh
            invs[at, :] = jnp.broadcast_to(inv, (tile, 128))
            n2s[at, :] = (xh * gain_ref[...]).astype(BF)
            dn[at, :] = jnp.zeros((tile, d), F32)

    def first(i, r):
        at = slice(i * rows + r, i * rows + r + tile)
        return dot(n2s[at, :], up_ref[...]), dot(cot_ref[i, r:r + tile, :], down_ref[...], NT)

    ahead = first(*tiles[0])
    for t, (i, r) in enumerate(tiles):
        u, g = ahead
        if t + 1 < len(tiles):
            ahead = first(*tiles[t + 1])
        at = slice(i * rows + r, i * rows + r + tile)
        act, slope = gelu_parts(u)
        pg = (slope * g).astype(BF)
        acc[at, :] += dot(act.astype(BF), down_ref[...])
        dn[at, :] += dot(pg, up_ref[...], NT)

    @pl.when(f == last)
    def _():
        for i, r in tiles:
            at = slice(i * rows + r, i * rows + r + tile)
            out_ref[i, r:r + tile, :] = acc[at, :].astype(BF)
            rg = cot_ref[i, r:r + tile, :].astype(F32) + norm_back(xhs[at, :], invs[at, :1], gain_ref[...], dn[at, :])
            res_ref[i, r:r + tile, :] = rg
            rgb = rg.astype(BF)
            for g in range(groups):
                mix_ref[g, i, r:r + tile, :] = dot(rgb, wo_ref[g * w:(g + 1) * w, :], NT).astype(BF)

def middle(x, att, cot, gain, wo, up, down, chunk=512, tile=512):
    docs, rows, d = x.shape
    groups, _, _, w = att.shape
    ff = up.shape[1]
    tile = min(tile, rows)
    full = lambda a: pl.BlockSpec(a.shape, lambda i: (0,) * a.ndim, pipeline_mode=pl.Buffered(1))
    outs = [jax.ShapeDtypeStruct((docs, rows, d), BF), jax.ShapeDtypeStruct((docs, rows, d), F32),
            jax.ShapeDtypeStruct((groups, docs, rows, w), BF)]
    n = docs * rows
    return pl.pallas_call(
        functools.partial(middle_kernel, tile=tile),
        grid=(ff // chunk,),
        in_specs=[full(x), full(att), full(cot), full(gain), full(wo),
                  pl.BlockSpec((d, chunk), lambda i: (0, i)), pl.BlockSpec((chunk, d), lambda i: (i, 0))],
        out_specs=[full(o) for o in outs],
        out_shape=outs,
        scratch_shapes=[pltpu.VMEM((n, d), F32), pltpu.VMEM((n, d), F32), pltpu.VMEM((n, d), F32),
                        pltpu.VMEM((n, d), BF), pltpu.VMEM((n, 128), F32)],
        compiler_params=pltpu.CompilerParams(vmem_limit_bytes=63 << 20),
        name="feed_forward",
    )(x, att, cot, gain, wo, up, down)

def final_kernel(x_ref, gain_ref, dq_ref, dk_ref, dv_ref, res_ref, low_ref, w_ref, down_ref, up_ref,
                 out_ref, gdown_ref, gup_ref):
    i = pl.program_id(0)
    groups, w = dq_ref.shape[0], dq_ref.shape[3]
    xh, inv = normalise(x_ref[0].astype(F32))
    n1 = (xh * gain_ref[...]).astype(BF)

    @pl.when(i == 0)
    def _():
        gdown_ref[...] = jnp.zeros_like(gdown_ref)
        gup_ref[...] = jnp.zeros_like(gup_ref)

    low = low_ref[0]
    fg = lg = None
    for g in range(groups):
        for part, ref in enumerate((dq_ref, dk_ref, dv_ref)):
            cols = slice((3 * g + part) * w, (3 * g + part + 1) * w)
            piece = ref[g, 0]
            y = dot(piece, w_ref[:, cols], NT)
            fg = y if fg is None else fg + y
            if part != 1:
                y = dot(piece, up_ref[:, cols], NT)
                lg = y if lg is None else lg + y
                gup_ref[:, cols] += dot(low, piece, TN)
    lgb = lg.astype(BF)
    fg = fg + dot(lgb, down_ref[...], NT)
    gdown_ref[...] += dot(lgb, n1, TN)
    out_ref[0] = (res_ref[0] + norm_back(xh, inv, gain_ref[...], fg)).astype(BF)

def final(x, gain, dq, dk, dv, res, low, w, down, up):
    docs, rows, d = x.shape
    groups, _, _, wid = dq.shape
    full = lambda a: pl.BlockSpec(a.shape, lambda i: (0,) * a.ndim)
    row = pl.BlockSpec((1, rows, d), lambda i: (i, 0, 0))
    part = pl.BlockSpec((groups, 1, rows, wid), lambda i: (0, i, 0, 0))
    outs = [jax.ShapeDtypeStruct((docs, rows, d), BF), jax.ShapeDtypeStruct((128, d), F32),
            jax.ShapeDtypeStruct((128, w.shape[1]), F32)]
    return pl.pallas_call(
        final_kernel,
        grid=(docs,),
        in_specs=[row, full(gain), part, part, part, row, pl.BlockSpec((1, rows, 128), lambda i: (i, 0, 0)),
                  full(w), full(down), full(up)],
        out_specs=[row, full(outs[1]), full(outs[2])],
        out_shape=outs,
        compiler_params=pltpu.CompilerParams(vmem_limit_bytes=60 << 20),
        name="projection_gradients",
    )(x, gain, dq, dk, dv, res, low, w, down, up)

ADAPTER_SCALE = 8.0
AXES = ("batch", "seq")


def swapped(b, s):
    return (b & ~1) | (s & 1), (s & ~1) | (b & 1)


def local(
    nb, ns,
    tokens, cotangent, layout, attention_norm_gain, feedforward_norm_gain,
    query_weight, key_weight, value_weight, attention_output_weight, up_weight, down_weight,
    query_down_adapter, query_up_adapter, value_down_adapter, value_up_adapter,
):
    docs, rows, d = tokens.shape
    size = rows * ns // layout.shape[0]
    w = d // ns
    swap = []
    for b in range(nb):
        for s in range(ns):
            b2, s2 = swapped(b, s)
            swap.append((b * ns + s, b2 * ns + s2))
    seq_index = (lax.axis_index("seq") & ~1) | (lax.axis_index("batch") & 1)

    def cross(a):
        return lax.ppermute(a, AXES, swap)

    def peer_swap(a, r):
        perm = []
        for b in range(nb):
            for s in range(ns):
                b2, s2 = swapped(b, s)
                b3, s3 = swapped(b2, s2 ^ r)
                perm.append((b * ns + s, b3 * ns + s3))
        return lax.ppermute(a, AXES, perm)

    def exchange(a):
        out = lax.dynamic_update_index_in_dim(
            jnp.zeros_like(a), lax.dynamic_index_in_dim(a, seq_index, 0), seq_index, 0)
        for r in range(1, ns):
            got = peer_swap(lax.dynamic_index_in_dim(a, seq_index ^ r, 0), r)
            out = lax.dynamic_update_index_in_dim(out, got, seq_index ^ r, 0)
        return out

    def interleave(q, k, v):
        cols = []
        for g in range(ns):
            for a in (q, k, v):
                cols.append(a[:, g * w:(g + 1) * w])
        return jnp.concatenate(cols, axis=1)

    x = cross(tokens)
    cot = cross(cotangent)
    w_qkv = lax.all_gather(interleave(query_weight, key_weight, value_weight), "batch", axis=0, tiled=True)
    w_o = lax.all_gather(attention_output_weight, "batch", axis=0, tiled=True)
    w_up = lax.all_gather(up_weight, "batch", axis=0, tiled=True)
    w_down = lax.all_gather(down_weight, "batch", axis=0, tiled=True)
    rank = query_up_adapter.shape[0]
    down8 = jnp.pad(jnp.concatenate([query_down_adapter, value_down_adapter], axis=1), ((0, 0), (0, 128 - 2 * rank)))
    none = jnp.zeros_like(query_up_adapter)
    up8 = jnp.pad(
        ADAPTER_SCALE * jnp.concatenate(
            [interleave(query_up_adapter, none, none), interleave(none, none, value_up_adapter)], axis=0),
        ((0, 128 - 2 * rank), (0, 0))).astype(BF)
    where = jnp.argsort(layout).astype(jnp.int32)
    gain1 = attention_norm_gain[None]
    gain2 = feedforward_norm_gain[None]

    qkv, low = project(x, gain1, w_qkv, down8, up8, ns)
    qkv = exchange(qkv)
    att, lse = att_fwd(where, qkv, size)
    layer_out, res, mix = middle(x, exchange(att), cot, gain2, w_o, w_up, w_down)
    layer_out = cross(layer_out)
    dq, dk, dv = att_bwd(where, qkv, att, exchange(mix), lse, size)
    dq, dk, dv = exchange(dq), exchange(dk), exchange(dv)
    input_grad, gdown, gup = final(x, gain1, dq, dk, dv, res, low, w_qkv, down8, up8)
    input_grad = cross(input_grad)
    gup = gup[:2 * rank].reshape(2 * rank, ns, 3, w)
    sums = jnp.concatenate([
        gdown[:rank], gdown[rank:2 * rank],
        ADAPTER_SCALE * gup[:rank, :, 0].reshape(rank, d),
        ADAPTER_SCALE * gup[rank:, :, 2].reshape(rank, d)], axis=0)
    sums = lax.psum(sums, AXES)
    return (layer_out, input_grad, sums[:rank].T, sums[2 * rank:3 * rank], sums[rank:2 * rank].T, sums[3 * rank:])


def solution(mesh):
    spec = P("batch", "seq", None)
    weight = P("batch", None)
    return jax.shard_map(
        functools.partial(local, mesh.shape["batch"], mesh.shape["seq"]),
        mesh=mesh,
        in_specs=(spec, spec, P(), P(), P()) + (weight,) * 6 + (P(),) * 4,
        out_specs=(spec, spec, P(), P(), P(), P()),
        check_vma=False,
    )
```

```python
import functools
import math

import jax
import jax.numpy as jnp
from jax import lax
from jax.experimental import pallas as pl
from jax.experimental.pallas import tpu as pltpu
from jax.sharding import PartitionSpec as P


EPSILON = 1e-05
ADAPTER_SCALE = 8.0
SCORE_SCALE = 0.125
NEG_FILL = -1e30
GELU_C = 0.7978845608028654
LOG2E = math.log2(math.e)
F32 = jnp.float32
BF = jnp.bfloat16
NN = (((1,), (0,)), ((), ()))
NT = (((1,), (1,)), ((), ()))
TN = (((0,), (0,)), ((), ()))
AXES = ("batch", "seq")


def dot(a, b, dims=NN):
    return lax.dot_general(a, b, dims, preferred_element_type=F32)


def normalise(x):
    mean = jnp.mean(x, axis=-1, keepdims=True)
    centred = x - mean
    inv = lax.rsqrt(jnp.mean(centred * centred, axis=-1, keepdims=True) + EPSILON)
    return centred * inv, inv


def norm_back(xh, inv, gain, up):
    t = up * gain
    return inv * (t - jnp.mean(t, axis=-1, keepdims=True) - xh * jnp.mean(t * xh, axis=-1, keepdims=True))


def gelu_parts(u):
    cubic = 0.044715 * u * u
    th = jnp.tanh(GELU_C * (u + cubic * u))
    half = 0.5 * (1.0 + th)
    return half * u, half + (0.5 * GELU_C) * u * (1.0 - th * th) * (1.0 + 3.0 * cubic)


MESH = pl.DeviceIdType.MESH


def flip(i, bits):
    out, bit = i, 1
    while bit <= bits:
        if bits & bit:
            out = out + bit - 2 * bit * ((i // bit) % 2)
        bit *= 2
    return out


def trade(b, s):
    return b - b % 2 + s % 2, s - s % 2 + b % 2


class Place:
    def __init__(self, nb, ns):
        self.nb, self.ns = nb, ns
        self.b, self.s = lax.axis_index("batch"), lax.axis_index("seq")
        self.lines = nb // 4
        self.line = self.b // 4
        self.partner = trade(self.b, self.s)
        self.stays = self.b % 2 == self.s % 2
        self.doc, self.part = trade(self.b, self.s)

    def peer(self, r):
        return trade(self.doc, flip(self.part, r))

    def greet(self, ways):
        bar = pltpu.get_barrier_semaphore()
        for device, cond in ways:
            def hello(device=device):
                pl.semaphore_signal(bar, inc=1, device_id=device, device_id_type=MESH)
            hello() if cond is None else pl.when(cond)(hello)
        count = 0
        for _, cond in ways:
            count = count + (1 if cond is None else jnp.where(cond, 1, 0))
        pl.semaphore_wait(bar, count)

    def gather_ways(self):
        b, s = self.b, self.s
        return [((b + 4, s), self.line + 1 < self.lines), ((b - 4, s), self.line > 0),
                ((flip(b, 2), s), None), ((flip(b, 1), s), None)]


class Gather:
    def __init__(self, place, own, full, send, recv):
        self.p, self.own, self.full, self.send, self.recv = place, own, full, send, recv

    def part(self, line, pair=0, core=0):
        b = self.p.b
        return line * 4 + flip(b, 2 * pair + core) % 4

    def copy(self, i, way, src=None):
        p = self.p
        to = [p.b + 4, p.b - 4, flip(p.b, 2), flip(p.b, 1)][way]
        return pltpu.make_async_remote_copy(
            src_ref=self.full.at[i] if src is None else src, dst_ref=self.full.at[i],
            send_sem=self.send.at[way, i], recv_sem=self.recv.at[i],
            device_id=(to, p.s), device_id_type=MESH)

    def mine(self):
        return pltpu.make_async_copy(self.own, self.full.at[self.p.b], self.recv.at[self.p.b])

    def start(self):
        p = self.p
        self.mine().start()
        pl.when(p.line + 1 < p.lines)(lambda: self.copy(p.b, 0, self.own).start())
        pl.when(p.line > 0)(lambda: self.copy(p.b, 1, self.own).start())
        self.copy(p.b, 2, self.own).start()
        self.copy(p.b, 3, self.own).start()

    def hop(self, k):
        p = self.p
        for way, cond in ((0, p.line >= k), (1, p.line + k < p.lines)):
            def take(way=way):
                i = self.part(p.line - k if way == 0 else p.line + k)
                self.copy(i, way).wait_recv()
                more = p.line + 1 < p.lines if way == 0 else p.line > 0
                pl.when(more)(lambda: self.copy(i, way).start())
                self.copy(i, 2).start()
                self.copy(i, 3).start()
            pl.when(cond)(take)

    def relay(self, k):
        p = self.p
        def take(line):
            i = self.part(line, pair=1)
            self.copy(i, 2).wait_recv()
            self.copy(i, 3).start()
        if k == 0:
            take(p.line)
        else:
            pl.when(p.line >= k)(lambda: take(p.line - k))
            pl.when(p.line + k < p.lines)(lambda: take(p.line + k))

    def finish(self):
        self.mine().wait()
        for line in range(self.p.lines):
            for pair in range(2):
                self.copy(self.part(line, pair, 1), 3).wait_recv()

    def drain(self):
        p = self.p
        for line in range(p.lines):
            i = self.part(line)
            pl.when((p.line >= line) & (p.line + 1 < p.lines))(lambda i=i: self.copy(i, 0).wait_send())
            pl.when((p.line <= line) & (p.line > 0))(lambda i=i: self.copy(i, 1).wait_send())
            self.copy(i, 2).wait_send()
            self.copy(i, 3).wait_send()
            self.copy(self.part(line, 1), 3).wait_send()

    def steps(self, ahead=None):
        out = []
        for k in range(1, self.p.lines):
            out.append(lambda k=k: self.hop(k))
            if k == 1 and ahead is not None:
                out.append(ahead)
            out.append(lambda k=k: self.relay(k - 1))
        out.append(lambda: self.relay(self.p.lines - 1))
        out.append(self.finish)
        return out


SKEW = 2


def project_kernel(nb, ns, x_hbm, wq_ref, wk_ref, wv_ref, wo_ref, gain_ref, down_ref, upq_ref, upv_ref,
                   q_out, k_out, v_out, low_out, x_out, wq_out, wk_out, wv_out, wo_out,
                   xs, n1s, stage, lows, wqs, wks, wvs, wos, send, recv, xsend, xrecv, osend, orecv, local_sem):
    docs, rows, d = x_hbm.shape
    w = d // ns
    p = Place(nb, ns)
    others = [p.peer(r) for r in range(1, ns)]
    p.greet(p.gather_ways() + [(p.partner, jnp.logical_not(p.stays))] + [(o, None) for o in others])

    def x_remote(i):
        return pltpu.make_async_remote_copy(
            src_ref=x_hbm.at[i], dst_ref=xs.at[i], send_sem=xsend.at[i], recv_sem=xrecv.at[i],
            device_id=p.partner, device_id_type=MESH)

    def x_local(i):
        return pltpu.make_async_copy(x_hbm.at[i], xs.at[i], xrecv.at[i])

    def x_keep(i):
        return pltpu.make_async_copy(xs.at[i], x_out.at[i], local_sem.at[i])

    for i in range(docs):
        pl.when(p.stays)(lambda i=i: x_local(i).start())
        pl.when(jnp.logical_not(p.stays))(lambda i=i: x_remote(i).start())

    def first(i):
        pl.when(p.stays)(lambda: x_local(i).wait())
        pl.when(jnp.logical_not(p.stays))(lambda: x_remote(i).wait())
        x_keep(i).start()
        xh, _ = normalise(xs[i].astype(F32))
        n1 = (xh * gain_ref[...]).astype(BF)
        n1s[i] = n1
        lows[i] = dot(n1, down_ref[...]).astype(BF)

    outs = (q_out, k_out, v_out)

    def away(part, i, r):
        return pltpu.make_async_remote_copy(
            src_ref=stage.at[part, i, flip(p.part, r)], dst_ref=outs[part].at[p.part, i],
            send_sem=osend.at[part, i, r], recv_sem=orecv.at[part, i, r],
            device_id=p.peer(r), device_id_type=MESH)

    def home(part, i):
        return pltpu.make_async_copy(stage.at[part, i, p.part], outs[part].at[p.part, i], osend.at[part, i, 0])

    def product(part, i):
        full = (wqs, wks, wvs)[part]
        y = dot(n1s[i], full[...].reshape(d, d))
        if part == 0:
            y = y + dot(lows[i], upq_ref[...])
        if part == 2:
            y = y + dot(lows[i], upv_ref[...])
        y = y.astype(BF)
        for g in range(ns):
            stage[part, i, g] = y[:, g * w:(g + 1) * w]
        home(part, i).start()
        for r in range(1, ns):
            away(part, i, r).start()

    gathers = [Gather(p, own, full, send.at[n], recv.at[n]) for n, (own, full) in enumerate(
        ((wq_ref, wqs), (wk_ref, wks), (wv_ref, wvs), (wo_ref, wos)))]
    keeps = [pltpu.make_async_copy(full, out, local_sem.at[docs + n]) for n, (full, out) in enumerate(
        ((wqs, wq_out), (wks, wk_out), (wvs, wv_out), (wos, wo_out)))]
    low_keep = pltpu.make_async_copy(lows, low_out, local_sem.at[docs + 4])

    ready = [len(gathers[0].steps()) + SKEW * n for n in range(4)]
    work = {}

    def place(t, task):
        work.setdefault(t, []).append(task)

    last = ready[3]
    for i in range(docs):
        at = min(ready[0] + 2 * SKEW * i // 2, last) if i < 2 else last
        place(at, functools.partial(first, i))
        for part in range(3):
            place(max(at, ready[part]), functools.partial(product, part, i))

    lists = [[g.start] + g.steps() for g in gathers]
    for t in range(len(lists[0]) + SKEW * (len(lists) - 1)):
        for n, steps in enumerate(lists):
            if 0 <= t - SKEW * n < len(steps):
                steps[t - SKEW * n]()
            if t - SKEW * n == len(steps) - 1:
                keeps[n].start()
        for task in work.get(t, []):
            task()
    low_keep.start()
    for part in range(3):
        for i in range(docs):
            home(part, i).wait()
            for r in range(1, ns):
                away(part, i, r).wait()
    for i in range(docs):
        x_keep(i).wait()
    for keep in keeps:
        keep.wait()
    low_keep.wait()
    for g in gathers:
        g.drain()


def project(nb, ns, x, wq, wk, wv, wo, gain, down, upq, upv):
    docs, rows, d = x.shape
    w = d // ns
    any_spec = pl.BlockSpec(memory_space=pl.ANY)
    vmem = pl.BlockSpec(memory_space=pltpu.VMEM)
    head = jax.ShapeDtypeStruct((ns, docs, rows, w), BF)
    full = jax.ShapeDtypeStruct((nb,) + wq.shape, BF)
    dma = pltpu.SemaphoreType.DMA
    return pl.pallas_call(
        functools.partial(project_kernel, nb, ns),
        in_specs=[any_spec] * 5 + [vmem] * 4,
        out_specs=[any_spec] * 9,
        out_shape=[head] * 3 + [jax.ShapeDtypeStruct((docs, rows, 128), BF), jax.ShapeDtypeStruct(x.shape, BF)] + [full] * 4,
        scratch_shapes=[pltpu.VMEM(x.shape, BF), pltpu.VMEM(x.shape, BF), pltpu.VMEM((3, docs, ns, rows, w), BF),
                        pltpu.VMEM((docs, rows, 128), BF)] + [pltpu.VMEM(full.shape, BF)] * 4 + [
                        dma((4, 4, nb)), dma((4, nb)), dma((docs,)), dma((docs,)),
                        dma((3, docs, ns)), dma((3, docs, ns)), dma((docs + 5,))],
        compiler_params=pltpu.CompilerParams(collective_id=0, has_side_effects=True, vmem_limit_bytes=60 << 20),
        name="projections",
    )(x, wq, wk, wv, wo, gain, down, upq, upv)


def in_order(ref, where, blocks, size):
    per = ref.shape[2] // size
    out = []
    for p in range(blocks):
        s = where[p]
        out.append(ref[s // per, 0, pl.ds(pl.multiple_of((s % per) * size, size), size), :])
    return jnp.concatenate(out, axis=0)


def chosen(blocks, which):
    out = blocks[0]
    for t in range(1, len(blocks)):
        out = jnp.where(which == t, blocks[t], out)
    return out


def picked(ref, where, blocks, size):
    per = ref.shape[2] // size
    stored = [ref[t // per, 0, (t % per) * size:(t % per + 1) * size, :] for t in range(blocks)]
    return jnp.concatenate([chosen(stored, where[p]) for p in range(blocks)], axis=0)


def store_back(ref, value, where, blocks, size):
    per = ref.shape[2] // size
    for t in range(blocks):
        piece = value[:size]
        for p in range(1, blocks):
            piece = jnp.where(where[p] == t, value[p * size:(p + 1) * size], piece)
        ref[t // per, 0, (t % per) * size:(t % per + 1) * size, :] = piece


def attention_forward_kernel(nb, ns, size, tile, items, where, q_ref, k_ref, v_ref, cot_hbm, own_hbm,
                             o_ref, lse_ref, cot_out, full_out, own, send, recv, csend, crecv, own_sem):
    docs = cot_hbm.shape[0]
    p = Place(nb, ns)
    step = pl.program_id(0) * pl.num_programs(1) + pl.program_id(1)
    cut = own_hbm.shape[0] // items
    gathers = [Gather(p, own.at[pl.ds(n * cut, cut)], full_out.at[:, pl.ds(n * cut, cut)], send.at[n], recv.at[n])
               for n in range(items)]

    def cross(i):
        return pltpu.make_async_remote_copy(
            src_ref=cot_hbm.at[i], dst_ref=cot_out.at[i], send_sem=csend.at[i], recv_sem=crecv.at[i],
            device_id=p.partner, device_id_type=MESH)

    def begin():
        fetch = pltpu.make_async_copy(own_hbm, own, own_sem)
        fetch.start()
        p.greet(p.gather_ways() + [(p.partner, jnp.logical_not(p.stays))])
        for i in range(docs):
            pl.when(jnp.logical_not(p.stays))(lambda i=i: cross(i).start())
        fetch.wait()
        for g in gathers:
            g.start()

    def end():
        for i in range(docs):
            pl.when(jnp.logical_not(p.stays))(lambda i=i: cross(i).wait())
        for g in gathers:
            g.drain()

    def together(calls):
        for call in calls:
            call()

    events = [begin] + [functools.partial(together, calls) for calls in zip(*[g.steps() for g in gathers])]
    steps = docs * (full_out.shape[2] // ns // 128)
    for n, event in enumerate(events):
        at = n * (steps - 1) // len(events)
        pl.when(step == at)(event)

    lane = lax.broadcasted_iota(jnp.int32, (1, 128), 1)
    parts, rows = q_ref.shape[0], q_ref.shape[2]
    n = parts * rows
    blocks = n // size
    q = picked(q_ref, where, blocks, size)
    k = picked(k_ref, where, blocks, size)
    v = picked(v_ref, where, blocks, size)
    vt = v.T
    c = SCORE_SCALE * LOG2E
    tri = lax.broadcasted_iota(jnp.int32, (tile, tile), 0) <= lax.broadcasted_iota(jnp.int32, (tile, tile), 1)
    work = [(i, h) for i in range(n // tile) for h in range(2)]
    lses = [[], []]
    mixed = {}

    def scores(i, h):
        qm = jnp.where((lane < 64) == (h == 0), q[i * tile:(i + 1) * tile], jnp.zeros((), BF))
        return dot(k[:(i + 1) * tile], qm, NT)

    ahead = scores(*work[0])
    for t, (i, h) in enumerate(work):
        st = ahead
        if t + 1 < len(work):
            ahead = scores(*work[t + 1])
        kk = (i + 1) * tile
        diag = jnp.where(tri, st[i * tile:], NEG_FILL)
        st = diag if i == 0 else jnp.concatenate([st[: i * tile], diag], axis=0)
        m = jnp.max(st, axis=0, keepdims=True) * c
        e = jnp.exp2(st * c - m)
        l = jnp.sum(e, axis=0, keepdims=True)
        o = dot(vt[64 * h:64 * h + 64, :kk], e.astype(BF))
        mixed[i, h] = o * (1.0 / l)
        lses[h].append(m + jnp.log2(l))
    outs = [jnp.concatenate([mixed[i, 0], mixed[i, 1]], axis=0).T.astype(BF) for i in range(n // tile)]
    store_back(o_ref, jnp.concatenate(outs, axis=0), where, blocks, size)
    for h in range(2):
        lse_ref[0, 0, h:h + 1, :] = jnp.concatenate(lses[h], axis=1)

    pl.when(step == steps - 1)(end)


def attention_forward(nb, ns, where, q, k, v, cot, own, size, tile=256, items=2):
    parts, docs, rows, w = q.shape
    pairs = w // 128
    n = parts * rows
    spec = pl.BlockSpec((parts, 1, rows, 128), lambda d, p: (0, d, 0, p))
    any_spec = pl.BlockSpec(memory_space=pl.ANY)
    dma = pltpu.SemaphoreType.DMA
    return pl.pallas_call(
        functools.partial(attention_forward_kernel, nb, ns, size, tile, items),
        grid=(docs, pairs),
        in_specs=[pl.BlockSpec(memory_space=pltpu.SMEM), spec, spec, spec, any_spec, any_spec],
        out_specs=[spec, pl.BlockSpec((1, 1, 2, n), lambda d, p: (d, p, 0, 0)), any_spec, any_spec],
        out_shape=[jax.ShapeDtypeStruct((parts, docs, rows, w), BF),
                   jax.ShapeDtypeStruct((docs, pairs, 2, n), F32),
                   jax.ShapeDtypeStruct(cot.shape, BF),
                   jax.ShapeDtypeStruct((nb,) + own.shape, BF)],
        scratch_shapes=[pltpu.VMEM(own.shape, BF), dma((items, 4, nb)), dma((items, nb)), dma((docs,)), dma((docs,)), dma],
        compiler_params=pltpu.CompilerParams(collective_id=1, has_side_effects=True, vmem_limit_bytes=60 << 20),
        name="attention_forward",
    )(where, q, k, v, cot, own)


def attention_backward_kernel(size, tile, where, q_ref, k_ref, v_ref, o_ref, g_ref, lse_ref, dq_ref, dk_ref, dv_ref, dqt):
    parts, rows = q_ref.shape[0], q_ref.shape[2]
    n = parts * rows
    blocks = n // size
    q = in_order(q_ref, where, blocks, size)
    k = in_order(k_ref, where, blocks, size)
    v = in_order(v_ref, where, blocks, size)
    o = in_order(o_ref, where, blocks, size)
    g = in_order(g_ref, where, blocks, size)
    kt = k.T
    lane = lax.broadcasted_iota(jnp.int32, (1, 128), 1)
    c = SCORE_SCALE * LOG2E
    tri = lax.broadcasted_iota(jnp.int32, (tile, tile), 0) <= lax.broadcasted_iota(jnp.int32, (tile, tile), 1)
    prod = (o.astype(F32) * g.astype(F32)).astype(BF)
    heads = (lax.broadcasted_iota(jnp.int32, (8, 128), 1) // 64 == lax.broadcasted_iota(jnp.int32, (8, 128), 0)).astype(BF)
    delta = dot(heads, prod, NT)
    zero = jnp.zeros((), BF)
    masks = [(lane < 64) == (h == 0) for h in range(2)]
    qms = [jnp.where(mk, q, zero) for mk in masks]
    gms = [jnp.where(mk, g, zero) for mk in masks]
    lse = lse_ref[0, 0]
    dks, dvs = [], []
    work = [(j, h) for j in range(n // tile) for h in range(2)]

    def products(j, h):
        lo, hi = j * tile, (j + 1) * tile
        return dot(k[lo:hi], qms[h][lo:], NT), dot(v[lo:hi], gms[h][lo:], NT)

    ahead = products(*work[0])
    for t, (j, h) in enumerate(work):
        st, dp = ahead
        if t + 1 < len(work):
            ahead = products(*work[t + 1])
        lo, hi = j * tile, (j + 1) * tile
        p = jnp.exp2(st * c - lse[h:h + 1, lo:])
        diag = jnp.where(tri, p[:, :tile], 0.0)
        p = diag if hi == n else jnp.concatenate([diag, p[:, tile:]], axis=1)
        ds = (p * (dp - delta[h:h + 1, lo:])).astype(BF)
        dvh = dot(p.astype(BF), gms[h][lo:])
        dkh = dot(ds, qms[h][lo:])
        dv = dvh if h == 0 else dv + dvh
        dk = dkh if h == 0 else dk + dkh
        dqh = dot(kt[64 * h:64 * h + 64, lo:hi], ds)
        if j == 0:
            dqt[64 * h:64 * h + 64, :] = dqh
        else:
            dqt[64 * h:64 * h + 64, lo:] += dqh
        if h == 1:
            dks.append((dk * SCORE_SCALE).astype(BF))
            dvs.append(dv.astype(BF))
    store_back(dq_ref, (dqt[...] * SCORE_SCALE).T.astype(BF), where, blocks, size)
    store_back(dk_ref, jnp.concatenate(dks, axis=0), where, blocks, size)
    store_back(dv_ref, jnp.concatenate(dvs, axis=0), where, blocks, size)


def attention_backward(where, q, k, v, o, g, lse, size, tile=256):
    parts, docs, rows, w = q.shape
    pairs = w // 128
    n = parts * rows
    spec = pl.BlockSpec((parts, 1, rows, 128), lambda d, p: (0, d, 0, p))
    return pl.pallas_call(
        functools.partial(attention_backward_kernel, size, tile),
        grid=(docs, pairs),
        in_specs=[pl.BlockSpec(memory_space=pltpu.SMEM)] + [spec] * 5
        + [pl.BlockSpec((1, 1, 2, n), lambda d, p: (d, p, 0, 0))],
        out_specs=[spec] * 3,
        out_shape=[jax.ShapeDtypeStruct(q.shape, BF)] * 3,
        scratch_shapes=[pltpu.VMEM((128, n), F32)],
        compiler_params=pltpu.CompilerParams(vmem_limit_bytes=60 << 20),
        name="attention_backward",
    )(where, q, k, v, o, g, lse)


def middle_kernel(nb, ns, chunk, x_hbm, att_hbm, kept_hbm, cot_hbm, gain_ref, wo_hbm, up_hbm, down_hbm,
                  out_hbm, rg_hbm, mix_hbm,
                  xs, atts, cots, wos, downs, ups, acc, xhs, dn, n2s, invs,
                  send, recv, asend, arecv, msend, mrecv, load, store):
    docs, rows, d = x_hbm.shape
    w = d // ns
    count = ups.shape[0]
    p = Place(nb, ns)
    loads = [pltpu.make_async_copy(wo_hbm, wos, load.at[0])]
    for i in range(docs):
        loads.append(pltpu.make_async_copy(x_hbm.at[i], xs.at[i], load.at[1 + i]))
    loads.append(pltpu.make_async_copy(down_hbm, downs, load.at[1 + docs]))
    for copy in loads:
        copy.start()

    def cot_load(source):
        return pltpu.make_async_copy(source, cots, load.at[2 + docs])

    pl.when(p.stays)(lambda: cot_load(kept_hbm).start())
    pl.when(jnp.logical_not(p.stays))(lambda: cot_load(cot_hbm).start())
    p.greet(p.gather_ways() + [(p.peer(r), None) for r in range(1, ns)])

    def gather(j):
        return Gather(p, up_hbm.at[:, pl.ds(pl.multiple_of(j * chunk, chunk), chunk)], ups.at[j], send.at[j % 3], recv.at[j])

    slots = 6
    listed = gather(0).steps()
    per = -(-len(listed) // (slots - 1))

    def gather_slot(j, slot):
        @pl.when(j < count)
        def _():
            g = gather(j)
            if slot == 0:
                pl.when(j >= 3)(lambda: gather(j - 3).drain())
                g.start()
            else:
                for step in g.steps()[(slot - 1) * per:slot * per]:
                    step()

    def att_away(i, r):
        return pltpu.make_async_remote_copy(
            src_ref=att_hbm.at[flip(p.part, r), i], dst_ref=atts.at[p.part, i], send_sem=asend.at[i, r],
            recv_sem=arecv.at[i, r], device_id=p.peer(r), device_id_type=MESH)

    def att_home(i):
        return pltpu.make_async_copy(att_hbm.at[p.part, i], atts.at[p.part, i], arecv.at[i, 0])

    for i in range(docs):
        att_home(i).start()
        for r in range(1, ns):
            att_away(i, r).start()
    gather_slot(0, 0)
    gather_slot(1, 0)
    loads[0].wait()
    for i in range(docs):
        at = slice(i * rows, (i + 1) * rows)
        loads[1 + i].wait()
        res = xs[i].astype(F32)
        for r in range(ns):
            att_home(i).wait() if r == 0 else att_away(i, r).wait()
            g = flip(p.part, r)
            res = res + dot(atts[g, i], wos[pl.ds(pl.multiple_of(g * w, w), w), :])
        acc[at, :] = res
        xh, inv = normalise(res)
        xhs[at, :] = xh
        invs[at, :] = jnp.broadcast_to(inv, (rows, 128))
        n2s[at, :] = (xh * gain_ref[...]).astype(BF)
        dn[at, :] = jnp.zeros((rows, d), F32)
        for slot in range(1 + 2 * i, 3 + 2 * i):
            if slot < slots:
                gather_slot(0, slot)
    for slot in range(1 + 2 * docs, slots):
        gather_slot(0, slot)
    for slot in range(1, 3):
        gather_slot(1, slot)
    loads[-1].wait()
    cot_load(cot_hbm).wait()

    def one_chunk(f, carry):
        up = ups[f].reshape(d, chunk)
        down = downs[pl.ds(pl.multiple_of(f * chunk, chunk), chunk), :]

        def first(i):
            return dot(n2s[i * rows:(i + 1) * rows, :], up), dot(cots[i], down, NT)

        ahead = first(0)
        for i in range(docs):
            at = slice(i * rows, (i + 1) * rows)
            u, g = ahead
            if i + 1 < docs:
                ahead = first(i + 1)
            act, slope = gelu_parts(u)
            pg = (slope * g).astype(BF)
            acc[at, :] += dot(act.astype(BF), down)
            dn[at, :] += dot(pg, up, NT)
            for slot in range(i * 3 // docs, (i + 1) * 3 // docs):
                gather_slot(f + 2, slot)
                gather_slot(f + 1, slot + 3)
        return carry

    lax.fori_loop(0, count, one_chunk, 0)

    keeps = []
    for i in range(docs):
        at = slice(i * rows, (i + 1) * rows)
        xs[i] = acc[at, :].astype(BF)
        keeps.append(pltpu.make_async_copy(xs.at[i], out_hbm.at[i], store.at[0, i]))
        keeps[-1].start()
        rg = cots[i].astype(F32) + norm_back(xhs[at, :], invs[at, :1], gain_ref[...], dn[at, :])
        xhs[at, :] = rg
        keeps.append(pltpu.make_async_copy(xhs.at[at], rg_hbm.at[i], store.at[1, i]))
        keeps[-1].start()
        mix = dot(rg.astype(BF), wos[...], NT).astype(BF)
        for g in range(ns):
            atts[g, i] = mix[:, g * w:(g + 1) * w]
        home = pltpu.make_async_copy(atts.at[p.part, i], mix_hbm.at[p.part, i], store.at[2, i])
        home.start()
        keeps.append(home)
        for r in range(1, ns):
            away = pltpu.make_async_remote_copy(
                src_ref=atts.at[flip(p.part, r), i], dst_ref=mix_hbm.at[p.part, i], send_sem=msend.at[i, r],
                recv_sem=mrecv.at[i, r], device_id=p.peer(r), device_id_type=MESH)
            away.start()
            keeps.append(away)
    for copy in keeps:
        copy.wait()
    for j in range(max(0, count - 3), count):
        gather(j).drain()


def middle(nb, ns, x, att, kept, cot, gain, wo, up, down, chunk=512):
    docs, rows, d = x.shape
    w = d // ns
    ff = up.shape[1]
    count = ff // chunk
    n = docs * rows
    any_spec = pl.BlockSpec(memory_space=pl.ANY)
    vmem = pl.BlockSpec(memory_space=pltpu.VMEM)
    dma = pltpu.SemaphoreType.DMA
    return pl.pallas_call(
        functools.partial(middle_kernel, nb, ns, chunk),
        in_specs=[any_spec] * 4 + [vmem] + [any_spec] * 3,
        out_specs=[any_spec] * 3,
        out_shape=[jax.ShapeDtypeStruct((docs, rows, d), BF), jax.ShapeDtypeStruct((docs, rows, d), F32),
                   jax.ShapeDtypeStruct((ns, docs, rows, w), BF)],
        scratch_shapes=[pltpu.VMEM((docs, rows, d), BF), pltpu.VMEM((ns, docs, rows, w), BF),
                        pltpu.VMEM((docs, rows, d), BF), pltpu.VMEM(wo.shape, BF), pltpu.VMEM(down.shape, BF),
                        pltpu.VMEM((count, nb, up.shape[0], chunk), BF), pltpu.VMEM((n, d), F32),
                        pltpu.VMEM((n, d), F32), pltpu.VMEM((n, d), F32), pltpu.VMEM((n, d), BF),
                        pltpu.VMEM((n, 128), F32),
                        dma((3, 4, nb)), dma((count, nb)), dma((docs, ns)), dma((docs, ns)),
                        dma((docs, ns)), dma((docs, ns)), dma((3 + docs,)), dma((3, docs))],
        compiler_params=pltpu.CompilerParams(collective_id=2, has_side_effects=True, vmem_limit_bytes=63 << 20),
        name="feed_forward",
    )(x, att, kept, cot, gain, wo, up, down)


def sum_over_devices(p, mine, first, second, total, sends, recvs):
    b, s, nb, ns = p.b, p.s, p.nb, p.ns
    slot, block = b % 16, b - b % 16
    many = nb // 16 * ns
    at = (b // 16) * ns + s

    def scatter(j):
        return pltpu.make_async_remote_copy(
            src_ref=mine.at[flip(slot, j)], dst_ref=first.at[slot], send_sem=sends.at[0, j], recv_sem=recvs.at[0, j],
            device_id=(block + flip(slot, j), s), device_id_type=MESH)

    def share(j):
        to = flip(at, j)
        return pltpu.make_async_remote_copy(
            src_ref=second.at[at], dst_ref=second.at[at], send_sem=sends.at[1, j], recv_sem=recvs.at[1, j],
            device_id=((to // ns) * 16 + slot, to % ns), device_id_type=MESH)

    def spread(j):
        return pltpu.make_async_remote_copy(
            src_ref=total.at[slot], dst_ref=total.at[slot], send_sem=sends.at[2, j], recv_sem=recvs.at[2, j],
            device_id=(block + flip(slot, j), s), device_id_type=MESH)

    for j in range(1, 16):
        scatter(j).start()
    first[slot] = mine[slot]
    for j in range(1, 16):
        scatter(j).wait()
    second[at] = jnp.sum(first[...], axis=0)
    for j in range(1, many):
        share(j).start()
    for j in range(1, many):
        share(j).wait()
    total[slot] = jnp.sum(second[...], axis=0)
    for j in range(1, 16):
        spread(j).start()
    for j in range(1, 16):
        spread(j).wait()


def sum_ways(p):
    b, s, nb, ns = p.b, p.s, p.nb, p.ns
    slot, block = b % 16, b - b % 16
    at = (b // 16) * ns + s
    ways = [((block + flip(slot, j), s), None) for j in range(1, 16)]
    for j in range(1, nb // 16 * ns):
        to = flip(at, j)
        ways.append((((to // ns) * 16 + slot, to % ns), None))
    return ways


def final_kernel(nb, ns, rank, x_hbm, gain_ref, dq_hbm, dk_hbm, dv_hbm, rg_hbm, low_hbm, wq_hbm, wk_hbm, wv_hbm,
                 down_ref, upq_ref, upv_ref, out_hbm, sum_ref,
                 xs, rgs, ds, fgs, lgs, wqs, wks, wvs, lows, outs, gds, gqs, gvs, mine, first, second,
                 load, dsend, drecv, osend, orecv, ssend, srecv):
    docs, rows, d = x_hbm.shape
    w = d // ns
    p = Place(nb, ns)
    grads = (dq_hbm, dk_hbm, dv_hbm)
    loads = [pltpu.make_async_copy(a, v, load.at[n]) for n, (a, v) in enumerate(
        ((wq_hbm, wqs), (wk_hbm, wks), (wv_hbm, wvs), (low_hbm, lows), (x_hbm, xs), (rg_hbm, rgs)))]

    def home(part, i):
        return pltpu.make_async_copy(grads[part].at[p.part, i], ds.at[part, p.part, i], drecv.at[part, i, 0])

    def away(part, i, r):
        return pltpu.make_async_remote_copy(
            src_ref=grads[part].at[flip(p.part, r), i], dst_ref=ds.at[part, p.part, i], send_sem=dsend.at[part, i, r],
            recv_sem=drecv.at[part, i, r], device_id=p.peer(r), device_id_type=MESH)

    def out_away(i):
        return pltpu.make_async_remote_copy(
            src_ref=outs.at[i], dst_ref=out_hbm.at[i], send_sem=osend.at[i], recv_sem=orecv.at[i],
            device_id=p.partner, device_id_type=MESH)

    def out_home(i):
        return pltpu.make_async_copy(outs.at[i], out_hbm.at[i], orecv.at[i])

    for i in range(docs):
        for part in range(3):
            home(part, i).start()
            if i == 0:
                loads[part].start()
    for copy in loads[3:]:
        copy.start()
    p.greet([(p.peer(r), None) for r in range(1, ns)] + [(p.partner, jnp.logical_not(p.stays))] + sum_ways(p))
    for i in range(docs):
        for part in range(3):
            for r in range(1, ns):
                away(part, i, r).start()
    gds[...] = jnp.zeros_like(gds)
    gqs[...] = jnp.zeros_like(gqs)
    gvs[...] = jnp.zeros_like(gvs)
    for r in range(ns):
        g = flip(p.part, r)
        cols = pl.ds(pl.multiple_of(g * w, w), w)
        for i in range(docs):
            fg = None if r == 0 else fgs[i]
            lg = None if r == 0 else lgs[i]
            for part, (full, up, total) in enumerate(((wqs, upq_ref, gqs), (wks, None, None), (wvs, upv_ref, gvs))):
                home(part, i).wait() if r == 0 else away(part, i, r).wait()
                if r == 0 and i == 0:
                    loads[part].wait()
                    if part == 0:
                        loads[3].wait()
                piece = ds[part, g, i]
                y = dot(piece, full[:, :, cols].reshape(d, w), NT)
                fg = y if fg is None else fg + y
                if up is not None:
                    y = dot(piece, up[:, cols], NT)
                    lg = y if lg is None else lg + y
                    total[:, cols] += dot(lows[i], piece, TN)
            if r + 1 < ns:
                fgs[i] = fg
                lgs[i] = lg
                continue
            if i == 0:
                for copy in loads[4:]:
                    copy.wait()
            lgb = lg.astype(BF)
            fg = fg + dot(lgb, down_ref[...], NT)
            xh, inv = normalise(xs[i].astype(F32))
            gds[...] += dot(lgb, (xh * gain_ref[...]).astype(BF), TN)
            outs[i] = (rgs[i] + norm_back(xh, inv, gain_ref[...], fg)).astype(BF)
            pl.when(p.stays)(lambda i=i: out_home(i).start())
            pl.when(jnp.logical_not(p.stays))(lambda i=i: out_away(i).start())
    upper = lax.broadcasted_iota(jnp.int32, (2 * rank, 1), 0) < rank
    both = jnp.where(upper, gqs[:2 * rank, :], gvs[:2 * rank, :]) * ADAPTER_SCALE
    for n in range(8):
        mine[n] = gds[:8, n * 128:(n + 1) * 128]
        mine[8 + n] = both[:, n * 128:(n + 1) * 128]
    sum_over_devices(p, mine, first, second, sum_ref, ssend, srecv)
    for i in range(docs):
        pl.when(p.stays)(lambda i=i: out_home(i).wait())
        pl.when(jnp.logical_not(p.stays))(lambda i=i: out_away(i).wait())


def final(nb, ns, rank, x, gain, dq, dk, dv, rg, low, wq, wk, wv, down, upq, upv):
    docs, rows, d = x.shape
    w = d // ns
    any_spec = pl.BlockSpec(memory_space=pl.ANY)
    vmem = pl.BlockSpec(memory_space=pltpu.VMEM)
    dma = pltpu.SemaphoreType.DMA
    many = max(16, nb // 16 * ns)
    return pl.pallas_call(
        functools.partial(final_kernel, nb, ns, rank),
        in_specs=[any_spec, vmem] + [any_spec] * 8 + [vmem] * 3,
        out_specs=[any_spec, vmem],
        out_shape=[jax.ShapeDtypeStruct(x.shape, BF), jax.ShapeDtypeStruct((16, 8, 128), F32)],
        scratch_shapes=[pltpu.VMEM(x.shape, BF), pltpu.VMEM(x.shape, F32), pltpu.VMEM((3, ns, docs, rows, w), BF),
                        pltpu.VMEM(x.shape, F32), pltpu.VMEM((docs, rows, 128), F32)]
        + [pltpu.VMEM(wq.shape, BF)] * 3
        + [pltpu.VMEM(low.shape, BF), pltpu.VMEM(x.shape, BF)] + [pltpu.VMEM((128, d), F32)] * 3
        + [pltpu.VMEM((16, 8, 128), F32), pltpu.VMEM((16, 8, 128), F32), pltpu.VMEM((nb // 16 * ns, 8, 128), F32),
           dma((6,)), dma((3, docs, ns)), dma((3, docs, ns)), dma((docs,)), dma((docs,)), dma((3, many)), dma((3, many))],
        compiler_params=pltpu.CompilerParams(collective_id=3, has_side_effects=True, vmem_limit_bytes=60 << 20),
        name="projection_gradients",
    )(x, gain, dq, dk, dv, rg, low, wq, wk, wv, down, upq, upv)


def local(
    nb, ns,
    tokens, cotangent, layout, attention_norm_gain, feedforward_norm_gain,
    query_weight, key_weight, value_weight, attention_output_weight, up_weight, down_weight,
    query_down_adapter, query_up_adapter, value_down_adapter, value_up_adapter,
):
    docs, rows, d = tokens.shape
    size = rows * ns // layout.shape[0]
    rank = query_up_adapter.shape[0]
    down = jnp.pad(jnp.concatenate([query_down_adapter, value_down_adapter], axis=1), ((0, 0), (0, 128 - 2 * rank)))
    upq = jnp.pad((ADAPTER_SCALE * query_up_adapter).astype(BF), ((0, 128 - rank), (0, 0)))
    upv = jnp.pad((ADAPTER_SCALE * value_up_adapter).astype(BF), ((rank, 128 - 2 * rank), (0, 0)))
    where = jnp.argsort(layout).astype(jnp.int32)
    gain1 = attention_norm_gain[None]
    gain2 = feedforward_norm_gain[None]

    q, k, v, low, x, wq, wk, wv, wo = project(
        nb, ns, tokens, query_weight, key_weight, value_weight, attention_output_weight, gain1, down, upq, upv)
    att, lse, cot, w_down = attention_forward(nb, ns, where, q, k, v, cotangent, down_weight, size)
    out, rg, mix = middle(nb, ns, x, att, cotangent, cot, gain2, wo.reshape(d, d), up_weight, w_down.reshape(-1, d))
    swap = []
    for b in range(nb):
        for s in range(ns):
            if b % 2 != s % 2:
                b2, s2 = trade(b, s)
                swap.append((b * ns + s, b2 * ns + s2))
    stays = lax.axis_index("batch") % 2 == lax.axis_index("seq") % 2
    layer_out = jnp.where(stays, out, lax.ppermute(out, AXES, swap))
    dq, dk, dv = attention_backward(where, q, k, v, att, mix, lse, size)
    input_grad, sums = final(nb, ns, rank, x, gain1, dq, dk, dv, rg, low, wq, wk, wv, down, upq, upv)
    sums = sums.reshape(2, d // 128, 2 * rank, 128).transpose(0, 2, 1, 3).reshape(2, 2 * rank, d)
    return (layer_out, input_grad, sums[0, :rank].T, sums[1, :rank], sums[0, rank:].T, sums[1, rank:])


def solution(mesh):
    spec = P("batch", "seq", None)
    weight = P("batch", None)
    return jax.shard_map(
        functools.partial(local, mesh.shape["batch"], mesh.shape["seq"]),
        mesh=mesh,
        in_specs=(spec, spec, P(), P(), P()) + (weight,) * 6 + (P(),) * 4,
        out_specs=(spec, spec, P(), P(), P(), P()),
        check_vma=False,
    )
```

```python
import functools
import math

import jax
import jax.numpy as jnp
from jax import lax
from jax.experimental import pallas as pl
from jax.experimental.pallas import tpu as pltpu
from jax.sharding import PartitionSpec as P


EPSILON = 1e-05
ADAPTER_SCALE = 8.0
SCORE_SCALE = 0.125
NEG_FILL = -1e30
GELU_C = 0.7978845608028654
LOG2E = math.log2(math.e)
F32 = jnp.float32
BF = jnp.bfloat16
NN = (((1,), (0,)), ((), ()))
NT = (((1,), (1,)), ((), ()))
TN = (((0,), (0,)), ((), ()))
AXES = ("batch", "seq")


def dot(a, b, dims=NN):
    return lax.dot_general(a, b, dims, preferred_element_type=F32)


def normalise(x):
    mean = jnp.mean(x, axis=-1, keepdims=True)
    centred = x - mean
    inv = lax.rsqrt(jnp.mean(centred * centred, axis=-1, keepdims=True) + EPSILON)
    return centred * inv, inv


def norm_back(xh, inv, gain, up):
    t = up * gain
    return inv * (t - jnp.mean(t, axis=-1, keepdims=True) - xh * jnp.mean(t * xh, axis=-1, keepdims=True))


def gelu_parts(u):
    cubic = 0.044715 * u * u
    th = jnp.tanh(GELU_C * (u + cubic * u))
    half = 0.5 * (1.0 + th)
    return half * u, half + (0.5 * GELU_C) * u * (1.0 - th * th) * (1.0 + 3.0 * cubic)


MESH = pl.DeviceIdType.MESH


def flip(i, bits, width=5):
    out = 0
    for n in range(width):
        bit = 1 << n
        out = out + ((i // bit) % 2 + (bits // bit) % 2) % 2 * bit
    return out


def trade(b, s):
    return b - b % 2 + s % 2, s - s % 2 + b % 2


class Place:
    def __init__(self, nb, ns):
        self.nb, self.ns = nb, ns
        self.b, self.s = lax.axis_index("batch"), lax.axis_index("seq")
        self.lines = nb // 4
        self.line = self.b // 4
        self.partner = trade(self.b, self.s)
        self.stays = self.b % 2 == self.s % 2
        self.doc, self.part = trade(self.b, self.s)

    def peer(self, r):
        return trade(self.doc, flip(self.part, r))

    def greet(self, ways):
        bar = pltpu.get_barrier_semaphore()
        for device, cond in ways:
            def hello(device=device):
                pl.semaphore_signal(bar, inc=1, device_id=device, device_id_type=MESH)
            hello() if cond is None else pl.when(cond)(hello)
        count = 0
        for _, cond in ways:
            count = count + (1 if cond is None else jnp.where(cond, 1, 0))
        pl.semaphore_wait(bar, count)

    def gather_ways(self):
        b, s = self.b, self.s
        return [((b + 4, s), self.line + 1 < self.lines), ((b - 4, s), self.line > 0),
                ((flip(b, 2), s), None), ((flip(b, 1), s), None)]


class Gather:
    def __init__(self, place, own, full, send, recv):
        self.p, self.own, self.full, self.send, self.recv = place, own, full, send, recv

    def part(self, line, pair=0, core=0):
        b = self.p.b
        return line * 4 + (b // 2 + pair) % 2 * 2 + (b + core) % 2

    def copy(self, i, way, src=None):
        p = self.p
        to = [p.b + 4, p.b - 4, self.part(p.line, 1), self.part(p.line, 0, 1)][way]
        return pltpu.make_async_remote_copy(
            src_ref=self.full.at[i] if src is None else src, dst_ref=self.full.at[i],
            send_sem=self.send.at[way, i], recv_sem=self.recv.at[i],
            device_id=(to, p.s), device_id_type=MESH)

    def mine(self):
        return pltpu.make_async_copy(self.own, self.full.at[self.p.b], self.recv.at[self.p.b])

    def start(self):
        p = self.p
        pl.when(p.line + 1 < p.lines)(lambda: self.copy(p.b, 0, self.own).start())
        pl.when(p.line > 0)(lambda: self.copy(p.b, 1, self.own).start())
        self.copy(p.b, 2, self.own).start()
        self.copy(p.b, 3, self.own).start()
        self.mine().start()

    def hop(self, k, pairs=True):
        p = self.p

        def take(way, line):
            i = self.part(line)
            self.copy(i, way).wait_recv()
            more = p.line + 1 < p.lines if way == 0 else p.line > 0
            pl.when(more)(lambda: self.copy(i, way).start())
            if pairs:
                self.copy(i, 2).start()
            self.copy(i, 3).start()

        below, above = p.line - k, p.line + k
        pl.when(below >= 0)(lambda: take(0, below))
        pl.when(above < p.lines)(lambda: take(1, above))

    def pair_line(self, line):
        self.copy(self.part(line), 2).start()

    def relay_line(self, line):
        i = self.part(line, 1)
        self.copy(i, 2).wait_recv()
        self.copy(i, 3).start()

    def relay(self, k):
        p = self.p
        if k == 0:
            self.relay_line(p.line)
        else:
            pl.when(p.line >= k)(lambda: self.relay_line(p.line - k))
            pl.when(p.line + k < p.lines)(lambda: self.relay_line(p.line + k))

    def from_core(self, line, pair):
        self.copy(self.part(line, pair, 1), 3).wait_recv()

    def finish(self):
        self.mine().wait()
        for line in range(self.p.lines):
            for pair in range(2):
                self.from_core(line, pair)

    def drain(self):
        p = self.p
        for line in range(p.lines):
            i = self.part(line)
            pl.when((p.line >= line) & (p.line + 1 < p.lines))(lambda i=i: self.copy(i, 0).wait_send())
            pl.when((p.line <= line) & (p.line > 0))(lambda i=i: self.copy(i, 1).wait_send())
            self.copy(i, 2).wait_send()
            self.copy(i, 3).wait_send()
            self.copy(self.part(line, 1), 3).wait_send()

    def steps(self):
        out = [self.start]
        for k in range(1, self.p.lines):
            out.append(functools.partial(run, [functools.partial(self.hop, k), functools.partial(self.relay, k - 1)]))
        out.append(functools.partial(self.relay, self.p.lines - 1))
        out.append(self.finish)
        return out


def run(calls):
    for call in calls:
        call()


def project_kernel(nb, ns, x_hbm, wq_ref, wk_ref, wv_ref, wo_ref, gain_ref, down_ref, ups_ref,
                   q_out, k_out, v_out, low_out, x_out, wq_out, wk_out, wv_out, wo_out,
                   xs, n1s, stage, lows, ws, send, recv, xsend, xrecv, osend, orecv, local_sem):
    docs, rows, d = x_hbm.shape
    w = d // ns
    p = Place(nb, ns)
    others = [p.peer(r) for r in range(1, ns)]
    p.greet(p.gather_ways() + [(p.partner, jnp.logical_not(p.stays))] + [(o, None) for o in others])

    def x_remote(i):
        return pltpu.make_async_remote_copy(
            src_ref=x_hbm.at[i], dst_ref=xs.at[i], send_sem=xsend.at[i], recv_sem=xrecv.at[i],
            device_id=p.partner, device_id_type=MESH)

    def x_local(i):
        return pltpu.make_async_copy(x_hbm.at[i], xs.at[i], xrecv.at[i])

    def x_keep(i):
        return pltpu.make_async_copy(xs.at[i], x_out.at[i], local_sem.at[i])

    for i in range(docs):
        pl.when(p.stays)(lambda i=i: x_local(i).start())
        pl.when(jnp.logical_not(p.stays))(lambda i=i: x_remote(i).start())

    def first(i):
        pl.when(p.stays)(lambda: x_local(i).wait())
        pl.when(jnp.logical_not(p.stays))(lambda: x_remote(i).wait())
        x_keep(i).start()
        xh, _ = normalise(xs[i].astype(F32))
        n1 = (xh * gain_ref[...]).astype(BF)
        n1s[i] = n1
        lows[i] = dot(n1, down_ref[...]).astype(BF)

    outs = (q_out, k_out, v_out)

    def away(part, i, r):
        return pltpu.make_async_remote_copy(
            src_ref=stage.at[part, i, flip(p.part, r)], dst_ref=outs[part].at[p.part, i],
            send_sem=osend.at[part, i, r], recv_sem=orecv.at[part, i, r],
            device_id=p.peer(r), device_id_type=MESH)

    def home(part, i):
        return pltpu.make_async_copy(stage.at[part, i, p.part], outs[part].at[p.part, i], osend.at[part, i, 0])

    def product(part, i):
        y = dot(n1s[i], ws[part].reshape(d, d)) + dot(lows[i], ups_ref[part])
        y = y.astype(BF)
        for g in range(ns):
            stage[part, i, g] = y[:, g * w:(g + 1) * w]
        for n in range(3):
            @pl.when(part == n)
            def _():
                home(n, i).start()
                for r in range(1, ns):
                    away(n, i, r).start()

    gathers = [Gather(p, own, full, send.at[n], recv.at[n]) for n, (own, full) in enumerate(
        ((wq_ref, ws.at[0]), (wk_ref, ws.at[1]), (wv_ref, ws.at[2]), (wo_ref, ws.at[3])))]
    keeps = [pltpu.make_async_copy(ws.at[n], out, local_sem.at[docs + n])
             for n, out in enumerate((wq_out, wk_out, wv_out, wo_out))]
    low_keep = pltpu.make_async_copy(lows, low_out, local_sem.at[docs + 4])

    lists = [g.steps() for g in gathers]
    delays = (0, 0, 2, 4)
    ready = [len(lists[0]) - 1 + delay for delay in delays]

    def slot(t):
        for n, steps in enumerate(lists):
            if 0 <= t - delays[n] < len(steps):
                steps[t - delays[n]]()
            if t == ready[n]:
                keeps[n].start()

    for t in range(ready[0] + 1):
        slot(t)
    places = {2 * docs - 5 + 2 * n: t for n, t in enumerate(range(ready[0] + 1, ready[3] + 1))}

    def one_product(n, carry):
        early = n < 2 * docs
        part = jnp.where(early, n % 2, 2)
        i = jnp.where(early, n // 2, n - 2 * docs)
        pl.when(early & (part == 0))(lambda: first(i))
        product(part, i)
        for at, t in places.items():
            pl.when(n == at)(functools.partial(slot, t))
        return carry

    lax.fori_loop(0, 3 * docs, one_product, 0)
    low_keep.start()
    for part in range(3):
        for i in range(docs):
            home(part, i).wait()
            for r in range(1, ns):
                away(part, i, r).wait()
    for i in range(docs):
        x_keep(i).wait()
    for keep in keeps:
        keep.wait()
    low_keep.wait()
    for g in gathers:
        g.drain()


def project(nb, ns, x, wq, wk, wv, wo, gain, down, ups):
    docs, rows, d = x.shape
    w = d // ns
    any_spec = pl.BlockSpec(memory_space=pl.ANY)
    vmem = pl.BlockSpec(memory_space=pltpu.VMEM)
    head = jax.ShapeDtypeStruct((ns, docs, rows, w), BF)
    full = jax.ShapeDtypeStruct((nb,) + wq.shape, BF)
    dma = pltpu.SemaphoreType.DMA
    return pl.pallas_call(
        functools.partial(project_kernel, nb, ns),
        in_specs=[any_spec] * 5 + [vmem] * 3,
        out_specs=[any_spec] * 9,
        out_shape=[head] * 3 + [jax.ShapeDtypeStruct((docs, rows, 128), BF), jax.ShapeDtypeStruct(x.shape, BF)] + [full] * 4,
        scratch_shapes=[pltpu.VMEM(x.shape, BF), pltpu.VMEM(x.shape, BF), pltpu.VMEM((3, docs, ns, rows, w), BF),
                        pltpu.VMEM((docs, rows, 128), BF)] + [pltpu.VMEM((4,) + full.shape, BF)] + [
                        dma((4, 4, nb)), dma((4, nb)), dma((docs,)), dma((docs,)),
                        dma((3, docs, ns)), dma((3, docs, ns)), dma((docs + 5,))],
        compiler_params=pltpu.CompilerParams(collective_id=0, has_side_effects=True, vmem_limit_bytes=60 << 20),
        name="projections",
    )(x, wq, wk, wv, wo, gain, down, ups)


def in_order(ref, where, blocks, size):
    per = ref.shape[2] // size
    out = []
    for p in range(blocks):
        s = where[p]
        out.append(ref[s // per, 0, pl.ds(pl.multiple_of((s % per) * size, size), size), :])
    return jnp.concatenate(out, axis=0)


def chosen(blocks, which):
    out = blocks[0]
    for t in range(1, len(blocks)):
        out = jnp.where(which == t, blocks[t], out)
    return out


def picked(ref, where, blocks, size):
    per = ref.shape[2] // size
    stored = [ref[t // per, 0, (t % per) * size:(t % per + 1) * size, :] for t in range(blocks)]
    return jnp.concatenate([chosen(stored, where[p]) for p in range(blocks)], axis=0)


def store_back(ref, value, where, blocks, size):
    per = ref.shape[2] // size
    for t in range(blocks):
        piece = value[:size]
        for p in range(1, blocks):
            piece = jnp.where(where[p] == t, value[p * size:(p + 1) * size], piece)
        ref[t // per, 0, (t % per) * size:(t % per + 1) * size, :] = piece


PACE = 4


def attention_forward_kernel(nb, ns, size, tile, where, q_ref, k_ref, v_ref, cot_hbm, up_hbm,
                             o_ref, lse_ref, cot_out, up_out, own, send, recv, csend, crecv, own_sem):
    docs = cot_hbm.shape[0]
    p = Place(nb, ns)
    step = pl.program_id(0) * pl.num_programs(1) + pl.program_id(1)
    steps = docs * (up_hbm.shape[0] * nb // ns // 128)
    gather = Gather(p, own, up_out, send, recv)
    events = gather.steps()

    def cross(i):
        return pltpu.make_async_remote_copy(
            src_ref=cot_hbm.at[i], dst_ref=cot_out.at[i], send_sem=csend.at[i], recv_sem=crecv.at[i],
            device_id=p.partner, device_id_type=MESH)

    def begin():
        fetch = pltpu.make_async_copy(up_hbm, own, own_sem)
        fetch.start()
        p.greet(p.gather_ways() + [(p.partner, jnp.logical_not(p.stays))])
        fetch.wait()
        events[0]()
        for i in range(docs):
            pl.when(jnp.logical_not(p.stays))(lambda i=i: cross(i).start())

    def end():
        for n, event in enumerate(events):
            if n and PACE * n >= steps:
                event()
        for i in range(docs):
            pl.when(jnp.logical_not(p.stays))(lambda i=i: cross(i).wait())
        gather.drain()

    pl.when(step == 0)(begin)
    for n, event in enumerate(events):
        if n and PACE * n < steps:
            pl.when(step == PACE * n)(event)

    lane = lax.broadcasted_iota(jnp.int32, (1, 128), 1)
    parts, rows = q_ref.shape[0], q_ref.shape[2]
    n = parts * rows
    blocks = n // size
    q = picked(q_ref, where, blocks, size)
    k = picked(k_ref, where, blocks, size)
    v = picked(v_ref, where, blocks, size)
    vt = v.T
    c = SCORE_SCALE * LOG2E
    tri = lax.broadcasted_iota(jnp.int32, (tile, tile), 0) <= lax.broadcasted_iota(jnp.int32, (tile, tile), 1)
    work = [(i, h) for i in range(n // tile) for h in range(2)]
    lses = [[], []]
    mixed = {}

    def scores(i, h):
        qm = jnp.where((lane < 64) == (h == 0), q[i * tile:(i + 1) * tile], jnp.zeros((), BF))
        return dot(k[:(i + 1) * tile], qm, NT)

    ahead = scores(*work[0])
    for t, (i, h) in enumerate(work):
        st = ahead
        if t + 1 < len(work):
            ahead = scores(*work[t + 1])
        kk = (i + 1) * tile
        diag = jnp.where(tri, st[i * tile:], NEG_FILL)
        st = diag if i == 0 else jnp.concatenate([st[: i * tile], diag], axis=0)
        m = jnp.max(st, axis=0, keepdims=True) * c
        e = jnp.exp2(st * c - m)
        l = jnp.sum(e, axis=0, keepdims=True)
        o = dot(vt[64 * h:64 * h + 64, :kk], e.astype(BF))
        mixed[i, h] = o * (1.0 / l)
        lses[h].append(m + jnp.log2(l))
    outs = [jnp.concatenate([mixed[i, 0], mixed[i, 1]], axis=0).T.astype(BF) for i in range(n // tile)]
    store_back(o_ref, jnp.concatenate(outs, axis=0), where, blocks, size)
    for h in range(2):
        lse_ref[0, 0, h:h + 1, :] = jnp.concatenate(lses[h], axis=1)

    pl.when(step == steps - 1)(end)


def attention_forward(nb, ns, where, q, k, v, cot, up, size, tile=256):
    parts, docs, rows, w = q.shape
    pairs = w // 128
    n = parts * rows
    spec = pl.BlockSpec((parts, 1, rows, 128), lambda d, p: (0, d, 0, p))
    any_spec = pl.BlockSpec(memory_space=pl.ANY)
    dma = pltpu.SemaphoreType.DMA
    return pl.pallas_call(
        functools.partial(attention_forward_kernel, nb, ns, size, tile),
        grid=(docs, pairs),
        in_specs=[pl.BlockSpec(memory_space=pltpu.SMEM), spec, spec, spec] + [any_spec] * 2,
        out_specs=[spec, pl.BlockSpec((1, 1, 2, n), lambda d, p: (d, p, 0, 0))] + [any_spec] * 2,
        out_shape=[jax.ShapeDtypeStruct((parts, docs, rows, w), BF),
                   jax.ShapeDtypeStruct((docs, pairs, 2, n), F32),
                   jax.ShapeDtypeStruct(cot.shape, BF),
                   jax.ShapeDtypeStruct((nb,) + up.shape, BF)],
        scratch_shapes=[pltpu.VMEM(up.shape, BF), dma((4, nb)), dma((nb,)), dma((docs,)), dma((docs,)), dma],
        compiler_params=pltpu.CompilerParams(collective_id=1, has_side_effects=True, vmem_limit_bytes=60 << 20),
        name="attention_forward",
    )(where, q, k, v, cot, up)


def attention_backward_kernel(size, tile, where, q_ref, k_ref, v_ref, o_ref, g_ref, lse_ref, dq_ref, dk_ref, dv_ref, dqt):
    parts, rows = q_ref.shape[0], q_ref.shape[2]
    n = parts * rows
    blocks = n // size
    q = in_order(q_ref, where, blocks, size)
    k = in_order(k_ref, where, blocks, size)
    v = in_order(v_ref, where, blocks, size)
    o = in_order(o_ref, where, blocks, size)
    g = in_order(g_ref, where, blocks, size)
    kt = k.T
    lane = lax.broadcasted_iota(jnp.int32, (1, 128), 1)
    c = SCORE_SCALE * LOG2E
    tri = lax.broadcasted_iota(jnp.int32, (tile, tile), 0) <= lax.broadcasted_iota(jnp.int32, (tile, tile), 1)
    prod = (o.astype(F32) * g.astype(F32)).astype(BF)
    heads = (lax.broadcasted_iota(jnp.int32, (8, 128), 1) // 64 == lax.broadcasted_iota(jnp.int32, (8, 128), 0)).astype(BF)
    delta = dot(heads, prod, NT)
    zero = jnp.zeros((), BF)
    masks = [(lane < 64) == (h == 0) for h in range(2)]
    qms = [jnp.where(mk, q, zero) for mk in masks]
    gms = [jnp.where(mk, g, zero) for mk in masks]
    lse = lse_ref[0, 0]
    dks, dvs = [], []
    work = [(j, h) for j in range(n // tile) for h in range(2)]

    def products(j, h):
        lo, hi = j * tile, (j + 1) * tile
        return dot(k[lo:hi], qms[h][lo:], NT), dot(v[lo:hi], gms[h][lo:], NT)

    ahead = products(*work[0])
    for t, (j, h) in enumerate(work):
        st, dp = ahead
        if t + 1 < len(work):
            ahead = products(*work[t + 1])
        lo, hi = j * tile, (j + 1) * tile
        p = jnp.exp2(st * c - lse[h:h + 1, lo:])
        diag = jnp.where(tri, p[:, :tile], 0.0)
        p = diag if hi == n else jnp.concatenate([diag, p[:, tile:]], axis=1)
        ds = (p * (dp - delta[h:h + 1, lo:])).astype(BF)
        dvh = dot(p.astype(BF), gms[h][lo:])
        dkh = dot(ds, qms[h][lo:])
        dv = dvh if h == 0 else dv + dvh
        dk = dkh if h == 0 else dk + dkh
        dqh = dot(kt[64 * h:64 * h + 64, lo:hi], ds)
        if j == 0:
            dqt[64 * h:64 * h + 64, :] = dqh
        else:
            dqt[64 * h:64 * h + 64, lo:] += dqh
        if h == 1:
            dks.append((dk * SCORE_SCALE).astype(BF))
            dvs.append(dv.astype(BF))
    store_back(dq_ref, (dqt[...] * SCORE_SCALE).T.astype(BF), where, blocks, size)
    store_back(dk_ref, jnp.concatenate(dks, axis=0), where, blocks, size)
    store_back(dv_ref, jnp.concatenate(dvs, axis=0), where, blocks, size)


def attention_backward(where, q, k, v, o, g, lse, size, tile=256):
    parts, docs, rows, w = q.shape
    pairs = w // 128
    n = parts * rows
    spec = pl.BlockSpec((parts, 1, rows, 128), lambda d, p: (0, d, 0, p))
    return pl.pallas_call(
        functools.partial(attention_backward_kernel, size, tile),
        grid=(docs, pairs),
        in_specs=[pl.BlockSpec(memory_space=pltpu.SMEM)] + [spec] * 5
        + [pl.BlockSpec((1, 1, 2, n), lambda d, p: (d, p, 0, 0))],
        out_specs=[spec] * 3,
        out_shape=[jax.ShapeDtypeStruct(q.shape, BF)] * 3,
        scratch_shapes=[pltpu.VMEM((128, n), F32)],
        compiler_params=pltpu.CompilerParams(vmem_limit_bytes=60 << 20),
        name="attention_backward",
    )(where, q, k, v, o, g, lse)


def middle_kernel(nb, ns, x_hbm, att_hbm, kept_hbm, cot_hbm, gain_ref, wo_hbm, up_hbm, down_hbm,
                  out_hbm, rg_hbm, mix_hbm,
                  xs, atts, cots, wos, downs, ups, acc, xhs, dn, n2s, invs, us, gs,
                  send, recv, asend, arecv, msend, mrecv, load, store):
    docs, rows, d = x_hbm.shape
    w = d // ns
    p = Place(nb, ns)
    held = down_hbm.shape[0]
    chunk = 2 * held
    loads = [pltpu.make_async_copy(wo_hbm, wos, load.at[0])]
    for i in range(docs):
        loads.append(pltpu.make_async_copy(x_hbm.at[i], xs.at[i], load.at[1 + i]))
    loads.append(pltpu.make_async_copy(up_hbm, ups, load.at[1 + docs]))
    for copy in loads:
        copy.start()

    def cot_load(source):
        return pltpu.make_async_copy(source, cots, load.at[2 + docs])

    pl.when(p.stays)(lambda: cot_load(kept_hbm).start())
    pl.when(jnp.logical_not(p.stays))(lambda: cot_load(cot_hbm).start())
    p.greet(p.gather_ways() + [(p.peer(r), None) for r in range(1, ns)])

    gather = Gather(p, down_hbm, downs, send, recv)

    def att_away(i, r):
        return pltpu.make_async_remote_copy(
            src_ref=att_hbm.at[flip(p.part, r), i], dst_ref=atts.at[p.part, i], send_sem=asend.at[i, r],
            recv_sem=arecv.at[i, r], device_id=p.peer(r), device_id_type=MESH)

    def att_home(i):
        return pltpu.make_async_copy(att_hbm.at[p.part, i], atts.at[p.part, i], arecv.at[i, 0])

    for i in range(docs):
        att_home(i).start()
        for r in range(1, ns):
            att_away(i, r).start()
    gather.start()
    for copy in loads[:-1]:
        copy.wait()
    for i in range(docs):
        att_home(i).wait()
        for r in range(1, ns):
            att_away(i, r).wait()

    def rows_of(i):
        return pl.ds(pl.multiple_of(i * rows, rows), rows)

    def second_norm(i, carry):
        at = rows_of(i)
        res = xs[i].astype(F32)
        for g in range(ns):
            res = res + dot(atts[g, i], wos[g * w:(g + 1) * w, :])
        acc[at, :] = res
        xh, inv = normalise(res)
        xhs[at, :] = xh
        invs[at, :] = jnp.broadcast_to(inv, (rows, 128))
        n2s[at, :] = (xh * gain_ref[...]).astype(BF)
        dn[at, :] = jnp.zeros((rows, d), F32)
        return carry

    lax.fori_loop(0, docs, second_norm, 0)
    loads[-1].wait()
    cot_load(cot_hbm).wait()
    gather.mine().wait()
    pair = p.b // 2 % 2

    def weights(f):
        base = flip(p.line, f // 2) * 4 + (pair + f) % 2 * 2
        up = ups[:, :, pl.ds(pl.multiple_of(base * held, chunk), chunk)].reshape(d, chunk)
        return up, downs[pl.ds(base, 2)].reshape(chunk, d)

    def hidden(t):
        up, down = weights(t // docs)
        us[t % 2] = dot(n2s[rows_of(t % docs), :], up)
        gs[t % 2] = dot(cots[t % docs], down, NT)

    def one_tile(t, carry):
        f, i = t // docs, t % docs

        @pl.when(t + 1 < nb // 2 * docs)
        def _():
            after = (t + 1) // docs
            pl.when(i == docs - 1)(lambda: gather.from_core(flip(p.line, after // 2), after % 2))

            @pl.when((i == docs - 1) & (f % 2 == 0))
            def _():
                pl.when(f // 2 + 1 < p.lines)(lambda: gather.hop(f // 2 + 1, pairs=False))
                pl.when(f // 2 + 1 < p.lines)(lambda: gather.pair_line(flip(p.line, f // 2 + 1)))

            pl.when((i == min(1, docs - 1)) & (f % 2 == 0))(lambda: gather.relay_line(flip(p.line, f // 2)))

        hidden(jnp.minimum(t + 1, nb // 2 * docs - 1))
        up, down = weights(f)
        act, slope = gelu_parts(us[t % 2])
        pg = (slope * gs[t % 2]).astype(BF)
        at = rows_of(i)
        acc[at, :] += dot(act.astype(BF), down)
        dn[at, :] += dot(pg, up, NT)
        return carry

    gather.from_core(p.line, 0)
    hidden(0)
    lax.fori_loop(0, nb // 2 * docs, one_tile, 0)

    def out_and_grad(i, carry):
        at = rows_of(i)
        xs[i] = acc[at, :].astype(BF)
        rg = cots[i].astype(F32) + norm_back(xhs[at, :], invs[at, :1], gain_ref[...], dn[at, :])
        xhs[at, :] = rg
        mix = dot(rg.astype(BF), wos[...], NT).astype(BF)
        for g in range(ns):
            atts[g, i] = mix[:, g * w:(g + 1) * w]
        for copy in results(i):
            copy.start()
        return carry

    def results(i):
        out = [pltpu.make_async_copy(atts.at[p.part, i], mix_hbm.at[p.part, i], store.at[2, i]),
               pltpu.make_async_copy(xs.at[i], out_hbm.at[i], store.at[0, i]),
               pltpu.make_async_copy(xhs.at[rows_of(i)], rg_hbm.at[i], store.at[1, i])]
        for r in range(1, ns):
            out.append(pltpu.make_async_remote_copy(
                src_ref=atts.at[flip(p.part, r), i], dst_ref=mix_hbm.at[p.part, i], send_sem=msend.at[i, r],
                recv_sem=mrecv.at[i, r], device_id=p.peer(r), device_id_type=MESH))
        return out

    lax.fori_loop(0, docs, out_and_grad, 0)
    for i in range(docs):
        for copy in results(i):
            copy.wait()
    gather.drain()


def middle(nb, ns, x, att, kept, cot, gain, wo, up, down):
    docs, rows, d = x.shape
    w = d // ns
    n = docs * rows
    any_spec = pl.BlockSpec(memory_space=pl.ANY)
    vmem = pl.BlockSpec(memory_space=pltpu.VMEM)
    dma = pltpu.SemaphoreType.DMA
    return pl.pallas_call(
        functools.partial(middle_kernel, nb, ns),
        in_specs=[any_spec] * 4 + [vmem] + [any_spec] * 3,
        out_specs=[any_spec] * 3,
        out_shape=[jax.ShapeDtypeStruct((docs, rows, d), BF), jax.ShapeDtypeStruct((docs, rows, d), F32),
                   jax.ShapeDtypeStruct((ns, docs, rows, w), BF)],
        scratch_shapes=[pltpu.VMEM((docs, rows, d), BF), pltpu.VMEM((ns, docs, rows, w), BF),
                        pltpu.VMEM((docs, rows, d), BF), pltpu.VMEM(wo.shape, BF), pltpu.VMEM((nb,) + down.shape, BF),
                        pltpu.VMEM(up.shape, BF), pltpu.VMEM((n, d), F32),
                        pltpu.VMEM((n, d), F32), pltpu.VMEM((n, d), F32), pltpu.VMEM((n, d), BF),
                        pltpu.VMEM((n, 128), F32), pltpu.VMEM((2, rows, 2 * down.shape[0]), F32),
                        pltpu.VMEM((2, rows, 2 * down.shape[0]), F32),
                        dma((4, nb)), dma((nb,)), dma((docs, ns)), dma((docs, ns)),
                        dma((docs, ns)), dma((docs, ns)), dma((3 + docs,)), dma((3, docs))],
        compiler_params=pltpu.CompilerParams(collective_id=2, has_side_effects=True, vmem_limit_bytes=63 << 20),
        name="feed_forward",
    )(x, att, kept, cot, gain, wo, up, down)


def sum_over_devices(p, mine, first, second, total, sends, recvs):
    b, s, nb, ns = p.b, p.s, p.nb, p.ns
    slot, block = b % 16, b - b % 16
    many = nb // 16 * ns
    at = (b // 16) * ns + s

    def scatter(j):
        return pltpu.make_async_remote_copy(
            src_ref=mine.at[flip(slot, j)], dst_ref=first.at[slot], send_sem=sends.at[0, j], recv_sem=recvs.at[0, j],
            device_id=(block + flip(slot, j), s), device_id_type=MESH)

    def share(j):
        to = flip(at, j)
        return pltpu.make_async_remote_copy(
            src_ref=second.at[at], dst_ref=second.at[at], send_sem=sends.at[1, j], recv_sem=recvs.at[1, j],
            device_id=((to // ns) * 16 + slot, to % ns), device_id_type=MESH)

    def spread(j):
        return pltpu.make_async_remote_copy(
            src_ref=total.at[slot], dst_ref=total.at[slot], send_sem=sends.at[2, j], recv_sem=recvs.at[2, j],
            device_id=(block + flip(slot, j), s), device_id_type=MESH)

    for j in range(1, 16):
        scatter(j).start()
    first[slot] = mine[slot]
    for j in range(1, 16):
        scatter(j).wait()
    second[at] = jnp.sum(first[...], axis=0)
    for j in range(1, many):
        share(j).start()
    for j in range(1, many):
        share(j).wait()
    total[slot] = jnp.sum(second[...], axis=0)
    for j in range(1, 16):
        spread(j).start()
    for j in range(1, 16):
        spread(j).wait()


def sum_ways(p):
    b, s, nb, ns = p.b, p.s, p.nb, p.ns
    slot, block = b % 16, b - b % 16
    at = (b // 16) * ns + s
    ways = [((block + flip(slot, j), s), None) for j in range(1, 16)]
    for j in range(1, nb // 16 * ns):
        to = flip(at, j)
        ways.append((((to // ns) * 16 + slot, to % ns), None))
    return ways


def final_kernel(nb, ns, rank, x_hbm, gain_ref, dq_hbm, dk_hbm, dv_hbm, rg_hbm, low_hbm, wq_hbm, wk_hbm, wv_hbm,
                 down_ref, upq_ref, upv_ref, out_hbm, sum_ref,
                 xs, rgs, ds, wqs, wks, wvs, lows, outs, gds, gqs, gvs, mine, first, second,
                 load, dsend, drecv, osend, orecv, ssend, srecv):
    docs, rows, d = x_hbm.shape
    w = d // ns
    p = Place(nb, ns)
    grads = (dq_hbm, dk_hbm, dv_hbm)
    loads = [pltpu.make_async_copy(a, v, load.at[n]) for n, (a, v) in enumerate(
        ((wq_hbm, wqs), (wk_hbm, wks), (wv_hbm, wvs), (low_hbm, lows), (x_hbm, xs), (rg_hbm, rgs)))]

    def home(part, i):
        return pltpu.make_async_copy(grads[part].at[p.part, i], ds.at[part, p.part, i], drecv.at[part, i, 0])

    def away(part, i, r):
        return pltpu.make_async_remote_copy(
            src_ref=grads[part].at[flip(p.part, r), i], dst_ref=ds.at[part, p.part, i], send_sem=dsend.at[part, i, r],
            recv_sem=drecv.at[part, i, r], device_id=p.peer(r), device_id_type=MESH)

    def out_away(i):
        return pltpu.make_async_remote_copy(
            src_ref=outs.at[i], dst_ref=out_hbm.at[i], send_sem=osend.at[i], recv_sem=orecv.at[i],
            device_id=p.partner, device_id_type=MESH)

    def out_home(i):
        return pltpu.make_async_copy(outs.at[i], out_hbm.at[i], orecv.at[i])

    for i in range(docs):
        for part in range(3):
            home(part, i).start()
            if i == 0:
                loads[part].start()
    for copy in loads[3:]:
        copy.start()
    p.greet([(p.peer(r), None) for r in range(1, ns)] + [(p.partner, jnp.logical_not(p.stays))] + sum_ways(p))
    for i in range(docs):
        for part in range(3):
            for r in range(1, ns):
                away(part, i, r).start()
    gds[...] = jnp.zeros_like(gds)
    gqs[...] = jnp.zeros_like(gqs)
    gvs[...] = jnp.zeros_like(gvs)
    for copy in loads[:4]:
        copy.wait()
    def one_document(i, carry):
        fg = lg = None
        for r in range(ns):
            g = flip(p.part, r)
            cols = pl.ds(pl.multiple_of(g * w, w), w)
            for part, (full, up, total) in enumerate(((wqs, upq_ref, gqs), (wks, None, None), (wvs, upv_ref, gvs))):
                home(part, i).wait() if r == 0 else away(part, i, r).wait()
                piece = ds[part, g, i]
                y = dot(piece, full[:, :, cols].reshape(d, w), NT)
                fg = y if fg is None else fg + y
                if up is not None:
                    y = dot(piece, up[:, cols], NT)
                    lg = y if lg is None else lg + y
                    total[:, cols] += dot(lows[i], piece, TN)

        @pl.when(i == 0)
        def _():
            for copy in loads[4:]:
                copy.wait()

        lgb = lg.astype(BF)
        fg = fg + dot(lgb, down_ref[...], NT)
        xh, inv = normalise(xs[i].astype(F32))
        gds[...] += dot(lgb, (xh * gain_ref[...]).astype(BF), TN)
        outs[i] = (rgs[i] + norm_back(xh, inv, gain_ref[...], fg)).astype(BF)
        pl.when(p.stays)(lambda: out_home(i).start())
        pl.when(jnp.logical_not(p.stays))(lambda: out_away(i).start())
        return carry

    lax.fori_loop(0, docs, one_document, 0)
    upper = lax.broadcasted_iota(jnp.int32, (2 * rank, 1), 0) < rank
    both = jnp.where(upper, gqs[:2 * rank, :], gvs[:2 * rank, :]) * ADAPTER_SCALE
    for n in range(8):
        mine[n] = gds[:8, n * 128:(n + 1) * 128]
        mine[8 + n] = both[:, n * 128:(n + 1) * 128]
    sum_over_devices(p, mine, first, second, sum_ref, ssend, srecv)
    for i in range(docs):
        pl.when(p.stays)(lambda i=i: out_home(i).wait())
        pl.when(jnp.logical_not(p.stays))(lambda i=i: out_away(i).wait())


def final(nb, ns, rank, x, gain, dq, dk, dv, rg, low, wq, wk, wv, down, upq, upv):
    docs, rows, d = x.shape
    w = d // ns
    any_spec = pl.BlockSpec(memory_space=pl.ANY)
    vmem = pl.BlockSpec(memory_space=pltpu.VMEM)
    dma = pltpu.SemaphoreType.DMA
    many = max(16, nb // 16 * ns)
    return pl.pallas_call(
        functools.partial(final_kernel, nb, ns, rank),
        in_specs=[any_spec, vmem] + [any_spec] * 8 + [vmem] * 3,
        out_specs=[any_spec, vmem],
        out_shape=[jax.ShapeDtypeStruct(x.shape, BF), jax.ShapeDtypeStruct((16, 8, 128), F32)],
        scratch_shapes=[pltpu.VMEM(x.shape, BF), pltpu.VMEM(x.shape, F32), pltpu.VMEM((3, ns, docs, rows, w), BF),]
        + [pltpu.VMEM(wq.shape, BF)] * 3
        + [pltpu.VMEM(low.shape, BF), pltpu.VMEM(x.shape, BF)] + [pltpu.VMEM((128, d), F32)] * 3
        + [pltpu.VMEM((16, 8, 128), F32), pltpu.VMEM((16, 8, 128), F32), pltpu.VMEM((nb // 16 * ns, 8, 128), F32),
           dma((6,)), dma((3, docs, ns)), dma((3, docs, ns)), dma((docs,)), dma((docs,)), dma((3, many)), dma((3, many))],
        compiler_params=pltpu.CompilerParams(collective_id=3, has_side_effects=True, vmem_limit_bytes=60 << 20),
        name="projection_gradients",
    )(x, gain, dq, dk, dv, rg, low, wq, wk, wv, down, upq, upv)


def local(
    nb, ns,
    tokens, cotangent, layout, attention_norm_gain, feedforward_norm_gain,
    query_weight, key_weight, value_weight, attention_output_weight, up_weight, down_weight,
    query_down_adapter, query_up_adapter, value_down_adapter, value_up_adapter,
):
    docs, rows, d = tokens.shape
    size = rows * ns // layout.shape[0]
    rank = query_up_adapter.shape[0]
    down = jnp.pad(jnp.concatenate([query_down_adapter, value_down_adapter], axis=1), ((0, 0), (0, 128 - 2 * rank)))
    upq = jnp.pad((ADAPTER_SCALE * query_up_adapter).astype(BF), ((0, 128 - rank), (0, 0)))
    upv = jnp.pad((ADAPTER_SCALE * value_up_adapter).astype(BF), ((rank, 128 - 2 * rank), (0, 0)))
    where = jnp.argsort(layout).astype(jnp.int32)
    gain1 = attention_norm_gain[None]
    gain2 = feedforward_norm_gain[None]

    q, k, v, low, x, wq, wk, wv, wo = project(
        nb, ns, tokens, query_weight, key_weight, value_weight, attention_output_weight, gain1, down,
        jnp.stack([upq, jnp.zeros_like(upq), upv]))
    att, lse, cot, w_up = attention_forward(nb, ns, where, q, k, v, cotangent, up_weight, size)
    out, rg, mix = middle(nb, ns, x, att, cotangent, cot, gain2, wo.reshape(d, d), w_up, down_weight)
    swap = []
    for b in range(nb):
        for s in range(ns):
            if b % 2 != s % 2:
                b2, s2 = trade(b, s)
                swap.append((b * ns + s, b2 * ns + s2))
    stays = lax.axis_index("batch") % 2 == lax.axis_index("seq") % 2
    layer_out = jnp.where(stays, out, lax.ppermute(out, AXES, swap))
    dq, dk, dv = attention_backward(where, q, k, v, att, mix, lse, size)
    input_grad, sums = final(nb, ns, rank, x, gain1, dq, dk, dv, rg, low, wq, wk, wv, down, upq, upv)
    sums = sums.reshape(2, d // 128, 2 * rank, 128).transpose(0, 2, 1, 3).reshape(2, 2 * rank, d)
    return (layer_out, input_grad, sums[0, :rank].T, sums[1, :rank], sums[0, rank:].T, sums[1, rank:])


def solution(mesh):
    spec = P("batch", "seq", None)
    weight = P("batch", None)
    return jax.shard_map(
        functools.partial(local, mesh.shape["batch"], mesh.shape["seq"]),
        mesh=mesh,
        in_specs=(spec, spec, P(), P(), P()) + (weight,) * 6 + (P(),) * 4,
        out_specs=(spec, spec, P(), P(), P(), P()),
        check_vma=False,
    )
```

```python
import functools
import math

import jax
import jax.numpy as jnp
from jax import lax
from jax.experimental import pallas as pl
from jax.experimental.pallas import tpu as pltpu
from jax.sharding import PartitionSpec as P


EPSILON = 1e-05
ADAPTER_SCALE = 8.0
SCORE_SCALE = 0.125
NEG_FILL = -1e30
GELU_C = 0.7978845608028654
LOG2E = math.log2(math.e)
F32 = jnp.float32
BF = jnp.bfloat16
NN = (((1,), (0,)), ((), ()))
NT = (((1,), (1,)), ((), ()))
TN = (((0,), (0,)), ((), ()))


def dot(a, b, dims=NN):
    return lax.dot_general(a, b, dims, preferred_element_type=F32)


def normalise(x):
    mean = jnp.mean(x, axis=-1, keepdims=True)
    centred = x - mean
    inv = lax.rsqrt(jnp.mean(centred * centred, axis=-1, keepdims=True) + EPSILON)
    return centred * inv, inv


def norm_back(xh, inv, gain, up):
    t = up * gain
    return inv * (t - jnp.mean(t, axis=-1, keepdims=True) - xh * jnp.mean(t * xh, axis=-1, keepdims=True))


def gelu_parts(u):
    cubic = 0.044715 * u * u
    th = jnp.tanh(GELU_C * (u + cubic * u))
    half = 0.5 * (1.0 + th)
    return half * u, half + (0.5 * GELU_C) * u * (1.0 - th * th) * (1.0 + 3.0 * cubic)


MESH = pl.DeviceIdType.MESH


def flip(i, bits, width=5):
    out = 0
    for n in range(width):
        bit = 1 << n
        out = out + ((i // bit) % 2 + (bits // bit) % 2) % 2 * bit
    return out


def trade(b, s):
    return b - b % 2 + s % 2, s - s % 2 + b % 2


class Place:
    def __init__(self, nb, ns):
        self.nb, self.ns = nb, ns
        self.b, self.s = lax.axis_index("batch"), lax.axis_index("seq")
        self.lines = nb // 4
        self.line = self.b // 4
        self.partner = trade(self.b, self.s)
        self.stays = self.b % 2 == self.s % 2
        self.doc, self.part = trade(self.b, self.s)

    def peer(self, r):
        return trade(self.doc, flip(self.part, r))

    def greet(self, ways):
        bar = pltpu.get_barrier_semaphore()
        for device, cond in ways:
            def hello(device=device):
                pl.semaphore_signal(bar, inc=1, device_id=device, device_id_type=MESH)
            hello() if cond is None else pl.when(cond)(hello)
        count = 0
        for _, cond in ways:
            count = count + (1 if cond is None else jnp.where(cond, 1, 0))
        pl.semaphore_wait(bar, count)

    def gather_ways(self):
        b, s = self.b, self.s
        return [((b + 4, s), self.line + 1 < self.lines), ((b - 4, s), self.line > 0),
                ((flip(b, 2), s), None), ((flip(b, 1), s), None)]


class Gather:
    def __init__(self, place, own, full, send, recv):
        self.p, self.own, self.full, self.send, self.recv = place, own, full, send, recv

    def part(self, line, pair=0, core=0):
        b = self.p.b
        return line * 4 + (b // 2 + pair) % 2 * 2 + (b + core) % 2

    def copy(self, i, way, src=None):
        p = self.p
        to = [p.b + 4, p.b - 4, self.part(p.line, 1), self.part(p.line, 0, 1)][way]
        return pltpu.make_async_remote_copy(
            src_ref=self.full.at[i] if src is None else src, dst_ref=self.full.at[i],
            send_sem=self.send.at[way, i], recv_sem=self.recv.at[i],
            device_id=(to, p.s), device_id_type=MESH)

    def mine(self):
        return pltpu.make_async_copy(self.own, self.full.at[self.p.b], self.recv.at[self.p.b])

    def start(self):
        p = self.p
        pl.when(p.line + 1 < p.lines)(lambda: self.copy(p.b, 0, self.own).start())
        pl.when(p.line > 0)(lambda: self.copy(p.b, 1, self.own).start())
        self.copy(p.b, 2, self.own).start()
        self.copy(p.b, 3, self.own).start()
        self.mine().start()

    def hop(self, k, pairs=True):
        p = self.p

        def take(way, line):
            i = self.part(line)
            self.copy(i, way).wait_recv()
            more = p.line + 1 < p.lines if way == 0 else p.line > 0
            pl.when(more)(lambda: self.copy(i, way).start())
            if pairs:
                self.copy(i, 2).start()
            self.copy(i, 3).start()

        below, above = p.line - k, p.line + k
        pl.when(below >= 0)(lambda: take(0, below))
        pl.when(above < p.lines)(lambda: take(1, above))

    def pair_line(self, line):
        self.copy(self.part(line), 2).start()

    def relay_line(self, line):
        i = self.part(line, 1)
        self.copy(i, 2).wait_recv()
        self.copy(i, 3).start()

    def relay(self, k):
        p = self.p
        if k == 0:
            self.relay_line(p.line)
        else:
            pl.when(p.line >= k)(lambda: self.relay_line(p.line - k))
            pl.when(p.line + k < p.lines)(lambda: self.relay_line(p.line + k))

    def from_core(self, line, pair):
        self.copy(self.part(line, pair, 1), 3).wait_recv()

    def finish(self):
        self.mine().wait()
        for line in range(self.p.lines):
            for pair in range(2):
                self.from_core(line, pair)

    def drain(self):
        p = self.p
        for line in range(p.lines):
            i = self.part(line)
            pl.when((p.line >= line) & (p.line + 1 < p.lines))(lambda i=i: self.copy(i, 0).wait_send())
            pl.when((p.line <= line) & (p.line > 0))(lambda i=i: self.copy(i, 1).wait_send())
            self.copy(i, 2).wait_send()
            self.copy(i, 3).wait_send()
            self.copy(self.part(line, 1), 3).wait_send()

    def steps(self):
        out = [self.start]
        for k in range(1, self.p.lines):
            out.append(functools.partial(run, [functools.partial(self.hop, k), functools.partial(self.relay, k - 1)]))
        out.append(functools.partial(self.relay, self.p.lines - 1))
        out.append(self.finish)
        return out


def run(calls):
    for call in calls:
        call()


def project_kernel(nb, ns, x_hbm, wq_ref, wk_ref, wv_ref, wo_ref, gain_ref, down_ref, ups_ref,
                   q_out, k_out, v_out, low_out, x_out, wq_out, wk_out, wv_out, wo_out,
                   xs, n1s, stage, lows, ws, send, recv, xsend, xrecv, osend, orecv, local_sem):
    docs, rows, d = x_hbm.shape
    w = d // ns
    p = Place(nb, ns)
    others = [p.peer(r) for r in range(1, ns)]
    p.greet(p.gather_ways() + [(p.partner, jnp.logical_not(p.stays))] + [(o, None) for o in others])

    def x_remote(i):
        return pltpu.make_async_remote_copy(
            src_ref=x_hbm.at[i], dst_ref=xs.at[i], send_sem=xsend.at[i], recv_sem=xrecv.at[i],
            device_id=p.partner, device_id_type=MESH)

    def x_local(i):
        return pltpu.make_async_copy(x_hbm.at[i], xs.at[i], xrecv.at[i])

    def x_keep(i):
        return pltpu.make_async_copy(xs.at[i], x_out.at[i], local_sem.at[i])

    for i in range(docs):
        pl.when(p.stays)(lambda i=i: x_local(i).start())
        pl.when(jnp.logical_not(p.stays))(lambda i=i: x_remote(i).start())

    def first(i):
        pl.when(p.stays)(lambda: x_local(i).wait())
        pl.when(jnp.logical_not(p.stays))(lambda: x_remote(i).wait())
        x_keep(i).start()
        xh, _ = normalise(xs[i].astype(F32))
        n1 = (xh * gain_ref[...]).astype(BF)
        n1s[i] = n1
        lows[i] = dot(n1, down_ref[...]).astype(BF)

    outs = (q_out, k_out, v_out)

    def away(part, i, r):
        return pltpu.make_async_remote_copy(
            src_ref=stage.at[part, i, flip(p.part, r)], dst_ref=outs[part].at[p.part, i],
            send_sem=osend.at[part, i, r], recv_sem=orecv.at[part, i, r],
            device_id=p.peer(r), device_id_type=MESH)

    def home(part, i):
        return pltpu.make_async_copy(stage.at[part, i, p.part], outs[part].at[p.part, i], osend.at[part, i, 0])

    def product(part, i):
        y = dot(n1s[i], ws[part].reshape(d, d)) + dot(lows[i], ups_ref[part])
        y = y.astype(BF)
        for g in range(ns):
            stage[part, i, g] = y[:, g * w:(g + 1) * w]
        for n in range(3):
            @pl.when(part == n)
            def _():
                home(n, i).start()
                for r in range(1, ns):
                    away(n, i, r).start()

    gathers = [Gather(p, own, full, send.at[n], recv.at[n]) for n, (own, full) in enumerate(
        ((wq_ref, ws.at[0]), (wk_ref, ws.at[1]), (wv_ref, ws.at[2]), (wo_ref, ws.at[3])))]
    keeps = [pltpu.make_async_copy(ws.at[n], out, local_sem.at[docs + n])
             for n, out in enumerate((wq_out, wk_out, wv_out, wo_out))]
    low_keep = pltpu.make_async_copy(lows, low_out, local_sem.at[docs + 4])

    lists = [g.steps() for g in gathers]
    delays = (0, 0, 2, 4)
    ready = [len(lists[0]) - 1 + delay for delay in delays]

    def slot(t):
        for n, steps in enumerate(lists):
            if 0 <= t - delays[n] < len(steps):
                steps[t - delays[n]]()
            if t == ready[n]:
                keeps[n].start()

    for t in range(ready[0] + 1):
        slot(t)
    places = {2 * docs - 5 + 2 * n: t for n, t in enumerate(range(ready[0] + 1, ready[3] + 1))}

    def one_product(n, carry):
        early = n < 2 * docs
        part = jnp.where(early, n % 2, 2)
        i = jnp.where(early, n // 2, n - 2 * docs)
        pl.when(early & (part == 0))(lambda: first(i))
        product(part, i)
        for at, t in places.items():
            pl.when(n == at)(functools.partial(slot, t))
        return carry

    lax.fori_loop(0, 3 * docs, one_product, 0)
    low_keep.start()
    for part in range(3):
        for i in range(docs):
            home(part, i).wait()
            for r in range(1, ns):
                away(part, i, r).wait()
    for i in range(docs):
        x_keep(i).wait()
    for keep in keeps:
        keep.wait()
    low_keep.wait()
    for g in gathers:
        g.drain()


def project(nb, ns, x, wq, wk, wv, wo, gain, down, ups):
    docs, rows, d = x.shape
    w = d // ns
    any_spec = pl.BlockSpec(memory_space=pl.ANY)
    vmem = pl.BlockSpec(memory_space=pltpu.VMEM)
    head = jax.ShapeDtypeStruct((ns, docs, rows, w), BF)
    full = jax.ShapeDtypeStruct((nb,) + wq.shape, BF)
    dma = pltpu.SemaphoreType.DMA
    return pl.pallas_call(
        functools.partial(project_kernel, nb, ns),
        in_specs=[any_spec] * 5 + [vmem] * 3,
        out_specs=[any_spec] * 9,
        out_shape=[head] * 3 + [jax.ShapeDtypeStruct((docs, rows, 128), BF), jax.ShapeDtypeStruct(x.shape, BF)] + [full] * 4,
        scratch_shapes=[pltpu.VMEM(x.shape, BF), pltpu.VMEM(x.shape, BF), pltpu.VMEM((3, docs, ns, rows, w), BF),
                        pltpu.VMEM((docs, rows, 128), BF)] + [pltpu.VMEM((4,) + full.shape, BF)] + [
                        dma((4, 4, nb)), dma((4, nb)), dma((docs,)), dma((docs,)),
                        dma((3, docs, ns)), dma((3, docs, ns)), dma((docs + 5,))],
        compiler_params=pltpu.CompilerParams(collective_id=0, has_side_effects=True, vmem_limit_bytes=60 << 20),
        name="projections",
    )(x, wq, wk, wv, wo, gain, down, ups)


def chosen(blocks, tests):
    out = blocks[0]
    for block, test in zip(blocks[1:], tests[1:]):
        out = jnp.where(test, block, out)
    return out


def picked(ref, layout, blocks, size):
    per = ref.shape[2] // size
    stored = [ref[t // per, 0, (t % per) * size:(t % per + 1) * size, :] for t in range(blocks)]
    return jnp.concatenate([chosen(stored, [layout[t] == p for t in range(blocks)]) for p in range(blocks)], axis=0)


def put_back(value, layout, blocks, size, store):
    pieces = [value[p * size:(p + 1) * size] for p in range(blocks)]
    for t in range(blocks):
        store(t, chosen(pieces, [layout[t] == p for p in range(blocks)]))


PACE = 4


def attention_forward_kernel(nb, ns, size, tile, layout, q_ref, k_ref, v_ref, cot_hbm, up_hbm,
                             o_ref, lse_ref, cot_out, up_out, own, send, recv, csend, crecv, own_sem):
    docs = cot_hbm.shape[0]
    p = Place(nb, ns)
    step = pl.program_id(0) * pl.num_programs(1) + pl.program_id(1)
    steps = docs * (up_hbm.shape[0] * nb // ns // 128)
    gather = Gather(p, own, up_out, send, recv)
    events = gather.steps()

    def cross(i):
        return pltpu.make_async_remote_copy(
            src_ref=cot_hbm.at[i], dst_ref=cot_out.at[i], send_sem=csend.at[i], recv_sem=crecv.at[i],
            device_id=p.partner, device_id_type=MESH)

    def begin():
        fetch = pltpu.make_async_copy(up_hbm, own, own_sem)
        fetch.start()
        p.greet(p.gather_ways() + [(p.partner, jnp.logical_not(p.stays))])
        fetch.wait()
        events[0]()
        for i in range(docs):
            pl.when(jnp.logical_not(p.stays))(lambda i=i: cross(i).start())

    def end():
        for n, event in enumerate(events):
            if n and PACE * n >= steps:
                event()
        for i in range(docs):
            pl.when(jnp.logical_not(p.stays))(lambda i=i: cross(i).wait())
        gather.drain()

    pl.when(step == 0)(begin)
    for n, event in enumerate(events):
        if n and PACE * n < steps:
            pl.when(step == PACE * n)(event)

    lane = lax.broadcasted_iota(jnp.int32, (1, 128), 1)
    parts, rows = q_ref.shape[0], q_ref.shape[2]
    n = parts * rows
    blocks = n // size
    q = picked(q_ref, layout, blocks, size)
    k = picked(k_ref, layout, blocks, size)
    v = picked(v_ref, layout, blocks, size)
    vt = v.T
    c = SCORE_SCALE * LOG2E
    tri = lax.broadcasted_iota(jnp.int32, (tile, tile), 0) <= lax.broadcasted_iota(jnp.int32, (tile, tile), 1)
    work = [(i, h) for i in range(n // tile) for h in range(2)]
    lses = [[], []]
    mixed = {}

    def scores(i, h):
        qm = jnp.where((lane < 64) == (h == 0), q[i * tile:(i + 1) * tile], jnp.zeros((), BF))
        return dot(k[:(i + 1) * tile], qm, NT)

    ahead = scores(*work[0])
    for t, (i, h) in enumerate(work):
        st = ahead
        if t + 1 < len(work):
            ahead = scores(*work[t + 1])
        kk = (i + 1) * tile
        diag = jnp.where(tri, st[i * tile:], NEG_FILL)
        st = diag if i == 0 else jnp.concatenate([st[: i * tile], diag], axis=0)
        m = jnp.max(st, axis=0, keepdims=True) * c
        e = jnp.exp2(st * c - m)
        l = jnp.sum(e, axis=0, keepdims=True)
        o = dot(vt[64 * h:64 * h + 64, :kk], e.astype(BF))
        mixed[i, h] = o * (1.0 / l)
        lses[h].append(m + jnp.log2(l))
    outs = [jnp.concatenate([mixed[i, 0], mixed[i, 1]], axis=0).T.astype(BF) for i in range(n // tile)]
    per = rows // size

    def store(t, piece):
        o_ref[t // per, 0, t % per * size:(t % per + 1) * size, :] = piece

    put_back(jnp.concatenate(outs, axis=0), layout, blocks, size, store)
    for h in range(2):
        lse_ref[0, 0, h:h + 1, :] = jnp.concatenate(lses[h], axis=1)

    pl.when(step == steps - 1)(end)


def attention_forward(nb, ns, layout, q, k, v, cot, up, size, tile=256):
    parts, docs, rows, w = q.shape
    pairs = w // 128
    n = parts * rows
    spec = pl.BlockSpec((parts, 1, rows, 128), lambda d, p: (0, d, 0, p))
    any_spec = pl.BlockSpec(memory_space=pl.ANY)
    dma = pltpu.SemaphoreType.DMA
    return pl.pallas_call(
        functools.partial(attention_forward_kernel, nb, ns, size, tile),
        grid=(docs, pairs),
        in_specs=[pl.BlockSpec(memory_space=pltpu.SMEM), spec, spec, spec] + [any_spec] * 2,
        out_specs=[spec, pl.BlockSpec((1, 1, 2, n), lambda d, p: (d, p, 0, 0))] + [any_spec] * 2,
        out_shape=[jax.ShapeDtypeStruct((parts, docs, rows, w), BF),
                   jax.ShapeDtypeStruct((docs, pairs, 2, n), F32),
                   jax.ShapeDtypeStruct(cot.shape, BF),
                   jax.ShapeDtypeStruct((nb,) + up.shape, BF)],
        scratch_shapes=[pltpu.VMEM(up.shape, BF), dma((4, nb)), dma((nb,)), dma((docs,)), dma((docs,)), dma],
        compiler_params=pltpu.CompilerParams(collective_id=1, has_side_effects=True, vmem_limit_bytes=60 << 20),
        name="attention_forward",
    )(layout, q, k, v, cot, up)


def middle_kernel(nb, ns, x_hbm, att_hbm, kept_hbm, cot_hbm, gain_ref, wo_hbm, up_hbm, down_hbm,
                  out_hbm, rg_hbm, mix_hbm,
                  xs, atts, cots, wos, downs, ups, acc, xhs, dn, n2s, invs, us, gs,
                  send, recv, asend, arecv, msend, mrecv, load, store):
    docs, rows, d = x_hbm.shape
    w = d // ns
    p = Place(nb, ns)
    held = down_hbm.shape[0]
    chunk = 2 * held
    loads = [pltpu.make_async_copy(wo_hbm, wos, load.at[0])]
    for i in range(docs):
        loads.append(pltpu.make_async_copy(x_hbm.at[i], xs.at[i], load.at[1 + i]))
    loads.append(pltpu.make_async_copy(up_hbm, ups, load.at[1 + docs]))
    for copy in loads:
        copy.start()

    def cot_load(source):
        return pltpu.make_async_copy(source, cots, load.at[2 + docs])

    pl.when(p.stays)(lambda: cot_load(kept_hbm).start())
    pl.when(jnp.logical_not(p.stays))(lambda: cot_load(cot_hbm).start())
    p.greet(p.gather_ways() + [(p.peer(r), None) for r in range(1, ns)])

    gather = Gather(p, down_hbm, downs, send, recv)

    def att_away(i, r):
        return pltpu.make_async_remote_copy(
            src_ref=att_hbm.at[flip(p.part, r), i], dst_ref=atts.at[p.part, i], send_sem=asend.at[i, r],
            recv_sem=arecv.at[i, r], device_id=p.peer(r), device_id_type=MESH)

    def att_home(i):
        return pltpu.make_async_copy(att_hbm.at[p.part, i], atts.at[p.part, i], arecv.at[i, 0])

    for i in range(docs):
        att_home(i).start()
        for r in range(1, ns):
            att_away(i, r).start()
    gather.start()
    for copy in loads[:-1]:
        copy.wait()
    for i in range(docs):
        att_home(i).wait()
        for r in range(1, ns):
            att_away(i, r).wait()

    def rows_of(i):
        return pl.ds(pl.multiple_of(i * rows, rows), rows)

    def second_norm(i, carry):
        at = rows_of(i)
        res = xs[i].astype(F32)
        for g in range(ns):
            res = res + dot(atts[g, i], wos[g * w:(g + 1) * w, :])
        acc[at, :] = res
        xh, inv = normalise(res)
        xhs[at, :] = xh
        invs[at, :] = jnp.broadcast_to(inv, (rows, 128))
        n2s[at, :] = (xh * gain_ref[...]).astype(BF)
        dn[at, :] = jnp.zeros((rows, d), F32)
        return carry

    lax.fori_loop(0, docs, second_norm, 0)
    loads[-1].wait()
    cot_load(cot_hbm).wait()
    gather.mine().wait()
    pair = p.b // 2 % 2

    def weights(f):
        base = flip(p.line, f // 2) * 4 + (pair + f) % 2 * 2
        up = ups[:, :, pl.ds(pl.multiple_of(base * held, chunk), chunk)].reshape(d, chunk)
        return up, downs[pl.ds(base, 2)].reshape(chunk, d)

    def hidden(t):
        up, down = weights(t // docs)
        us[t % 2] = dot(n2s[rows_of(t % docs), :], up)
        gs[t % 2] = dot(cots[t % docs], down, NT)

    def one_tile(t, carry):
        f, i = t // docs, t % docs

        @pl.when(t + 1 < nb // 2 * docs)
        def _():
            after = (t + 1) // docs
            pl.when(i == docs - 1)(lambda: gather.from_core(flip(p.line, after // 2), after % 2))

            @pl.when((i == docs - 1) & (f % 2 == 0))
            def _():
                pl.when(f // 2 + 1 < p.lines)(lambda: gather.hop(f // 2 + 1, pairs=False))
                pl.when(f // 2 + 1 < p.lines)(lambda: gather.pair_line(flip(p.line, f // 2 + 1)))

            pl.when((i == min(1, docs - 1)) & (f % 2 == 0))(lambda: gather.relay_line(flip(p.line, f // 2)))

        hidden(jnp.minimum(t + 1, nb // 2 * docs - 1))
        up, down = weights(f)
        act, slope = gelu_parts(us[t % 2])
        pg = (slope * gs[t % 2]).astype(BF)
        at = rows_of(i)
        acc[at, :] += dot(act.astype(BF), down)
        dn[at, :] += dot(pg, up, NT)
        return carry

    gather.from_core(p.line, 0)
    hidden(0)
    lax.fori_loop(0, nb // 2 * docs, one_tile, 0)

    def out_and_grad(i, carry):
        at = rows_of(i)
        xs[i] = acc[at, :].astype(BF)
        rg = cots[i].astype(F32) + norm_back(xhs[at, :], invs[at, :1], gain_ref[...], dn[at, :])
        xhs[at, :] = rg
        mix = dot(rg.astype(BF), wos[...], NT).astype(BF)
        for g in range(ns):
            atts[g, i] = mix[:, g * w:(g + 1) * w]
        for copy in results(i):
            copy.start()
        return carry

    def results(i):
        out = [pltpu.make_async_copy(atts.at[p.part, i], mix_hbm.at[p.part, i], store.at[2, i]),
               pltpu.make_async_copy(xs.at[i], out_hbm.at[i], store.at[0, i]),
               pltpu.make_async_copy(xhs.at[rows_of(i)], rg_hbm.at[i], store.at[1, i])]
        for r in range(1, ns):
            out.append(pltpu.make_async_remote_copy(
                src_ref=atts.at[flip(p.part, r), i], dst_ref=mix_hbm.at[p.part, i], send_sem=msend.at[i, r],
                recv_sem=mrecv.at[i, r], device_id=p.peer(r), device_id_type=MESH))
        return out

    lax.fori_loop(0, docs, out_and_grad, 0)
    for i in range(docs):
        for copy in results(i):
            copy.wait()
    gather.drain()


def middle(nb, ns, x, att, kept, cot, gain, wo, up, down):
    docs, rows, d = x.shape
    w = d // ns
    n = docs * rows
    any_spec = pl.BlockSpec(memory_space=pl.ANY)
    vmem = pl.BlockSpec(memory_space=pltpu.VMEM)
    dma = pltpu.SemaphoreType.DMA
    return pl.pallas_call(
        functools.partial(middle_kernel, nb, ns),
        in_specs=[any_spec] * 4 + [vmem] + [any_spec] * 3,
        out_specs=[any_spec] * 3,
        out_shape=[jax.ShapeDtypeStruct((docs, rows, d), BF), jax.ShapeDtypeStruct((docs, rows, d), F32),
                   jax.ShapeDtypeStruct((ns, docs, rows, w), BF)],
        scratch_shapes=[pltpu.VMEM((docs, rows, d), BF), pltpu.VMEM((ns, docs, rows, w), BF),
                        pltpu.VMEM((docs, rows, d), BF), pltpu.VMEM(wo.shape, BF), pltpu.VMEM((nb,) + down.shape, BF),
                        pltpu.VMEM(up.shape, BF), pltpu.VMEM((n, d), F32),
                        pltpu.VMEM((n, d), F32), pltpu.VMEM((n, d), F32), pltpu.VMEM((n, d), BF),
                        pltpu.VMEM((n, 128), F32), pltpu.VMEM((2, rows, 2 * down.shape[0]), F32),
                        pltpu.VMEM((2, rows, 2 * down.shape[0]), F32),
                        dma((4, nb)), dma((nb,)), dma((docs, ns)), dma((docs, ns)),
                        dma((docs, ns)), dma((docs, ns)), dma((3 + docs,)), dma((3, docs))],
        compiler_params=pltpu.CompilerParams(collective_id=2, has_side_effects=True, vmem_limit_bytes=63 << 20),
        name="feed_forward",
    )(x, att, kept, cot, gain, wo, up, down)


def sum_over_devices(p, mine, first, second, total, sends, recvs):
    b, s, nb, ns = p.b, p.s, p.nb, p.ns
    slot, block = b % 16, b - b % 16
    many = nb // 16 * ns
    at = (b // 16) * ns + s

    def scatter(j):
        return pltpu.make_async_remote_copy(
            src_ref=mine.at[flip(slot, j)], dst_ref=first.at[slot], send_sem=sends.at[0, j], recv_sem=recvs.at[0, j],
            device_id=(block + flip(slot, j), s), device_id_type=MESH)

    def share(j):
        to = flip(at, j)
        return pltpu.make_async_remote_copy(
            src_ref=second.at[at], dst_ref=second.at[at], send_sem=sends.at[1, j], recv_sem=recvs.at[1, j],
            device_id=((to // ns) * 16 + slot, to % ns), device_id_type=MESH)

    def spread(j):
        return pltpu.make_async_remote_copy(
            src_ref=total.at[slot], dst_ref=total.at[slot], send_sem=sends.at[2, j], recv_sem=recvs.at[2, j],
            device_id=(block + flip(slot, j), s), device_id_type=MESH)

    for j in range(1, 16):
        scatter(j).start()
    first[slot] = mine[slot]
    for j in range(1, 16):
        scatter(j).wait()
    second[at] = jnp.sum(first[...], axis=0)
    for j in range(1, many):
        share(j).start()
    for j in range(1, many):
        share(j).wait()
    total[slot] = jnp.sum(second[...], axis=0)
    for j in range(1, 16):
        spread(j).start()
    for j in range(1, 16):
        spread(j).wait()


def sum_ways(p):
    b, s, nb, ns = p.b, p.s, p.nb, p.ns
    slot, block = b % 16, b - b % 16
    at = (b // 16) * ns + s
    ways = [((block + flip(slot, j), s), None) for j in range(1, 16)]
    for j in range(1, nb // 16 * ns):
        to = flip(at, j)
        ways.append((((to // ns) * 16 + slot, to % ns), None))
    return ways


CUTS = 2


def backward_kernel(nb, ns, rank, size, tile, layout, q_ref, k_ref, v_ref, o_ref, g_ref, lse_ref, top_hbm, x_hbm, gain_ref,
                    rg_hbm, low_hbm, wq_hbm, wk_hbm, wv_hbm, down_ref, upq_ref, upv_ref, top_out, out_hbm, sum_ref,
                    dqt, stage, xs, rgs, ds, wqs, wks, wvs, lows, outs, gds, gqs, gvs, mine, first, second, summed,
                    load, dsend, drecv, osend, orecv, tsend, trecv, ssend, srecv):
    docs, rows, d = x_hbm.shape
    w = d // ns
    p = Place(nb, ns)
    doc, pair = pl.program_id(0), pl.program_id(1)
    pairs = w // 128
    loads = [pltpu.make_async_copy(a, v, load.at[n]) for n, (a, v) in enumerate(
        ((wq_hbm, wqs), (wk_hbm, wks), (wv_hbm, wvs), (low_hbm, lows), (x_hbm, xs), (rg_hbm, rgs)))]

    def away(t, i, r):
        return pltpu.make_async_remote_copy(
            src_ref=stage.at[i, t, flip(p.part, r)], dst_ref=ds.at[t, p.part, i], send_sem=dsend.at[t, i, r],
            recv_sem=drecv.at[t, i, r], device_id=p.peer(r), device_id_type=MESH)

    cut = rows // CUTS

    def out_away(i, n):
        at = pl.ds(pl.multiple_of(n * cut, cut), cut)
        return pltpu.make_async_remote_copy(
            src_ref=outs.at[i, at], dst_ref=out_hbm.at[i, at], send_sem=osend.at[i, n], recv_sem=orecv.at[i, n],
            device_id=p.partner, device_id_type=MESH)

    def out_home(i, n):
        at = pl.ds(pl.multiple_of(n * cut, cut), cut)
        return pltpu.make_async_copy(outs.at[i, at], out_hbm.at[i, at], orecv.at[i, n])

    def top_away(i):
        return pltpu.make_async_remote_copy(
            src_ref=top_hbm.at[i], dst_ref=top_out.at[i], send_sem=tsend.at[i], recv_sem=trecv.at[i],
            device_id=p.partner, device_id_type=MESH)

    @pl.when((doc == 0) & (pair == 0))
    def _():
        for copy in loads:
            copy.start()
        p.greet([(p.peer(r), None) for r in range(1, ns)] + [(p.partner, jnp.logical_not(p.stays))] + sum_ways(p))
        for i in range(docs):
            pl.when(jnp.logical_not(p.stays))(lambda i=i: top_away(i).start())
        gds[...] = jnp.zeros_like(gds)
        gqs[...] = jnp.zeros_like(gqs)
        gvs[...] = jnp.zeros_like(gvs)

    @pl.when((doc > 0) & (pair == min(1, pairs - 1)))
    def _():
        i = doc - 1

        @pl.when(i == 0)
        def _():
            for copy in loads:
                copy.wait()

        for t in range(3):
            for r in range(1, ns):
                away(t, i, r).wait()

        def some_rows(n, carry):
            at = pl.ds(pl.multiple_of(n * cut, cut), cut)
            low = lows[i, at, :]
            fg = lg = None
            for r in range(ns):
                g = flip(p.part, r)
                cols = pl.ds(pl.multiple_of(g * w, w), w)
                for t, (full, up, total) in enumerate(((wqs, upq_ref, gqs), (wks, None, None), (wvs, upv_ref, gvs))):
                    piece = ds[t, g, i, at, :] if r else stage[i, t, p.part, at, :]
                    y = dot(piece, full[:, :, cols].reshape(d, w), NT)
                    fg = y if fg is None else fg + y
                    if up is not None:
                        y = dot(piece, up[:, cols], NT)
                        lg = y if lg is None else lg + y
                        total[:, cols] += dot(low, piece, TN)
            lgb = lg.astype(BF)
            fg = fg + dot(lgb, down_ref[...], NT)
            xh, inv = normalise(xs[i, at, :].astype(F32))
            gds[...] += dot(lgb, (xh * gain_ref[...]).astype(BF), TN)
            outs[i, at, :] = (rgs[i, at, :] + norm_back(xh, inv, gain_ref[...], fg)).astype(BF)
            pl.when(p.stays)(lambda: out_home(i, n).start())
            pl.when(jnp.logical_not(p.stays))(lambda: out_away(i, n).start())
            return carry

        lax.fori_loop(0, CUTS, some_rows, 0)

    @pl.when(doc < docs)
    def _():
        attention_gradients(layout, q_ref, k_ref, v_ref, o_ref, g_ref, lse_ref, stage, dqt, doc, pair, size, tile)

        @pl.when(pair == pairs - 1)
        def _():
            for t in range(3):
                for r in range(1, ns):
                    away(t, doc, r).start()

    @pl.when((doc == docs) & (pair == pairs - 1))
    def _():
        upper = lax.broadcasted_iota(jnp.int32, (2 * rank, 1), 0) < rank
        both = jnp.where(upper, gqs[:2 * rank, :], gvs[:2 * rank, :]) * ADAPTER_SCALE
        for n in range(8):
            mine[n] = gds[:8, n * 128:(n + 1) * 128]
            mine[8 + n] = both[:, n * 128:(n + 1) * 128]
        sum_over_devices(p, mine, first, second, summed, ssend, srecv)
        sum_ref[...] = summed[...]
        for i in range(docs):
            for n in range(CUTS):
                pl.when(p.stays)(lambda i=i, n=n: out_home(i, n).wait())
                pl.when(jnp.logical_not(p.stays))(lambda i=i, n=n: out_away(i, n).wait())
            pl.when(jnp.logical_not(p.stays))(lambda i=i: top_away(i).wait())


def attention_gradients(layout, q_ref, k_ref, v_ref, o_ref, g_ref, lse_ref, stage, dqt, doc, pair, size, tile):
    parts, rows = q_ref.shape[0], q_ref.shape[2]
    n = parts * rows
    blocks, per = n // size, rows // size
    q = picked(q_ref, layout, blocks, size)
    k = picked(k_ref, layout, blocks, size)
    v = picked(v_ref, layout, blocks, size)
    o = picked(o_ref, layout, blocks, size)
    g = picked(g_ref, layout, blocks, size)
    kt = k.T
    lane = lax.broadcasted_iota(jnp.int32, (1, 128), 1)
    c = SCORE_SCALE * LOG2E
    tri = lax.broadcasted_iota(jnp.int32, (tile, tile), 0) <= lax.broadcasted_iota(jnp.int32, (tile, tile), 1)
    prod = (o.astype(F32) * g.astype(F32)).astype(BF)
    heads = (lax.broadcasted_iota(jnp.int32, (8, 128), 1) // 64 == lax.broadcasted_iota(jnp.int32, (8, 128), 0)).astype(BF)
    delta = dot(heads, prod, NT)
    zero = jnp.zeros((), BF)
    masks = [(lane < 64) == (h == 0) for h in range(2)]
    qms = [jnp.where(mk, q, zero) for mk in masks]
    gms = [jnp.where(mk, g, zero) for mk in masks]
    lse = lse_ref[0, 0]
    dks, dvs = [], []
    work = [(j, h) for j in range(n // tile) for h in range(2)]

    def products(j, h):
        lo, hi = j * tile, (j + 1) * tile
        return dot(k[lo:hi], qms[h][lo:], NT), dot(v[lo:hi], gms[h][lo:], NT)

    ahead = products(*work[0])
    for t, (j, h) in enumerate(work):
        st, dp = ahead
        if t + 1 < len(work):
            ahead = products(*work[t + 1])
        lo, hi = j * tile, (j + 1) * tile
        p = jnp.exp2(st * c - lse[h:h + 1, lo:])
        diag = jnp.where(tri, p[:, :tile], 0.0)
        p = diag if hi == n else jnp.concatenate([diag, p[:, tile:]], axis=1)
        ds = (p * (dp - delta[h:h + 1, lo:])).astype(BF)
        dvh = dot(p.astype(BF), gms[h][lo:])
        dkh = dot(ds, qms[h][lo:])
        dv = dvh if h == 0 else dv + dvh
        dk = dkh if h == 0 else dk + dkh
        dqh = dot(kt[64 * h:64 * h + 64, lo:hi], ds)
        if j == 0:
            dqt[64 * h:64 * h + 64, :] = dqh
        else:
            dqt[64 * h:64 * h + 64, lo:] += dqh
        if h == 1:
            dks.append((dk * SCORE_SCALE).astype(BF))
            dvs.append(dv.astype(BF))
    lanes = pl.ds(pl.multiple_of(pair * 128, 128), 128)
    for t, value in enumerate(((dqt[...] * SCORE_SCALE).T.astype(BF), jnp.concatenate(dks, axis=0),
                               jnp.concatenate(dvs, axis=0))):
        def store(b, piece, t=t):
            stage[doc, t, b // per, b % per * size:(b % per + 1) * size, lanes] = piece
        put_back(value, layout, blocks, size, store)


def backward(nb, ns, rank, layout, q, k, v, o, g, lse, top, x, gain, rg, low, wq, wk, wv, down, upq, upv, size, tile=256):
    docs, rows, d = x.shape
    parts = q.shape[0]
    w = d // ns
    n = parts * rows
    any_spec = pl.BlockSpec(memory_space=pl.ANY)
    vmem = pl.BlockSpec(memory_space=pltpu.VMEM)
    dma = pltpu.SemaphoreType.DMA
    many = max(16, nb // 16 * ns)
    spec = pl.BlockSpec((parts, 1, rows, 128), lambda i, j: (0, jnp.minimum(i, docs - 1), 0, j))
    row = jax.ShapeDtypeStruct(x.shape, BF)
    return pl.pallas_call(
        functools.partial(backward_kernel, nb, ns, rank, size, tile),
        grid=(docs + 1, w // 128),
        in_specs=[pl.BlockSpec(memory_space=pltpu.SMEM)] + [spec] * 5
        + [pl.BlockSpec((1, 1, 2, n), lambda i, j: (jnp.minimum(i, docs - 1), j, 0, 0))]
        + [any_spec] * 2 + [vmem] + [any_spec] * 5 + [vmem] * 3,
        out_specs=[any_spec, any_spec, vmem],
        out_shape=[row, row, jax.ShapeDtypeStruct((16, 8, 128), F32)],
        scratch_shapes=[pltpu.VMEM((128, n), F32), pltpu.VMEM((docs, 3, parts, rows, w), BF),
                        pltpu.VMEM(x.shape, BF), pltpu.VMEM(x.shape, F32), pltpu.VMEM((3, ns, docs, rows, w), BF)]
        + [pltpu.VMEM(wq.shape, BF)] * 3
        + [pltpu.VMEM(low.shape, BF), pltpu.VMEM(x.shape, BF)] + [pltpu.VMEM((128, d), F32)] * 3
        + [pltpu.VMEM((16, 8, 128), F32), pltpu.VMEM((16, 8, 128), F32), pltpu.VMEM((nb // 16 * ns, 8, 128), F32),
           pltpu.VMEM((16, 8, 128), F32),
           dma((6,)), dma((3, docs, ns)), dma((3, docs, ns)), dma((docs, CUTS)), dma((docs, CUTS)), dma((docs,)), dma((docs,)),
           dma((3, many)), dma((3, many))],
        compiler_params=pltpu.CompilerParams(collective_id=3, has_side_effects=True, vmem_limit_bytes=62 << 20),
        name="backward",
    )(layout, q, k, v, o, g, lse, top, x, gain, rg, low, wq, wk, wv, down, upq, upv)


def local(
    nb, ns,
    tokens, cotangent, layout, attention_norm_gain, feedforward_norm_gain,
    query_weight, key_weight, value_weight, attention_output_weight, up_weight, down_weight,
    query_down_adapter, query_up_adapter, value_down_adapter, value_up_adapter,
):
    docs, rows, d = tokens.shape
    size = rows * ns // layout.shape[0]
    rank = query_up_adapter.shape[0]
    down = jnp.pad(jnp.concatenate([query_down_adapter, value_down_adapter], axis=1), ((0, 0), (0, 128 - 2 * rank)))
    upq = jnp.pad((ADAPTER_SCALE * query_up_adapter).astype(BF), ((0, 128 - rank), (0, 0)))
    upv = jnp.pad((ADAPTER_SCALE * value_up_adapter).astype(BF), ((rank, 128 - 2 * rank), (0, 0)))
    gain1 = attention_norm_gain[None]
    gain2 = feedforward_norm_gain[None]

    q, k, v, low, x, wq, wk, wv, wo = project(
        nb, ns, tokens, query_weight, key_weight, value_weight, attention_output_weight, gain1, down,
        jnp.stack([upq, jnp.zeros_like(upq), upv]))
    att, lse, cot, w_up = attention_forward(nb, ns, layout, q, k, v, cotangent, up_weight, size)
    out, rg, mix = middle(nb, ns, x, att, cotangent, cot, gain2, wo.reshape(d, d), w_up, down_weight)
    stays = lax.axis_index("batch") % 2 == lax.axis_index("seq") % 2
    got, input_grad, sums = backward(
        nb, ns, rank, layout, q, k, v, att, mix, lse, out, x, gain1, rg, low, wq, wk, wv, down, upq, upv, size)
    layer_out = jnp.where(stays, out, got)
    sums = sums.reshape(2, d // 128, 2 * rank, 128).transpose(0, 2, 1, 3).reshape(2, 2 * rank, d)
    return (layer_out, input_grad, sums[0, :rank].T, sums[1, :rank], sums[0, rank:].T, sums[1, rank:])


def solution(mesh):
    spec = P("batch", "seq", None)
    weight = P("batch", None)
    return jax.shard_map(
        functools.partial(local, mesh.shape["batch"], mesh.shape["seq"]),
        mesh=mesh,
        in_specs=(spec, spec, P(), P(), P()) + (weight,) * 6 + (P(),) * 4,
        out_specs=(spec, spec, P(), P(), P(), P()),
        check_vma=False,
    )
```

```python
import functools
import math

import jax
import jax.numpy as jnp
from jax import lax
from jax.experimental import pallas as pl
from jax.experimental.pallas import tpu as pltpu
from jax.sharding import PartitionSpec as P


EPSILON = 1e-05
ADAPTER_SCALE = 8.0
SCORE_SCALE = 0.125
NEG_FILL = -1e30
GELU_C = 0.7978845608028654
LOG2E = math.log2(math.e)
F32 = jnp.float32
BF = jnp.bfloat16
NN = (((1,), (0,)), ((), ()))
NT = (((1,), (1,)), ((), ()))
TN = (((0,), (0,)), ((), ()))


def dot(a, b, dims=NN):
    return lax.dot_general(a, b, dims, preferred_element_type=F32)


def normalise(x):
    mean = jnp.mean(x, axis=-1, keepdims=True)
    centred = x - mean
    inv = lax.rsqrt(jnp.mean(centred * centred, axis=-1, keepdims=True) + EPSILON)
    return centred * inv, inv


def norm_back(xh, inv, gain, up):
    t = up * gain
    return inv * (t - jnp.mean(t, axis=-1, keepdims=True) - xh * jnp.mean(t * xh, axis=-1, keepdims=True))


def gelu_parts(u):
    cubic = 0.044715 * u * u
    th = jnp.tanh(GELU_C * (u + cubic * u))
    half = 0.5 * (1.0 + th)
    return half * u, half + (0.5 * GELU_C) * u * (1.0 - th * th) * (1.0 + 3.0 * cubic)


MESH = pl.DeviceIdType.MESH


def flip(i, bits, width=5):
    out = 0
    for n in range(width):
        bit = 1 << n
        out = out + ((i // bit) % 2 + (bits // bit) % 2) % 2 * bit
    return out


def trade(b, s):
    return b - b % 2 + s % 2, s - s % 2 + b % 2


class Place:
    def __init__(self, nb, ns):
        self.nb, self.ns = nb, ns
        self.b, self.s = lax.axis_index("batch"), lax.axis_index("seq")
        self.lines = nb // 4
        self.line = self.b // 4
        self.partner = trade(self.b, self.s)
        self.stays = self.b % 2 == self.s % 2
        self.doc, self.part = trade(self.b, self.s)

    def peer(self, r):
        return trade(self.doc, flip(self.part, r))

    def greet(self, ways):
        bar = pltpu.get_barrier_semaphore()
        for device, cond in ways:
            def hello(device=device):
                pl.semaphore_signal(bar, inc=1, device_id=device, device_id_type=MESH)
            hello() if cond is None else pl.when(cond)(hello)
        count = 0
        for _, cond in ways:
            count = count + (1 if cond is None else jnp.where(cond, 1, 0))
        pl.semaphore_wait(bar, count)

    def gather_ways(self):
        b, s = self.b, self.s
        return [((b + 4, s), self.line + 1 < self.lines), ((b - 4, s), self.line > 0),
                ((flip(b, 2), s), None), ((flip(b, 1), s), None)]


class Gather:
    def __init__(self, place, own, full, send, recv):
        self.p, self.own, self.full, self.send, self.recv = place, own, full, send, recv

    def part(self, line, pair=0, core=0):
        b = self.p.b
        return line * 4 + (b // 2 + pair) % 2 * 2 + (b + core) % 2

    def copy(self, i, way, src=None):
        p = self.p
        to = [p.b + 4, p.b - 4, self.part(p.line, 1), self.part(p.line, 0, 1)][way]
        return pltpu.make_async_remote_copy(
            src_ref=self.full.at[i] if src is None else src, dst_ref=self.full.at[i],
            send_sem=self.send.at[way, i], recv_sem=self.recv.at[i],
            device_id=(to, p.s), device_id_type=MESH)

    def mine(self):
        return pltpu.make_async_copy(self.own, self.full.at[self.p.b], self.recv.at[self.p.b])

    def start(self):
        p = self.p
        pl.when(p.line + 1 < p.lines)(lambda: self.copy(p.b, 0, self.own).start())
        pl.when(p.line > 0)(lambda: self.copy(p.b, 1, self.own).start())
        self.copy(p.b, 2, self.own).start()
        self.copy(p.b, 3, self.own).start()
        self.mine().start()

    def hop(self, k, pairs=True):
        p = self.p

        def take(way, line):
            i = self.part(line)
            self.copy(i, way).wait_recv()
            more = p.line + 1 < p.lines if way == 0 else p.line > 0
            pl.when(more)(lambda: self.copy(i, way).start())
            if pairs:
                self.copy(i, 2).start()
            self.copy(i, 3).start()

        below, above = p.line - k, p.line + k
        pl.when(below >= 0)(lambda: take(0, below))
        pl.when(above < p.lines)(lambda: take(1, above))

    def pair_line(self, line):
        self.copy(self.part(line), 2).start()

    def relay_line(self, line):
        i = self.part(line, 1)
        self.copy(i, 2).wait_recv()
        self.copy(i, 3).start()

    def relay(self, k):
        p = self.p
        if k == 0:
            self.relay_line(p.line)
        else:
            pl.when(p.line >= k)(lambda: self.relay_line(p.line - k))
            pl.when(p.line + k < p.lines)(lambda: self.relay_line(p.line + k))

    def from_core(self, line, pair):
        self.copy(self.part(line, pair, 1), 3).wait_recv()

    def finish(self):
        self.mine().wait()
        for line in range(self.p.lines):
            for pair in range(2):
                self.from_core(line, pair)

    def drain(self):
        p = self.p
        for line in range(p.lines):
            i = self.part(line)
            pl.when((p.line >= line) & (p.line + 1 < p.lines))(lambda i=i: self.copy(i, 0).wait_send())
            pl.when((p.line <= line) & (p.line > 0))(lambda i=i: self.copy(i, 1).wait_send())
            self.copy(i, 2).wait_send()
            self.copy(i, 3).wait_send()
            self.copy(self.part(line, 1), 3).wait_send()

    def steps(self):
        out = [self.start]
        for k in range(1, self.p.lines):
            out.append(functools.partial(run, [functools.partial(self.hop, k), functools.partial(self.relay, k - 1)]))
        out.append(functools.partial(self.relay, self.p.lines - 1))
        out.append(self.finish)
        return out


def run(calls):
    for call in calls:
        call()


def chosen(blocks, tests):
    out = blocks[0]
    for block, test in zip(blocks[1:], tests[1:]):
        out = jnp.where(test, block, out)
    return out


def picked(ref, layout, blocks, size):
    per = ref.shape[2] // size
    stored = [ref[t // per, 0, (t % per) * size:(t % per + 1) * size, :] for t in range(blocks)]
    return jnp.concatenate([chosen(stored, [layout[t] == p for t in range(blocks)]) for p in range(blocks)], axis=0)


def put_back(value, layout, blocks, size, store):
    pieces = [value[p * size:(p + 1) * size] for p in range(blocks)]
    for t in range(blocks):
        store(t, chosen(pieces, [layout[t] == p for p in range(blocks)]))


def attend(layout, qkv, out, lse_ref, doc, pair, size, tile):
    parts, rows = qkv.shape[1], qkv.shape[3]
    n = parts * rows
    blocks, per = n // size, rows // size
    lanes = pl.ds(pl.multiple_of(pair * 128, 128), 128)

    def in_order(t):
        stored = [qkv[t, b // per, doc, b % per * size:(b % per + 1) * size, lanes] for b in range(blocks)]
        return jnp.concatenate([chosen(stored, [layout[b] == p for b in range(blocks)]) for p in range(blocks)], axis=0)

    q, k, v = in_order(0), in_order(1), in_order(2)
    vt = v.T
    lane = lax.broadcasted_iota(jnp.int32, (1, 128), 1)
    c = SCORE_SCALE * LOG2E
    tri = lax.broadcasted_iota(jnp.int32, (tile, tile), 0) <= lax.broadcasted_iota(jnp.int32, (tile, tile), 1)
    work = [(i, h) for i in range(n // tile) for h in range(2)]
    lses = [[], []]
    mixed = {}

    def scores(i, h):
        qm = jnp.where((lane < 64) == (h == 0), q[i * tile:(i + 1) * tile], jnp.zeros((), BF))
        return dot(k[:(i + 1) * tile], qm, NT)

    ahead = scores(*work[0])
    for t, (i, h) in enumerate(work):
        st = ahead
        if t + 1 < len(work):
            ahead = scores(*work[t + 1])
        kk = (i + 1) * tile
        diag = jnp.where(tri, st[i * tile:], NEG_FILL)
        st = diag if i == 0 else jnp.concatenate([st[: i * tile], diag], axis=0)
        m = jnp.max(st, axis=0, keepdims=True) * c
        e = jnp.exp2(st * c - m)
        l = jnp.sum(e, axis=0, keepdims=True)
        o = dot(vt[64 * h:64 * h + 64, :kk], e.astype(BF))
        mixed[i, h] = o * (1.0 / l)
        lses[h].append(m + jnp.log2(l))
    outs = [jnp.concatenate([mixed[i, 0], mixed[i, 1]], axis=0).T.astype(BF) for i in range(n // tile)]

    def store(b, piece):
        out[b // per, doc, b % per * size:(b % per + 1) * size, lanes] = piece

    put_back(jnp.concatenate(outs, axis=0), layout, blocks, size, store)
    for h in range(2):
        lse_ref[doc, pair, h:h + 1, :] = jnp.concatenate(lses[h], axis=1)


PACE = 4


def front_kernel(nb, ns, size, tile, layout, x_hbm, cot_hbm, wq_ref, wk_ref, wv_ref, wo_ref, up_hbm, gain_ref, down_ref, ups_ref,
                 qkv_out, att_out, mixed_out, lse_ref, low_out, x_out, cot_out, wq_out, wk_out, wv_out, wo_out, up_out,
                 xs, n1s, stage, qkv, att, lows, ws, own, send, recv, usend, urecv, xsend, xrecv, csend, crecv,
                 osend, orecv, asend, arecv, local_sem, qkv_sem, att_sem):
    docs, rows, d = x_hbm.shape
    w = d // ns
    pairs = w // 128
    p = Place(nb, ns)
    fetch = pltpu.make_async_copy(up_hbm, own, local_sem.at[docs + 5])
    fetch.start()
    p.greet(p.gather_ways() + [(p.partner, jnp.logical_not(p.stays))] + [(p.peer(r), None) for r in range(1, ns)])

    def x_remote(i):
        return pltpu.make_async_remote_copy(
            src_ref=x_hbm.at[i], dst_ref=xs.at[i], send_sem=xsend.at[i], recv_sem=xrecv.at[i],
            device_id=p.partner, device_id_type=MESH)

    def cot_remote(i):
        return pltpu.make_async_remote_copy(
            src_ref=cot_hbm.at[i], dst_ref=cot_out.at[i], send_sem=csend.at[i], recv_sem=crecv.at[i],
            device_id=p.partner, device_id_type=MESH)

    def x_local(i):
        return pltpu.make_async_copy(x_hbm.at[i], xs.at[i], xrecv.at[i])

    def x_keep(i):
        return pltpu.make_async_copy(xs.at[i], x_out.at[i], local_sem.at[i])

    for i in range(docs):
        pl.when(p.stays)(lambda i=i: x_local(i).start())
        pl.when(jnp.logical_not(p.stays))(lambda i=i: x_remote(i).start())
    for i in range(docs):
        pl.when(jnp.logical_not(p.stays))(lambda i=i: cot_remote(i).start())

    def first(i):
        pl.when(p.stays)(lambda: x_local(i).wait())
        pl.when(jnp.logical_not(p.stays))(lambda: x_remote(i).wait())
        x_keep(i).start()
        xh, _ = normalise(xs[i].astype(F32))
        n1 = (xh * gain_ref[...]).astype(BF)
        n1s[i] = n1
        lows[i] = dot(n1, down_ref[...]).astype(BF)

    def away(part, i, r):
        return pltpu.make_async_remote_copy(
            src_ref=stage.at[part, i, flip(p.part, r)], dst_ref=qkv.at[part, p.part, i],
            send_sem=osend.at[part, i, r], recv_sem=orecv.at[part, i, r],
            device_id=p.peer(r), device_id_type=MESH)

    def product(part, i):
        y = dot(n1s[i], ws[part].reshape(d, d)) + dot(lows[i], ups_ref[part])
        y = y.astype(BF)
        for g in range(ns):
            piece = y[:, g * w:(g + 1) * w]

            @pl.when(p.part == g)
            def _():
                qkv[part, p.part, i] = piece

            @pl.when(p.part != g)
            def _():
                stage[part, i, g] = piece
        for r in range(1, ns):
            away(part, i, r).start()

    gathers = [Gather(p, own_ref, ws.at[n], send.at[n], recv.at[n])
               for n, own_ref in enumerate((wq_ref, wk_ref, wv_ref, wo_ref))]
    keeps = [pltpu.make_async_copy(ws.at[n], out, local_sem.at[docs + n])
             for n, out in enumerate((wq_out, wk_out, wv_out, wo_out))]
    low_keep = pltpu.make_async_copy(lows, low_out, local_sem.at[docs + 4])
    up_steps = Gather(p, own, up_out, usend, urecv).steps()

    lists = [g.steps() for g in gathers]
    delays = (0, 0, 2, 4)
    ready = [len(lists[0]) - 1 + delay for delay in delays]

    def slot(t):
        for n, steps in enumerate(lists):
            if 0 <= t - delays[n] < len(steps):
                steps[t - delays[n]]()
            if t == ready[n]:
                keeps[n].start()
        if t == ready[0] + 1:
            fetch.wait()
            up_steps[0]()

    for t in range(ready[0] + 1):
        slot(t)
    places = {2 * docs - 5 + 2 * n: t for n, t in enumerate(range(ready[0] + 1, ready[3] + 1))}

    def one_product(n, carry):
        early = n < 2 * docs
        part = jnp.where(early, n % 2, 2)
        i = jnp.where(early, n // 2, n - 2 * docs)
        pl.when(early & (part == 0))(lambda: first(i))
        product(part, i)
        for at, t in places.items():
            pl.when(n == at)(functools.partial(slot, t))
        return carry

    lax.fori_loop(0, 3 * docs, one_product, 0)
    low_keep.start()

    def qkv_keep(i):
        return pltpu.make_async_copy(qkv.at[:, :, i], qkv_out.at[:, :, i], qkv_sem.at[i])

    def att_keep(i):
        return pltpu.make_async_copy(att.at[:, i], att_out.at[:, i], att_sem.at[i, 0])

    def att_home(i):
        return pltpu.make_async_copy(att.at[p.part, i], mixed_out.at[p.part, i], att_sem.at[i, 1])

    def att_away(i, r):
        return pltpu.make_async_remote_copy(
            src_ref=att.at[flip(p.part, r), i], dst_ref=mixed_out.at[p.part, i], send_sem=asend.at[i, r],
            recv_sem=arecv.at[i, r], device_id=p.peer(r), device_id_type=MESH)

    def one_pair(m, carry):
        doc, pair = m // pairs, m % pairs
        for n in range(1, len(up_steps)):
            if PACE * (n - 1) < docs * pairs:
                pl.when(m == PACE * (n - 1))(up_steps[n])

        @pl.when(pair == 0)
        def _():
            for part in range(3):
                for r in range(1, ns):
                    away(part, doc, r).wait()
            qkv_keep(doc).start()

        attend(layout, qkv, att, lse_ref, doc, pair, size, tile)

        @pl.when(pair == pairs - 1)
        def _():
            att_keep(doc).start()
            att_home(doc).start()
            for r in range(1, ns):
                att_away(doc, r).start()

        return carry

    lax.fori_loop(0, docs * pairs, one_pair, 0)
    for n in range(1, len(up_steps)):
        if PACE * (n - 1) >= docs * pairs:
            up_steps[n]()
    for i in range(docs):
        x_keep(i).wait()
        pl.when(jnp.logical_not(p.stays))(lambda i=i: cot_remote(i).wait())
        qkv_keep(i).wait()
        att_keep(i).wait()
        att_home(i).wait()
        for r in range(1, ns):
            att_away(i, r).wait()
    for keep in keeps:
        keep.wait()
    low_keep.wait()
    for g in gathers + [Gather(p, own, up_out, usend, urecv)]:
        g.drain()


def front(nb, ns, layout, x, cot, wq, wk, wv, wo, up, gain, down, ups, size, tile=256):
    docs, rows, d = x.shape
    w = d // ns
    n = rows * ns
    any_spec = pl.BlockSpec(memory_space=pl.ANY)
    vmem = pl.BlockSpec(memory_space=pltpu.VMEM)
    dma = pltpu.SemaphoreType.DMA
    like = lambda *shape: jax.ShapeDtypeStruct(shape, BF)
    heads = (ns, docs, rows, w)
    outs = [like(3, *heads), like(*heads), like(*heads), jax.ShapeDtypeStruct((docs, w // 128, 2, n), F32),
            like(docs, rows, 128), like(*x.shape), like(*x.shape)] + [like(nb, *wq.shape)] * 4 + [like(nb, *up.shape)]
    return pl.pallas_call(
        functools.partial(front_kernel, nb, ns, size, tile),
        in_specs=[pl.BlockSpec(memory_space=pltpu.SMEM)] + [any_spec] * 7 + [vmem] * 3,
        out_specs=[any_spec] * 3 + [vmem] + [any_spec] * 8,
        out_shape=outs,
        scratch_shapes=[pltpu.VMEM(x.shape, BF), pltpu.VMEM(x.shape, BF), pltpu.VMEM((3, docs, ns, rows, w), BF),
                        pltpu.VMEM((3,) + heads, BF), pltpu.VMEM(heads, BF), pltpu.VMEM((docs, rows, 128), BF),
                        pltpu.VMEM((4, nb) + wq.shape, BF), pltpu.VMEM(up.shape, BF),
                        dma((4, 4, nb)), dma((4, nb)), dma((4, nb)), dma((nb,)), dma((docs,)), dma((docs,)),
                        dma((docs,)), dma((docs,)), dma((3, docs, ns)), dma((3, docs, ns)), dma((docs, ns)), dma((docs, ns)),
                        dma((docs + 6,)), dma((docs,)), dma((docs, 2))],
        compiler_params=pltpu.CompilerParams(collective_id=0, has_side_effects=True, vmem_limit_bytes=62 << 20),
        name="front",
    )(layout, x, cot, wq, wk, wv, wo, up, gain, down, ups)


def middle_kernel(nb, ns, x_hbm, att_hbm, kept_hbm, cot_hbm, gain_ref, wo_hbm, up_hbm, down_hbm,
                  out_hbm, rg_hbm, mix_hbm,
                  xs, atts, cots, wos, downs, ups, acc, xhs, dn, n2s, invs, us, gs,
                  send, recv, msend, mrecv, load, store):
    docs, rows, d = x_hbm.shape
    w = d // ns
    p = Place(nb, ns)
    held = down_hbm.shape[0]
    chunk = 2 * held
    loads = [pltpu.make_async_copy(wo_hbm, wos, load.at[0]), pltpu.make_async_copy(att_hbm, atts, load.at[3 + docs])]
    for i in range(docs):
        loads.append(pltpu.make_async_copy(x_hbm.at[i], xs.at[i], load.at[1 + i]))
    loads.append(pltpu.make_async_copy(up_hbm, ups, load.at[1 + docs]))
    for copy in loads:
        copy.start()

    def cot_load(source):
        return pltpu.make_async_copy(source, cots, load.at[2 + docs])

    pl.when(p.stays)(lambda: cot_load(kept_hbm).start())
    pl.when(jnp.logical_not(p.stays))(lambda: cot_load(cot_hbm).start())
    p.greet(p.gather_ways() + [(p.peer(r), None) for r in range(1, ns)])

    gather = Gather(p, down_hbm, downs, send, recv)

    gather.start()
    for copy in loads[:-1]:
        copy.wait()
    def rows_of(i):
        return pl.ds(pl.multiple_of(i * rows, rows), rows)

    def second_norm(i, carry):
        at = rows_of(i)
        res = xs[i].astype(F32)
        for g in range(ns):
            res = res + dot(atts[g, i], wos[g * w:(g + 1) * w, :])
        acc[at, :] = res
        xh, inv = normalise(res)
        xhs[at, :] = xh
        invs[at, :] = jnp.broadcast_to(inv, (rows, 128))
        n2s[at, :] = (xh * gain_ref[...]).astype(BF)
        dn[at, :] = jnp.zeros((rows, d), F32)
        return carry

    lax.fori_loop(0, docs, second_norm, 0)
    loads[-1].wait()
    cot_load(cot_hbm).wait()
    gather.mine().wait()
    pair = p.b // 2 % 2

    def weights(f):
        base = flip(p.line, f // 2) * 4 + (pair + f) % 2 * 2
        up = ups[:, :, pl.ds(pl.multiple_of(base * held, chunk), chunk)].reshape(d, chunk)
        return up, downs[pl.ds(base, 2)].reshape(chunk, d)

    def hidden(t):
        up, down = weights(t // docs)
        us[t % 2] = dot(n2s[rows_of(t % docs), :], up)
        gs[t % 2] = dot(cots[t % docs], down, NT)

    def one_tile(t, carry):
        f, i = t // docs, t % docs

        @pl.when(t + 1 < nb // 2 * docs)
        def _():
            after = (t + 1) // docs
            pl.when(i == docs - 1)(lambda: gather.from_core(flip(p.line, after // 2), after % 2))

            @pl.when((i == docs - 1) & (f % 2 == 0))
            def _():
                pl.when(f // 2 + 1 < p.lines)(lambda: gather.hop(f // 2 + 1, pairs=False))
                pl.when(f // 2 + 1 < p.lines)(lambda: gather.pair_line(flip(p.line, f // 2 + 1)))

            pl.when((i == min(1, docs - 1)) & (f % 2 == 0))(lambda: gather.relay_line(flip(p.line, f // 2)))

        hidden(jnp.minimum(t + 1, nb // 2 * docs - 1))
        up, down = weights(f)
        act, slope = gelu_parts(us[t % 2])
        pg = (slope * gs[t % 2]).astype(BF)
        at = rows_of(i)
        acc[at, :] += dot(act.astype(BF), down)
        dn[at, :] += dot(pg, up, NT)
        return carry

    gather.from_core(p.line, 0)
    hidden(0)
    lax.fori_loop(0, nb // 2 * docs, one_tile, 0)

    def out_and_grad(i, carry):
        at = rows_of(i)
        xs[i] = acc[at, :].astype(BF)
        rg = cots[i].astype(F32) + norm_back(xhs[at, :], invs[at, :1], gain_ref[...], dn[at, :])
        xhs[at, :] = rg
        mix = dot(rg.astype(BF), wos[...], NT).astype(BF)
        for g in range(ns):
            atts[g, i] = mix[:, g * w:(g + 1) * w]
        for copy in results(i):
            copy.start()
        return carry

    def results(i):
        out = [pltpu.make_async_copy(atts.at[p.part, i], mix_hbm.at[p.part, i], store.at[2, i]),
               pltpu.make_async_copy(xs.at[i], out_hbm.at[i], store.at[0, i]),
               pltpu.make_async_copy(xhs.at[rows_of(i)], rg_hbm.at[i], store.at[1, i])]
        for r in range(1, ns):
            out.append(pltpu.make_async_remote_copy(
                src_ref=atts.at[flip(p.part, r), i], dst_ref=mix_hbm.at[p.part, i], send_sem=msend.at[i, r],
                recv_sem=mrecv.at[i, r], device_id=p.peer(r), device_id_type=MESH))
        return out

    lax.fori_loop(0, docs, out_and_grad, 0)
    for i in range(docs):
        for copy in results(i):
            copy.wait()
    gather.drain()


def middle(nb, ns, x, att, kept, cot, gain, wo, up, down):
    docs, rows, d = x.shape
    w = d // ns
    n = docs * rows
    any_spec = pl.BlockSpec(memory_space=pl.ANY)
    vmem = pl.BlockSpec(memory_space=pltpu.VMEM)
    dma = pltpu.SemaphoreType.DMA
    return pl.pallas_call(
        functools.partial(middle_kernel, nb, ns),
        in_specs=[any_spec] * 4 + [vmem] + [any_spec] * 3,
        out_specs=[any_spec] * 3,
        out_shape=[jax.ShapeDtypeStruct((docs, rows, d), BF), jax.ShapeDtypeStruct((docs, rows, d), F32),
                   jax.ShapeDtypeStruct((ns, docs, rows, w), BF)],
        scratch_shapes=[pltpu.VMEM((docs, rows, d), BF), pltpu.VMEM((ns, docs, rows, w), BF),
                        pltpu.VMEM((docs, rows, d), BF), pltpu.VMEM(wo.shape, BF), pltpu.VMEM((nb,) + down.shape, BF),
                        pltpu.VMEM(up.shape, BF), pltpu.VMEM((n, d), F32),
                        pltpu.VMEM((n, d), F32), pltpu.VMEM((n, d), F32), pltpu.VMEM((n, d), BF),
                        pltpu.VMEM((n, 128), F32), pltpu.VMEM((2, rows, 2 * down.shape[0]), F32),
                        pltpu.VMEM((2, rows, 2 * down.shape[0]), F32),
                        dma((4, nb)), dma((nb,)), dma((docs, ns)), dma((docs, ns)), dma((4 + docs,)), dma((3, docs))],
        compiler_params=pltpu.CompilerParams(collective_id=2, has_side_effects=True, vmem_limit_bytes=63 << 20),
        name="feed_forward",
    )(x, att, kept, cot, gain, wo, up, down)


def sum_over_devices(p, mine, first, second, total, sends, recvs):
    b, s, nb, ns = p.b, p.s, p.nb, p.ns
    slot, block = b % 16, b - b % 16
    many = nb // 16 * ns
    at = (b // 16) * ns + s

    def scatter(j):
        return pltpu.make_async_remote_copy(
            src_ref=mine.at[flip(slot, j)], dst_ref=first.at[slot], send_sem=sends.at[0, j], recv_sem=recvs.at[0, j],
            device_id=(block + flip(slot, j), s), device_id_type=MESH)

    def share(j):
        to = flip(at, j)
        return pltpu.make_async_remote_copy(
            src_ref=second.at[at], dst_ref=second.at[at], send_sem=sends.at[1, j], recv_sem=recvs.at[1, j],
            device_id=((to // ns) * 16 + slot, to % ns), device_id_type=MESH)

    def spread(j):
        return pltpu.make_async_remote_copy(
            src_ref=total.at[slot], dst_ref=total.at[slot], send_sem=sends.at[2, j], recv_sem=recvs.at[2, j],
            device_id=(block + flip(slot, j), s), device_id_type=MESH)

    for j in range(1, 16):
        scatter(j).start()
    first[slot] = mine[slot]
    for j in range(1, 16):
        scatter(j).wait()
    second[at] = jnp.sum(first[...], axis=0)
    for j in range(1, many):
        share(j).start()
    for j in range(1, many):
        share(j).wait()
    total[slot] = jnp.sum(second[...], axis=0)
    for j in range(1, 16):
        spread(j).start()
    for j in range(1, 16):
        spread(j).wait()


def sum_ways(p):
    b, s, nb, ns = p.b, p.s, p.nb, p.ns
    slot, block = b % 16, b - b % 16
    at = (b // 16) * ns + s
    ways = [((block + flip(slot, j), s), None) for j in range(1, 16)]
    for j in range(1, nb // 16 * ns):
        to = flip(at, j)
        ways.append((((to // ns) * 16 + slot, to % ns), None))
    return ways


CUTS = 2


def backward_kernel(nb, ns, rank, size, tile, layout, q_ref, k_ref, v_ref, o_ref, g_ref, lse_ref, top_hbm, x_hbm, gain_ref,
                    rg_hbm, low_hbm, wq_hbm, wk_hbm, wv_hbm, down_ref, upq_ref, upv_ref, top_out, out_hbm, sum_ref,
                    dqt, stage, xs, rgs, ds, wqs, wks, wvs, lows, outs, gds, gqs, gvs, mine, first, second, summed,
                    load, dsend, drecv, osend, orecv, tsend, trecv, ssend, srecv):
    docs, rows, d = x_hbm.shape
    w = d // ns
    p = Place(nb, ns)
    doc, pair = pl.program_id(0), pl.program_id(1)
    pairs = w // 128
    loads = [pltpu.make_async_copy(a, v, load.at[n]) for n, (a, v) in enumerate(
        ((wq_hbm, wqs), (wk_hbm, wks), (wv_hbm, wvs), (low_hbm, lows), (x_hbm, xs), (rg_hbm, rgs)))]

    def away(t, i, r):
        return pltpu.make_async_remote_copy(
            src_ref=stage.at[i, t, flip(p.part, r)], dst_ref=ds.at[t, p.part, i], send_sem=dsend.at[t, i, r],
            recv_sem=drecv.at[t, i, r], device_id=p.peer(r), device_id_type=MESH)

    cut = rows // CUTS

    def out_away(i, n):
        at = pl.ds(pl.multiple_of(n * cut, cut), cut)
        return pltpu.make_async_remote_copy(
            src_ref=outs.at[i, at], dst_ref=out_hbm.at[i, at], send_sem=osend.at[i, n], recv_sem=orecv.at[i, n],
            device_id=p.partner, device_id_type=MESH)

    def out_home(i, n):
        at = pl.ds(pl.multiple_of(n * cut, cut), cut)
        return pltpu.make_async_copy(outs.at[i, at], out_hbm.at[i, at], orecv.at[i, n])

    def top_away(i):
        return pltpu.make_async_remote_copy(
            src_ref=top_hbm.at[i], dst_ref=top_out.at[i], send_sem=tsend.at[i], recv_sem=trecv.at[i],
            device_id=p.partner, device_id_type=MESH)

    @pl.when((doc == 0) & (pair == 0))
    def _():
        for copy in loads:
            copy.start()
        p.greet([(p.peer(r), None) for r in range(1, ns)] + [(p.partner, jnp.logical_not(p.stays))] + sum_ways(p))
        for i in range(docs):
            pl.when(jnp.logical_not(p.stays))(lambda i=i: top_away(i).start())
        gds[...] = jnp.zeros_like(gds)
        gqs[...] = jnp.zeros_like(gqs)
        gvs[...] = jnp.zeros_like(gvs)

    @pl.when((doc > 0) & (pair == min(1, pairs - 1)))
    def _():
        i = doc - 1

        @pl.when(i == 0)
        def _():
            for copy in loads:
                copy.wait()

        for t in range(3):
            for r in range(1, ns):
                away(t, i, r).wait()

        def some_rows(n, carry):
            at = pl.ds(pl.multiple_of(n * cut, cut), cut)
            low = lows[i, at, :]
            fg = lg = None
            for r in range(ns):
                g = flip(p.part, r)
                cols = pl.ds(pl.multiple_of(g * w, w), w)
                for t, (full, up, total) in enumerate(((wqs, upq_ref, gqs), (wks, None, None), (wvs, upv_ref, gvs))):
                    piece = ds[t, g, i, at, :] if r else stage[i, t, p.part, at, :]
                    y = dot(piece, full[:, :, cols].reshape(d, w), NT)
                    fg = y if fg is None else fg + y
                    if up is not None:
                        y = dot(piece, up[:, cols], NT)
                        lg = y if lg is None else lg + y
                        total[:, cols] += dot(low, piece, TN)
            lgb = lg.astype(BF)
            fg = fg + dot(lgb, down_ref[...], NT)
            xh, inv = normalise(xs[i, at, :].astype(F32))
            gds[...] += dot(lgb, (xh * gain_ref[...]).astype(BF), TN)
            outs[i, at, :] = (rgs[i, at, :] + norm_back(xh, inv, gain_ref[...], fg)).astype(BF)
            pl.when(p.stays)(lambda: out_home(i, n).start())
            pl.when(jnp.logical_not(p.stays))(lambda: out_away(i, n).start())
            return carry

        lax.fori_loop(0, CUTS, some_rows, 0)

    @pl.when(doc < docs)
    def _():
        attention_gradients(layout, q_ref, k_ref, v_ref, o_ref, g_ref, lse_ref, stage, dqt, doc, pair, size, tile)

        @pl.when(pair == pairs - 1)
        def _():
            for t in range(3):
                for r in range(1, ns):
                    away(t, doc, r).start()

    @pl.when((doc == docs) & (pair == pairs - 1))
    def _():
        upper = lax.broadcasted_iota(jnp.int32, (2 * rank, 1), 0) < rank
        both = jnp.where(upper, gqs[:2 * rank, :], gvs[:2 * rank, :]) * ADAPTER_SCALE
        for n in range(8):
            mine[n] = gds[:8, n * 128:(n + 1) * 128]
            mine[8 + n] = both[:, n * 128:(n + 1) * 128]
        sum_over_devices(p, mine, first, second, summed, ssend, srecv)
        sum_ref[...] = summed[...]
        for i in range(docs):
            for n in range(CUTS):
                pl.when(p.stays)(lambda i=i, n=n: out_home(i, n).wait())
                pl.when(jnp.logical_not(p.stays))(lambda i=i, n=n: out_away(i, n).wait())
            pl.when(jnp.logical_not(p.stays))(lambda i=i: top_away(i).wait())


def attention_gradients(layout, q_ref, k_ref, v_ref, o_ref, g_ref, lse_ref, stage, dqt, doc, pair, size, tile):
    parts, rows = o_ref.shape[0], o_ref.shape[2]
    n = parts * rows
    blocks, per = n // size, rows // size
    q = picked(q_ref.at[0], layout, blocks, size)
    k = picked(k_ref.at[0], layout, blocks, size)
    v = picked(v_ref.at[0], layout, blocks, size)
    o = picked(o_ref, layout, blocks, size)
    g = picked(g_ref, layout, blocks, size)
    kt = k.T
    lane = lax.broadcasted_iota(jnp.int32, (1, 128), 1)
    c = SCORE_SCALE * LOG2E
    tri = lax.broadcasted_iota(jnp.int32, (tile, tile), 0) <= lax.broadcasted_iota(jnp.int32, (tile, tile), 1)
    prod = (o.astype(F32) * g.astype(F32)).astype(BF)
    heads = (lax.broadcasted_iota(jnp.int32, (8, 128), 1) // 64 == lax.broadcasted_iota(jnp.int32, (8, 128), 0)).astype(BF)
    delta = dot(heads, prod, NT)
    zero = jnp.zeros((), BF)
    masks = [(lane < 64) == (h == 0) for h in range(2)]
    qms = [jnp.where(mk, q, zero) for mk in masks]
    gms = [jnp.where(mk, g, zero) for mk in masks]
    lse = lse_ref[0, 0]
    dks, dvs = [], []
    work = [(j, h) for j in range(n // tile) for h in range(2)]

    def products(j, h):
        lo, hi = j * tile, (j + 1) * tile
        return dot(k[lo:hi], qms[h][lo:], NT), dot(v[lo:hi], gms[h][lo:], NT)

    ahead = products(*work[0])
    for t, (j, h) in enumerate(work):
        st, dp = ahead
        if t + 1 < len(work):
            ahead = products(*work[t + 1])
        lo, hi = j * tile, (j + 1) * tile
        p = jnp.exp2(st * c - lse[h:h + 1, lo:])
        diag = jnp.where(tri, p[:, :tile], 0.0)
        p = diag if hi == n else jnp.concatenate([diag, p[:, tile:]], axis=1)
        ds = (p * (dp - delta[h:h + 1, lo:])).astype(BF)
        dvh = dot(p.astype(BF), gms[h][lo:])
        dkh = dot(ds, qms[h][lo:])
        dv = dvh if h == 0 else dv + dvh
        dk = dkh if h == 0 else dk + dkh
        dqh = dot(kt[64 * h:64 * h + 64, lo:hi], ds)
        if j == 0:
            dqt[64 * h:64 * h + 64, :] = dqh
        else:
            dqt[64 * h:64 * h + 64, lo:] += dqh
        if h == 1:
            dks.append((dk * SCORE_SCALE).astype(BF))
            dvs.append(dv.astype(BF))
    lanes = pl.ds(pl.multiple_of(pair * 128, 128), 128)
    for t, value in enumerate(((dqt[...] * SCORE_SCALE).T.astype(BF), jnp.concatenate(dks, axis=0),
                               jnp.concatenate(dvs, axis=0))):
        def store(b, piece, t=t):
            stage[doc, t, b // per, b % per * size:(b % per + 1) * size, lanes] = piece
        put_back(value, layout, blocks, size, store)


def backward(nb, ns, rank, layout, qkv, o, g, lse, top, x, gain, rg, low, wq, wk, wv, down, upq, upv, size, tile=256):
    docs, rows, d = x.shape
    parts = o.shape[0]
    w = d // ns
    n = parts * rows
    any_spec = pl.BlockSpec(memory_space=pl.ANY)
    vmem = pl.BlockSpec(memory_space=pltpu.VMEM)
    dma = pltpu.SemaphoreType.DMA
    many = max(16, nb // 16 * ns)
    spec = pl.BlockSpec((parts, 1, rows, 128), lambda i, j: (0, jnp.minimum(i, docs - 1), 0, j))
    row = jax.ShapeDtypeStruct(x.shape, BF)

    def third(t):
        return pl.BlockSpec((1, parts, 1, rows, 128), lambda i, j: (t, 0, jnp.minimum(i, docs - 1), 0, j))

    return pl.pallas_call(
        functools.partial(backward_kernel, nb, ns, rank, size, tile),
        grid=(docs + 1, w // 128),
        in_specs=[pl.BlockSpec(memory_space=pltpu.SMEM), third(0), third(1), third(2), spec, spec]
        + [pl.BlockSpec((1, 1, 2, n), lambda i, j: (jnp.minimum(i, docs - 1), j, 0, 0))]
        + [any_spec] * 2 + [vmem] + [any_spec] * 5 + [vmem] * 3,
        out_specs=[any_spec, any_spec, vmem],
        out_shape=[row, row, jax.ShapeDtypeStruct((16, 8, 128), F32)],
        scratch_shapes=[pltpu.VMEM((128, n), F32), pltpu.VMEM((docs, 3, parts, rows, w), BF),
                        pltpu.VMEM(x.shape, BF), pltpu.VMEM(x.shape, F32), pltpu.VMEM((3, ns, docs, rows, w), BF)]
        + [pltpu.VMEM(wq.shape, BF)] * 3
        + [pltpu.VMEM(low.shape, BF), pltpu.VMEM(x.shape, BF)] + [pltpu.VMEM((128, d), F32)] * 3
        + [pltpu.VMEM((16, 8, 128), F32), pltpu.VMEM((16, 8, 128), F32), pltpu.VMEM((nb // 16 * ns, 8, 128), F32),
           pltpu.VMEM((16, 8, 128), F32),
           dma((6,)), dma((3, docs, ns)), dma((3, docs, ns)), dma((docs, CUTS)), dma((docs, CUTS)), dma((docs,)), dma((docs,)),
           dma((3, many)), dma((3, many))],
        compiler_params=pltpu.CompilerParams(collective_id=3, has_side_effects=True, vmem_limit_bytes=62 << 20),
        name="backward",
    )(layout, qkv, qkv, qkv, o, g, lse, top, x, gain, rg, low, wq, wk, wv, down, upq, upv)


def local(
    nb, ns,
    tokens, cotangent, layout, attention_norm_gain, feedforward_norm_gain,
    query_weight, key_weight, value_weight, attention_output_weight, up_weight, down_weight,
    query_down_adapter, query_up_adapter, value_down_adapter, value_up_adapter,
):
    docs, rows, d = tokens.shape
    size = rows * ns // layout.shape[0]
    rank = query_up_adapter.shape[0]
    down = jnp.pad(jnp.concatenate([query_down_adapter, value_down_adapter], axis=1), ((0, 0), (0, 128 - 2 * rank)))
    upq = jnp.pad((ADAPTER_SCALE * query_up_adapter).astype(BF), ((0, 128 - rank), (0, 0)))
    upv = jnp.pad((ADAPTER_SCALE * value_up_adapter).astype(BF), ((rank, 128 - 2 * rank), (0, 0)))
    gain1 = attention_norm_gain[None]
    gain2 = feedforward_norm_gain[None]

    qkv, att, mixed, lse, low, x, cot, wq, wk, wv, wo, w_up = front(
        nb, ns, layout, tokens, cotangent, query_weight, key_weight, value_weight, attention_output_weight, up_weight,
        gain1, down, jnp.stack([upq, jnp.zeros_like(upq), upv]), size)
    out, rg, mix = middle(nb, ns, x, mixed, cotangent, cot, gain2, wo.reshape(d, d), w_up, down_weight)
    stays = lax.axis_index("batch") % 2 == lax.axis_index("seq") % 2
    got, input_grad, sums = backward(
        nb, ns, rank, layout, qkv, att, mix, lse, out, x, gain1, rg, low, wq, wk, wv, down, upq, upv, size)
    layer_out = jnp.where(stays, out, got)
    sums = sums.reshape(2, d // 128, 2 * rank, 128).transpose(0, 2, 1, 3).reshape(2, 2 * rank, d)
    return (layer_out, input_grad, sums[0, :rank].T, sums[1, :rank], sums[0, rank:].T, sums[1, rank:])


def solution(mesh):
    spec = P("batch", "seq", None)
    weight = P("batch", None)
    return jax.shard_map(
        functools.partial(local, mesh.shape["batch"], mesh.shape["seq"]),
        mesh=mesh,
        in_specs=(spec, spec, P(), P(), P()) + (weight,) * 6 + (P(),) * 4,
        out_specs=(spec, spec, P(), P(), P(), P()),
        check_vma=False,
    )
```

```python
import functools
import math

import jax
import jax.numpy as jnp
from jax import lax
from jax.experimental import pallas as pl
from jax.experimental.pallas import tpu as pltpu
from jax.sharding import PartitionSpec as P


EPSILON = 1e-05
ADAPTER_SCALE = 8.0
SCORE_SCALE = 0.125
NEG_FILL = -1e30
GELU_C = 0.7978845608028654
LOG2E = math.log2(math.e)
F32 = jnp.float32
BF = jnp.bfloat16
NN = (((1,), (0,)), ((), ()))
NT = (((1,), (1,)), ((), ()))
TN = (((0,), (0,)), ((), ()))


def dot(a, b, dims=NN):
    return lax.dot_general(a, b, dims, preferred_element_type=F32)


def normalise(x):
    mean = jnp.mean(x, axis=-1, keepdims=True)
    centred = x - mean
    inv = lax.rsqrt(jnp.mean(centred * centred, axis=-1, keepdims=True) + EPSILON)
    return centred * inv, inv


def norm_back(xh, inv, gain, up):
    t = up * gain
    return inv * (t - jnp.mean(t, axis=-1, keepdims=True) - xh * jnp.mean(t * xh, axis=-1, keepdims=True))


def gelu_parts(u):
    cubic = 0.044715 * u * u
    th = jnp.tanh(GELU_C * (u + cubic * u))
    half = 0.5 * (1.0 + th)
    return half * u, half + (0.5 * GELU_C) * u * (1.0 - th * th) * (1.0 + 3.0 * cubic)


MESH = pl.DeviceIdType.MESH


def flip(i, bits, width=5):
    out = 0
    for n in range(width):
        bit = 1 << n
        out = out + ((i // bit) % 2 + (bits // bit) % 2) % 2 * bit
    return out


def trade(b, s):
    return b - b % 2 + s % 2, s - s % 2 + b % 2


class Place:
    def __init__(self, nb, ns):
        self.nb, self.ns = nb, ns
        self.b, self.s = lax.axis_index("batch"), lax.axis_index("seq")
        self.lines = nb // 4
        self.line = self.b // 4
        self.partner = trade(self.b, self.s)
        self.stays = self.b % 2 == self.s % 2
        self.doc, self.part = trade(self.b, self.s)

    def peer(self, r):
        return trade(self.doc, flip(self.part, r))

    def hello(self, ways):
        bar = pltpu.get_barrier_semaphore()
        for device, cond in ways:
            def signal(device=device):
                pl.semaphore_signal(bar, inc=1, device_id=device, device_id_type=MESH)
            signal() if cond is None else pl.when(cond)(signal)

    def met(self, ways):
        count = 0
        for _, cond in ways:
            count = count + (1 if cond is None else jnp.where(cond, 1, 0))
        pl.semaphore_wait(pltpu.get_barrier_semaphore(), count)

    def greet(self, ways):
        self.hello(ways)
        self.met(ways)

    def gather_ways(self):
        b, s = self.b, self.s
        return [((b + 4, s), self.line + 1 < self.lines), ((b - 4, s), self.line > 0),
                ((flip(b, 2), s), None), ((flip(b, 1), s), None)]


class Gather:
    def __init__(self, place, own, full, send, recv):
        self.p, self.own, self.full, self.send, self.recv = place, own, full, send, recv

    def part(self, line, pair=0, core=0):
        b = self.p.b
        return line * 4 + (b // 2 + pair) % 2 * 2 + (b + core) % 2

    def copy(self, i, way, src=None):
        p = self.p
        to = [p.b + 4, p.b - 4, self.part(p.line, 1), self.part(p.line, 0, 1)][way]
        return pltpu.make_async_remote_copy(
            src_ref=self.full.at[i] if src is None else src, dst_ref=self.full.at[i],
            send_sem=self.send.at[way, i], recv_sem=self.recv.at[i],
            device_id=(to, p.s), device_id_type=MESH)

    def mine(self):
        return pltpu.make_async_copy(self.own, self.full.at[self.p.b], self.recv.at[self.p.b])

    def start(self):
        p = self.p
        pl.when(p.line + 1 < p.lines)(lambda: self.copy(p.b, 0, self.own).start())
        pl.when(p.line > 0)(lambda: self.copy(p.b, 1, self.own).start())
        self.copy(p.b, 2, self.own).start()
        self.copy(p.b, 3, self.own).start()
        self.mine().start()

    def hop(self, k, pairs=True):
        p = self.p

        def take(way, line):
            i = self.part(line)
            self.copy(i, way).wait_recv()
            more = p.line + 1 < p.lines if way == 0 else p.line > 0
            pl.when(more)(lambda: self.copy(i, way).start())
            if pairs:
                self.copy(i, 2).start()
            self.copy(i, 3).start()

        below, above = p.line - k, p.line + k
        pl.when(below >= 0)(lambda: take(0, below))
        pl.when(above < p.lines)(lambda: take(1, above))

    def pair_line(self, line):
        self.copy(self.part(line), 2).start()

    def relay_line(self, line):
        i = self.part(line, 1)
        self.copy(i, 2).wait_recv()
        self.copy(i, 3).start()

    def relay(self, k):
        p = self.p
        if k == 0:
            self.relay_line(p.line)
        else:
            pl.when(p.line >= k)(lambda: self.relay_line(p.line - k))
            pl.when(p.line + k < p.lines)(lambda: self.relay_line(p.line + k))

    def from_core(self, line, pair):
        self.copy(self.part(line, pair, 1), 3).wait_recv()

    def finish(self):
        self.mine().wait()
        for line in range(self.p.lines):
            for pair in range(2):
                self.from_core(line, pair)

    def drain(self):
        p = self.p
        for line in range(p.lines):
            i = self.part(line)
            pl.when((p.line >= line) & (p.line + 1 < p.lines))(lambda i=i: self.copy(i, 0).wait_send())
            pl.when((p.line <= line) & (p.line > 0))(lambda i=i: self.copy(i, 1).wait_send())
            self.copy(i, 2).wait_send()
            self.copy(i, 3).wait_send()
            self.copy(self.part(line, 1), 3).wait_send()

    def steps(self):
        out = [self.start]
        for k in range(1, self.p.lines):
            out.append(functools.partial(run, [functools.partial(self.hop, k), functools.partial(self.relay, k - 1)]))
        out.append(functools.partial(self.relay, self.p.lines - 1))
        out.append(self.finish)
        return out


def run(calls):
    for call in calls:
        call()


def chosen(blocks, tests):
    out = blocks[0]
    for block, test in zip(blocks[1:], tests[1:]):
        out = jnp.where(test, block, out)
    return out


def picked(ref, layout, blocks, size):
    per = ref.shape[2] // size
    stored = [ref[t // per, 0, (t % per) * size:(t % per + 1) * size, :] for t in range(blocks)]
    return jnp.concatenate([chosen(stored, [layout[t] == p for t in range(blocks)]) for p in range(blocks)], axis=0)


def put_back(value, layout, blocks, size, store):
    pieces = [value[p * size:(p + 1) * size] for p in range(blocks)]
    for t in range(blocks):
        store(t, chosen(pieces, [layout[t] == p for p in range(blocks)]))


def attend(layout, qkv, out, lse_ref, doc, pair, size, tile):
    parts, rows = qkv.shape[1], qkv.shape[3]
    n = parts * rows
    blocks, per = n // size, rows // size
    lanes = pl.ds(pl.multiple_of(pair * 128, 128), 128)

    def in_order(t):
        stored = [qkv[t, b // per, doc, b % per * size:(b % per + 1) * size, lanes] for b in range(blocks)]
        return jnp.concatenate([chosen(stored, [layout[b] == p for b in range(blocks)]) for p in range(blocks)], axis=0)

    q, k, v = in_order(0), in_order(1), in_order(2)
    vt = v.T
    ones = jnp.ones((16, n), BF)
    vts = [jnp.concatenate([vt[64 * h:64 * h + 64], ones], axis=0) for h in range(2)]
    lane = lax.broadcasted_iota(jnp.int32, (1, 128), 1)
    c = SCORE_SCALE * LOG2E
    tri = lax.broadcasted_iota(jnp.int32, (tile, tile), 0) <= lax.broadcasted_iota(jnp.int32, (tile, tile), 1)
    work = [(i, h) for i in range(n // tile) for h in range(2)]
    lses = [[], []]
    mixed = {}
    waiting = []

    def scores(i, h):
        qm = jnp.where((lane < 64) == (h == 0), q[i * tile:(i + 1) * tile], jnp.zeros((), BF))
        return dot(k[:(i + 1) * tile], qm, NT)

    def settle():
        i, h, e, m = waiting.pop(0)
        o = dot(vts[h][:, :(i + 1) * tile], e)
        l = o[64:65]
        mixed[i, h] = o[:64] * (1.0 / l)
        lses[h].append(m + jnp.log2(l))

    ahead = [scores(*work[0]), scores(*work[1])]
    for t, (i, h) in enumerate(work):
        st = ahead.pop(0)
        if t + 2 < len(work):
            ahead.append(scores(*work[t + 2]))
        diag = jnp.where(tri, st[i * tile:], NEG_FILL)
        st = diag if i == 0 else jnp.concatenate([st[: i * tile], diag], axis=0)
        m = jnp.max(st, axis=0, keepdims=True) * c
        waiting.append((i, h, jnp.exp2(st * c - m).astype(BF), m))
        if t:
            settle()
    settle()
    outs = [jnp.concatenate([mixed[i, 0], mixed[i, 1]], axis=0).T.astype(BF) for i in range(n // tile)]

    def store(b, piece):
        out[b // per, doc, b % per * size:(b % per + 1) * size, lanes] = piece

    put_back(jnp.concatenate(outs, axis=0), layout, blocks, size, store)
    for h in range(2):
        lse_ref[doc, pair, h:h + 1, :] = jnp.concatenate(lses[h], axis=1)


UP_START = 1
UP_PLACES = (0, 4, 8)


def one_hot(rows, columns, first):
    at = lax.broadcasted_iota(jnp.int32, (rows, columns), 0) + first
    return (at == lax.broadcasted_iota(jnp.int32, (rows, columns), 1)).astype(BF)


def down_maps(qd, vd):
    rank = qd.shape[0]
    return (dot(qd, one_hot(rank, 128, 0), TN) + dot(vd, one_hot(rank, 128, rank), TN)).astype(BF)


def up_map(up, first):
    return (ADAPTER_SCALE * dot(one_hot(up.shape[0], 128, first), up, TN)).astype(BF)


def front_kernel(nb, ns, size, tile, layout, x_hbm, cot_hbm, wq_ref, wk_ref, wv_ref, wo_ref, up_hbm, gain_ref, qd_ref, qu_ref, vd_ref, vu_ref,
                 qkv_out, att_out, mixed_out, lse_ref, low_out, x_out, cot_out, wq_out, wk_out, wv_out, wo_out, up_out,
                 xs, n1s, stage, qkv, att, lows, ws, own, down_ref, ups_ref, send, recv, usend, urecv, xsend, xrecv, csend, crecv,
                 osend, orecv, asend, arecv, local_sem, qkv_sem, att_sem):
    docs, rows, d = x_hbm.shape
    w = d // ns
    pairs = w // 128
    p = Place(nb, ns)
    fetch = pltpu.make_async_copy(up_hbm, own, local_sem.at[docs + 5])
    fetch.start()
    p.greet(p.gather_ways() + [(p.partner, jnp.logical_not(p.stays))] + [(p.peer(r), None) for r in range(1, ns)])

    def x_remote(i):
        return pltpu.make_async_remote_copy(
            src_ref=x_hbm.at[i], dst_ref=xs.at[i], send_sem=xsend.at[i], recv_sem=xrecv.at[i],
            device_id=p.partner, device_id_type=MESH)

    def cot_remote(i):
        return pltpu.make_async_remote_copy(
            src_ref=cot_hbm.at[i], dst_ref=cot_out.at[i], send_sem=csend.at[i], recv_sem=crecv.at[i],
            device_id=p.partner, device_id_type=MESH)

    def x_local(i):
        return pltpu.make_async_copy(x_hbm.at[i], xs.at[i], xrecv.at[i])

    def x_keep(i):
        return pltpu.make_async_copy(xs.at[i], x_out.at[i], local_sem.at[i])

    for i in range(docs):
        pl.when(p.stays)(lambda i=i: x_local(i).start())
        pl.when(jnp.logical_not(p.stays))(lambda i=i: x_remote(i).start())
    for i in range(docs):
        pl.when(jnp.logical_not(p.stays))(lambda i=i: cot_remote(i).start())

    def first(i):
        pl.when(p.stays)(lambda: x_local(i).wait())
        pl.when(jnp.logical_not(p.stays))(lambda: x_remote(i).wait())
        x_keep(i).start()
        xh, _ = normalise(xs[i].astype(F32))
        n1 = (xh * gain_ref[...]).astype(BF)
        n1s[i] = n1
        lows[i] = dot(n1, down_ref[...]).astype(BF)

    def away(part, i, r):
        return pltpu.make_async_remote_copy(
            src_ref=stage.at[part, i, flip(p.part, r)], dst_ref=qkv.at[part, p.part, i],
            send_sem=osend.at[part, i, r], recv_sem=orecv.at[part, i, r],
            device_id=p.peer(r), device_id_type=MESH)

    def product(part, i):
        y = dot(n1s[i], ws[part].reshape(d, d)) + dot(lows[i], ups_ref[part])
        y = y.astype(BF)
        for g in range(ns):
            piece = y[:, g * w:(g + 1) * w]

            @pl.when(p.part == g)
            def _():
                qkv[part, p.part, i] = piece

            @pl.when(p.part != g)
            def _():
                stage[part, i, g] = piece
        for r in range(1, ns):
            away(part, i, r).start()

    gathers = [Gather(p, own_ref, ws.at[n], send.at[n], recv.at[n])
               for n, own_ref in enumerate((wq_ref, wk_ref, wv_ref, wo_ref))]
    keeps = [pltpu.make_async_copy(ws.at[n], out, local_sem.at[docs + n])
             for n, out in enumerate((wq_out, wk_out, wv_out, wo_out))]
    low_keep = pltpu.make_async_copy(lows, low_out, local_sem.at[docs + 4])
    up_steps = Gather(p, own, up_out, usend, urecv).steps()

    lists = [g.steps() for g in gathers]
    delays = (0, 0, 2, 4)
    ready = [len(lists[0]) - 1 + delay for delay in delays]

    def slot(t):
        for n, steps in enumerate(lists):
            if 0 <= t - delays[n] < len(steps):
                steps[t - delays[n]]()
            if t == ready[n]:
                keeps[n].start()
        if t == UP_START + ready[0]:
            fetch.wait()
            up_steps[0]()

    slot(0)
    rank = qu_ref.shape[0]
    down_ref[...] = down_maps(qd_ref[...], vd_ref[...])
    ups_ref[0] = up_map(qu_ref[...], 0)
    ups_ref[1] = jnp.zeros((128, d), BF)
    ups_ref[2] = up_map(vu_ref[...], rank)
    for t in range(1, ready[0] + 1):
        slot(t)
    places = {2 * docs - 5 + 2 * n: t for n, t in enumerate(range(ready[0] + 1, ready[3] + 1))}

    def one_product(n, carry):
        early = n < 2 * docs
        part = jnp.where(early, n % 2, 2)
        i = jnp.where(early, n // 2, n - 2 * docs)
        pl.when(early & (part == 0))(lambda: first(i))
        product(part, i)
        for at, t in places.items():
            pl.when(n == at)(functools.partial(slot, t))
        return carry

    lax.fori_loop(0, 3 * docs, one_product, 0)
    low_keep.start()

    def qkv_keep(i):
        return pltpu.make_async_copy(qkv.at[:, :, i], qkv_out.at[:, :, i], qkv_sem.at[i])

    def att_keep(i):
        return pltpu.make_async_copy(att.at[:, i], att_out.at[:, i], att_sem.at[i, 0])

    def att_home(i):
        return pltpu.make_async_copy(att.at[p.part, i], mixed_out.at[p.part, i], att_sem.at[i, 1])

    def att_away(i, r):
        return pltpu.make_async_remote_copy(
            src_ref=att.at[flip(p.part, r), i], dst_ref=mixed_out.at[p.part, i], send_sem=asend.at[i, r],
            recv_sem=arecv.at[i, r], device_id=p.peer(r), device_id_type=MESH)

    inside = [n for n in range(1, len(up_steps)) if n <= len(UP_PLACES) and UP_PLACES[n - 1] < docs * pairs]

    def one_pair(m, carry):
        doc, pair = m // pairs, m % pairs
        for n in inside:
            pl.when(m == UP_PLACES[n - 1])(up_steps[n])

        @pl.when(pair == 0)
        def _():
            for part in range(3):
                for r in range(1, ns):
                    away(part, doc, r).wait()
            qkv_keep(doc).start()

        attend(layout, qkv, att, lse_ref, doc, pair, size, tile)

        @pl.when(pair == pairs - 1)
        def _():
            att_keep(doc).start()
            att_home(doc).start()
            for r in range(1, ns):
                att_away(doc, r).start()

        return carry

    lax.fori_loop(0, docs * pairs, one_pair, 0)
    for n in range(1, len(up_steps)):
        if n not in inside:
            up_steps[n]()
    for i in range(docs):
        x_keep(i).wait()
        pl.when(jnp.logical_not(p.stays))(lambda i=i: cot_remote(i).wait())
        qkv_keep(i).wait()
        att_keep(i).wait()
        att_home(i).wait()
        for r in range(1, ns):
            att_away(i, r).wait()
    for keep in keeps:
        keep.wait()
    low_keep.wait()
    for g in gathers + [Gather(p, own, up_out, usend, urecv)]:
        g.drain()


def front(nb, ns, layout, x, cot, wq, wk, wv, wo, up, gain, adapters, size, tile=256):
    docs, rows, d = x.shape
    w = d // ns
    n = rows * ns
    any_spec = pl.BlockSpec(memory_space=pl.ANY)
    vmem = pl.BlockSpec(memory_space=pltpu.VMEM)
    dma = pltpu.SemaphoreType.DMA
    like = lambda *shape: jax.ShapeDtypeStruct(shape, BF)
    heads = (ns, docs, rows, w)
    outs = [like(3, *heads), like(*heads), like(*heads), jax.ShapeDtypeStruct((docs, w // 128, 2, n), F32),
            like(docs, rows, 128), like(*x.shape), like(*x.shape)] + [like(nb, *wq.shape)] * 4 + [like(nb, *up.shape)]
    return pl.pallas_call(
        functools.partial(front_kernel, nb, ns, size, tile),
        in_specs=[pl.BlockSpec(memory_space=pltpu.SMEM)] + [any_spec] * 7 + [vmem] * 5,
        out_specs=[any_spec] * 3 + [vmem] + [any_spec] * 8,
        out_shape=outs,
        scratch_shapes=[pltpu.VMEM(x.shape, BF), pltpu.VMEM(x.shape, BF), pltpu.VMEM((3, docs, ns, rows, w), BF),
                        pltpu.VMEM((3,) + heads, BF), pltpu.VMEM(heads, BF), pltpu.VMEM((docs, rows, 128), BF),
                        pltpu.VMEM((4, nb) + wq.shape, BF), pltpu.VMEM(up.shape, BF),
                        pltpu.VMEM((d, 128), BF), pltpu.VMEM((3, 128, d), BF), dma((4, 4, nb)), dma((4, nb)), dma((4, nb)), dma((nb,)), dma((docs,)), dma((docs,)),
                        dma((docs,)), dma((docs,)), dma((3, docs, ns)), dma((3, docs, ns)), dma((docs, ns)), dma((docs, ns)),
                        dma((docs + 6,)), dma((docs,)), dma((docs, 2))],
        compiler_params=pltpu.CompilerParams(collective_id=0, has_side_effects=True, vmem_limit_bytes=62 << 20),
        name="front",
    )(layout, x, cot, wq, wk, wv, wo, up, gain, *adapters)


def middle_kernel(nb, ns, x_hbm, att_hbm, kept_hbm, cot_hbm, gain_ref, wo_hbm, up_hbm, down_hbm,
                  out_hbm, rg_hbm, mix_hbm,
                  xs, atts, cots, wos, downs, ups, acc, xhs, dn, n2s, invs, us, gs,
                  send, recv, msend, mrecv, load, store):
    docs, rows, d = x_hbm.shape
    w = d // ns
    p = Place(nb, ns)
    held = down_hbm.shape[0]
    chunk = 2 * held
    loads = [pltpu.make_async_copy(wo_hbm, wos, load.at[0]), pltpu.make_async_copy(att_hbm, atts, load.at[3 + docs])]
    for i in range(docs):
        loads.append(pltpu.make_async_copy(x_hbm.at[i], xs.at[i], load.at[1 + i]))
    loads.append(pltpu.make_async_copy(up_hbm, ups, load.at[1 + docs]))
    for copy in loads:
        copy.start()

    def cot_load(source):
        return pltpu.make_async_copy(source, cots, load.at[2 + docs])

    pl.when(p.stays)(lambda: cot_load(kept_hbm).start())
    pl.when(jnp.logical_not(p.stays))(lambda: cot_load(cot_hbm).start())
    p.greet(p.gather_ways() + [(p.peer(r), None) for r in range(1, ns)])

    gather = Gather(p, down_hbm, downs, send, recv)

    gather.start()
    for copy in loads[:-1]:
        copy.wait()
    def rows_of(i):
        return pl.ds(pl.multiple_of(i * rows, rows), rows)

    def second_norm(i, carry):
        at = rows_of(i)
        res = xs[i].astype(F32)
        for g in range(ns):
            res = res + dot(atts[g, i], wos[g * w:(g + 1) * w, :])
        acc[at, :] = res
        xh, inv = normalise(res)
        xhs[at, :] = xh
        invs[at, :] = jnp.broadcast_to(inv, (rows, 128))
        n2s[at, :] = (xh * gain_ref[...]).astype(BF)
        dn[at, :] = jnp.zeros((rows, d), F32)
        return carry

    lax.fori_loop(0, docs, second_norm, 0)
    loads[-1].wait()
    cot_load(cot_hbm).wait()
    gather.mine().wait()
    pair = p.b // 2 % 2

    def weights(f):
        base = flip(p.line, f // 2) * 4 + (pair + f) % 2 * 2
        up = ups[:, :, pl.ds(pl.multiple_of(base * held, chunk), chunk)].reshape(d, chunk)
        return up, downs[pl.ds(base, 2)].reshape(chunk, d)

    def hidden(t):
        up, down = weights(t // docs)
        us[t % 2] = dot(n2s[rows_of(t % docs), :], up)
        gs[t % 2] = dot(cots[t % docs], down, NT)

    def one_tile(t, carry):
        f, i = t // docs, t % docs

        @pl.when(t + 1 < nb // 2 * docs)
        def _():
            after = (t + 1) // docs
            pl.when(i == docs - 1)(lambda: gather.from_core(flip(p.line, after // 2), after % 2))

            @pl.when((i == docs - 1) & (f % 2 == 0))
            def _():
                pl.when(f // 2 + 1 < p.lines)(lambda: gather.hop(f // 2 + 1, pairs=False))
                pl.when(f // 2 + 1 < p.lines)(lambda: gather.pair_line(flip(p.line, f // 2 + 1)))

            pl.when((i == min(1, docs - 1)) & (f % 2 == 0))(lambda: gather.relay_line(flip(p.line, f // 2)))

        hidden(jnp.minimum(t + 1, nb // 2 * docs - 1))
        up, down = weights(f)
        act, slope = gelu_parts(us[t % 2])
        pg = (slope * gs[t % 2]).astype(BF)
        at = rows_of(i)
        acc[at, :] += dot(act.astype(BF), down)
        dn[at, :] += dot(pg, up, NT)
        return carry

    gather.from_core(p.line, 0)
    hidden(0)
    lax.fori_loop(0, nb // 2 * docs, one_tile, 0)

    def out_and_grad(i, carry):
        at = rows_of(i)
        xs[i] = acc[at, :].astype(BF)
        rg = cots[i].astype(F32) + norm_back(xhs[at, :], invs[at, :1], gain_ref[...], dn[at, :])
        xhs[at, :] = rg
        mix = dot(rg.astype(BF), wos[...], NT).astype(BF)
        for g in range(ns):
            atts[g, i] = mix[:, g * w:(g + 1) * w]
        for copy in results(i):
            copy.start()
        return carry

    def results(i):
        out = [pltpu.make_async_copy(atts.at[p.part, i], mix_hbm.at[p.part, i], store.at[2, i]),
               pltpu.make_async_copy(xs.at[i], out_hbm.at[i], store.at[0, i]),
               pltpu.make_async_copy(xhs.at[rows_of(i)], rg_hbm.at[i], store.at[1, i])]
        for r in range(1, ns):
            out.append(pltpu.make_async_remote_copy(
                src_ref=atts.at[flip(p.part, r), i], dst_ref=mix_hbm.at[p.part, i], send_sem=msend.at[i, r],
                recv_sem=mrecv.at[i, r], device_id=p.peer(r), device_id_type=MESH))
        return out

    lax.fori_loop(0, docs, out_and_grad, 0)
    for i in range(docs):
        for copy in results(i):
            copy.wait()
    gather.drain()


def middle(nb, ns, x, att, kept, cot, gain, wo, up, down):
    docs, rows, d = x.shape
    w = d // ns
    n = docs * rows
    any_spec = pl.BlockSpec(memory_space=pl.ANY)
    vmem = pl.BlockSpec(memory_space=pltpu.VMEM)
    dma = pltpu.SemaphoreType.DMA
    return pl.pallas_call(
        functools.partial(middle_kernel, nb, ns),
        in_specs=[any_spec] * 4 + [vmem] + [any_spec] * 3,
        out_specs=[any_spec] * 3,
        out_shape=[jax.ShapeDtypeStruct((docs, rows, d), BF), jax.ShapeDtypeStruct((docs, rows, d), F32),
                   jax.ShapeDtypeStruct((ns, docs, rows, w), BF)],
        scratch_shapes=[pltpu.VMEM((docs, rows, d), BF), pltpu.VMEM((ns, docs, rows, w), BF),
                        pltpu.VMEM((docs, rows, d), BF), pltpu.VMEM(wo.shape, BF), pltpu.VMEM((nb,) + down.shape, BF),
                        pltpu.VMEM(up.shape, BF), pltpu.VMEM((n, d), F32),
                        pltpu.VMEM((n, d), F32), pltpu.VMEM((n, d), F32), pltpu.VMEM((n, d), BF),
                        pltpu.VMEM((n, 128), F32), pltpu.VMEM((2, rows, 2 * down.shape[0]), F32),
                        pltpu.VMEM((2, rows, 2 * down.shape[0]), F32),
                        dma((4, nb)), dma((nb,)), dma((docs, ns)), dma((docs, ns)), dma((4 + docs,)), dma((3, docs))],
        compiler_params=pltpu.CompilerParams(collective_id=2, has_side_effects=True, vmem_limit_bytes=63 << 20),
        name="feed_forward",
    )(x, att, kept, cot, gain, wo, up, down)


class DeviceSum:
    def __init__(self, p, mine, first, second, total, sends, recvs):
        self.p, self.mine, self.first, self.second, self.total = p, mine, first, second, total
        self.sends, self.recvs = sends, recvs
        self.slot, self.block = p.b % 16, p.b - p.b % 16
        self.many = p.nb // 16 * p.ns
        self.at = (p.b // 16) * p.ns + p.s

    def copy(self, phase, j, src, dst, device):
        return pltpu.make_async_remote_copy(
            src_ref=src, dst_ref=dst, send_sem=self.sends.at[phase, j], recv_sem=self.recvs.at[phase, j],
            device_id=device, device_id_type=MESH)

    def fellow(self, j):
        return (self.block + flip(self.slot, j), self.p.s)

    def scatter(self, j):
        return self.copy(0, j, self.mine.at[flip(self.slot, j)], self.first.at[self.slot], self.fellow(j))

    def share(self, j):
        to, ns = flip(self.at, j), self.p.ns
        return self.copy(1, j, self.second.at[self.at], self.second.at[self.at], ((to // ns) * 16 + self.slot, to % ns))

    def spread(self, j):
        return self.copy(2, j, self.total.at[self.slot], self.total.at[self.slot], self.fellow(j))

    def begin(self):
        for j in range(1, 16):
            self.scatter(j).start()
        self.first[self.slot] = self.mine[self.slot]

    def middle(self):
        for j in range(1, 16):
            self.scatter(j).wait()
        self.second[self.at] = jnp.sum(self.first[...], axis=0)
        for j in range(1, self.many):
            self.share(j).start()

    def end(self):
        for j in range(1, self.many):
            self.share(j).wait()
        self.total[self.slot] = jnp.sum(self.second[...], axis=0)
        for j in range(1, 16):
            self.spread(j).start()

    def finish(self):
        for j in range(1, 16):
            self.spread(j).wait()


def sum_ways(p):
    b, s, nb, ns = p.b, p.s, p.nb, p.ns
    slot, block = b % 16, b - b % 16
    at = (b // 16) * ns + s
    ways = [((block + flip(slot, j), s), None) for j in range(1, 16)]
    for j in range(1, nb // 16 * ns):
        to = flip(at, j)
        ways.append((((to // ns) * 16 + slot, to % ns), None))
    return ways


CUTS = 2


def backward_kernel(nb, ns, rank, size, tile, layout, q_ref, k_ref, v_ref, o_ref, g_ref, lse_ref, top_hbm, x_hbm, gain_ref,
                    rg_hbm, low_hbm, wq_hbm, wk_hbm, wv_hbm, qd_ref, qu_ref, vd_ref, vu_ref, top_out, out_hbm, sum_ref,
                    dqt, stage, xs, rgs, ds, wqs, wks, wvs, lows, outs, gds, gqs, gvs, mine, first, second, summed,
                    tops, xhs, lgs, down_ref, upq_ref, upv_ref,
                    load, dsend, drecv, osend, orecv, tsend, trecv, ssend, srecv):
    docs, rows, d = x_hbm.shape
    w = d // ns
    p = Place(nb, ns)
    doc, pair = pl.program_id(0), pl.program_id(1)
    pairs = w // 128
    loads = [pltpu.make_async_copy(a, v, load.at[n]) for n, (a, v) in enumerate(
        ((wq_hbm, wqs), (wk_hbm, wks), (wv_hbm, wvs), (low_hbm, lows), (x_hbm, xs), (rg_hbm, rgs)))]

    def away(t, i, r, n):
        at = pl.ds(pl.multiple_of(n * 128, 128), 128)
        return pltpu.make_async_remote_copy(
            src_ref=stage.at[i, t, flip(p.part, r), :, at], dst_ref=ds.at[t, p.part, i, :, at], send_sem=dsend.at[t, i, r, n],
            recv_sem=drecv.at[t, i, r, n], device_id=p.peer(r), device_id_type=MESH)

    cut = rows // CUTS

    def out_away(i, n):
        at = pl.ds(pl.multiple_of(n * cut, cut), cut)
        return pltpu.make_async_remote_copy(
            src_ref=outs.at[i, at], dst_ref=out_hbm.at[i, at], send_sem=osend.at[i, n], recv_sem=orecv.at[i, n],
            device_id=p.partner, device_id_type=MESH)

    def out_home(i, n):
        at = pl.ds(pl.multiple_of(n * cut, cut), cut)
        return pltpu.make_async_copy(outs.at[i, at], out_hbm.at[i, at], orecv.at[i, n])

    def top_away(i):
        return pltpu.make_async_remote_copy(
            src_ref=top_hbm.at[i], dst_ref=top_out.at[i], send_sem=tsend.at[i], recv_sem=trecv.at[i],
            device_id=p.partner, device_id_type=MESH)

    top_in = pltpu.make_async_copy(top_hbm, tops, tsend.at[0])
    top_home = pltpu.make_async_copy(tops, top_out, trecv.at[0])
    ways = [(p.peer(r), None) for r in range(1, ns)] + [(p.partner, jnp.logical_not(p.stays))] + sum_ways(p)
    total = DeviceSum(p, mine, first, second, summed, ssend, srecv)

    @pl.when((doc == 0) & (pair == 0))
    def _():
        p.hello(ways)
        for copy in loads:
            copy.start()
        pl.when(p.stays)(lambda: top_in.start())
        down_ref[...] = down_maps(qd_ref[...], vd_ref[...])
        upq_ref[...] = up_map(qu_ref[...], 0)
        upv_ref[...] = up_map(vu_ref[...], rank)
        gds[...] = jnp.zeros_like(gds)
        gqs[...] = jnp.zeros_like(gqs)
        gvs[...] = jnp.zeros_like(gvs)

    @pl.when(doc < docs)
    def _():
        attention_gradients(layout, q_ref, k_ref, v_ref, o_ref, g_ref, lse_ref, stage, dqt, doc, pair, size, tile)

        @pl.when((doc == 0) & (pair == 0))
        def _():
            p.met(ways)
            pl.when(p.stays)(lambda: top_in.wait())
            pl.when(p.stays)(lambda: top_home.start())
            for i in range(docs):
                pl.when(jnp.logical_not(p.stays))(lambda i=i: top_away(i).start())

        for t in range(3):
            for r in range(1, ns):
                away(t, doc, r, pair).start()

    @pl.when((doc > 0) & (pair == 0))
    def _():
        i = doc - 1

        @pl.when(i == 0)
        def _():
            for copy in loads:
                copy.wait()

        for t in range(3):
            for r in range(1, ns):
                for n in range(pairs):
                    away(t, i, r, n).wait()

        xh, inv = normalise(xs[i].astype(F32))
        xhs[:, :d] = xh
        xhs[:, d:] = jnp.broadcast_to(inv, (rows, 128))
        lg = jnp.zeros((rows, 128), F32)
        for r in range(ns):
            g = flip(p.part, r)
            cols = pl.ds(pl.multiple_of(g * w, w), w)
            for t, up, grads in ((0, upq_ref, gqs), (2, upv_ref, gvs)):
                piece = ds[t, g, i] if r else stage[i, t, p.part]
                lg = lg + dot(piece, up[:, cols], NT)
                grads[:, cols] += dot(lows[i], piece, TN)
        lgs[...] = lg.astype(BF)
        gds[...] += dot(lgs[...], (xh * gain_ref[...]).astype(BF), TN)

        @pl.when(i == docs - 1)
        def _():
            upper = lax.broadcasted_iota(jnp.int32, (2 * rank, 1), 0) < rank
            both = jnp.where(upper, gqs[:2 * rank, :], gvs[:2 * rank, :]) * ADAPTER_SCALE
            for n in range(8):
                mine[n] = gds[:8, n * 128:(n + 1) * 128]
                mine[8 + n] = both[:, n * 128:(n + 1) * 128]
            total.begin()

        def some_rows(n, carry):
            at = pl.ds(pl.multiple_of(n * cut, cut), cut)
            fg = dot(lgs[at, :], down_ref[...], NT)
            for r in range(ns):
                g = flip(p.part, r)
                cols = pl.ds(pl.multiple_of(g * w, w), w)
                for t, full in enumerate((wqs, wks, wvs)):
                    piece = ds[t, g, i, at, :] if r else stage[i, t, p.part, at, :]
                    fg = fg + dot(piece, full[:, :, cols].reshape(d, w), NT)
            outs[i, at, :] = (rgs[i, at, :] + norm_back(xhs[at, :d], xhs[at, d:d + 1], gain_ref[...], fg)).astype(BF)
            pl.when(p.stays)(lambda: out_home(i, n).start())
            pl.when(jnp.logical_not(p.stays))(lambda: out_away(i, n).start())
            pl.when((i == docs - 1) & (n == 0))(total.middle)
            return carry

        lax.fori_loop(0, CUTS, some_rows, 0)
        pl.when(i == docs - 1)(total.end)

    @pl.when((doc == docs) & (pair == pairs - 1))
    def _():
        total.finish()
        sum_ref[...] = summed[...]
        pl.when(p.stays)(lambda: top_home.wait())
        for i in range(docs):
            for n in range(CUTS):
                pl.when(p.stays)(lambda i=i, n=n: out_home(i, n).wait())
                pl.when(jnp.logical_not(p.stays))(lambda i=i, n=n: out_away(i, n).wait())
            pl.when(jnp.logical_not(p.stays))(lambda i=i: top_away(i).wait())


def attention_gradients(layout, q_ref, k_ref, v_ref, o_ref, g_ref, lse_ref, stage, dqt, doc, pair, size, tile):
    parts, rows = o_ref.shape[0], o_ref.shape[2]
    n = parts * rows
    blocks, per = n // size, rows // size
    q = picked(q_ref.at[0], layout, blocks, size)
    k = picked(k_ref.at[0], layout, blocks, size)
    v = picked(v_ref.at[0], layout, blocks, size)
    o = picked(o_ref, layout, blocks, size)
    g = picked(g_ref, layout, blocks, size)
    kt = k.T
    lane = lax.broadcasted_iota(jnp.int32, (1, 128), 1)
    c = SCORE_SCALE * LOG2E
    tri = lax.broadcasted_iota(jnp.int32, (tile, tile), 0) <= lax.broadcasted_iota(jnp.int32, (tile, tile), 1)
    prod = (o.astype(F32) * g.astype(F32)).astype(BF)
    heads = (lax.broadcasted_iota(jnp.int32, (8, 128), 1) // 64 == lax.broadcasted_iota(jnp.int32, (8, 128), 0)).astype(BF)
    delta = dot(heads, prod, NT)
    zero = jnp.zeros((), BF)
    masks = [(lane < 64) == (h == 0) for h in range(2)]
    qms = [jnp.where(mk, q, zero) for mk in masks]
    gms = [jnp.where(mk, g, zero) for mk in masks]
    lse = lse_ref[0, 0]
    dks, dvs = [], []
    work = [(j, h) for j in range(n // tile) for h in range(2)]

    def products(j, h):
        lo, hi = j * tile, (j + 1) * tile
        return dot(k[lo:hi], qms[h][lo:], NT), dot(v[lo:hi], gms[h][lo:], NT)

    waiting = []
    sums = {}

    def settle():
        j, h, p, ds = waiting.pop(0)
        lo, hi = j * tile, (j + 1) * tile
        dv = dot(p, gms[h][lo:])
        dk = dot(ds, qms[h][lo:])
        dq = dot(kt[64 * h:64 * h + 64, lo:hi], ds)
        if j == 0:
            dqt[64 * h:64 * h + 64, :] = dq
        else:
            dqt[64 * h:64 * h + 64, lo:] += dq
        if h == 0:
            sums[j] = dk, dv
        else:
            dks.append(((sums[j][0] + dk) * SCORE_SCALE).astype(BF))
            dvs.append((sums[j][1] + dv).astype(BF))

    ahead = products(*work[0])
    for t, (j, h) in enumerate(work):
        st, dp = ahead
        if t + 1 < len(work):
            ahead = products(*work[t + 1])
        lo, hi = j * tile, (j + 1) * tile
        p = jnp.exp2(st * c - lse[h:h + 1, lo:])
        diag = jnp.where(tri, p[:, :tile], 0.0)
        p = diag if hi == n else jnp.concatenate([diag, p[:, tile:]], axis=1)
        waiting.append((j, h, p.astype(BF), (p * (dp - delta[h:h + 1, lo:])).astype(BF)))
        if t:
            settle()
    settle()
    lanes = pl.ds(pl.multiple_of(pair * 128, 128), 128)
    for t, value in enumerate(((dqt[...] * SCORE_SCALE).T.astype(BF), jnp.concatenate(dks, axis=0),
                               jnp.concatenate(dvs, axis=0))):
        def store(b, piece, t=t):
            stage[doc, t, b // per, b % per * size:(b % per + 1) * size, lanes] = piece
        put_back(value, layout, blocks, size, store)


def backward(nb, ns, rank, layout, qkv, o, g, lse, top, x, gain, rg, low, wq, wk, wv, adapters, size, tile=256):
    docs, rows, d = x.shape
    parts = o.shape[0]
    w = d // ns
    n = parts * rows
    any_spec = pl.BlockSpec(memory_space=pl.ANY)
    vmem = pl.BlockSpec(memory_space=pltpu.VMEM)
    dma = pltpu.SemaphoreType.DMA
    many = max(16, nb // 16 * ns)
    spec = pl.BlockSpec((parts, 1, rows, 128), lambda i, j: (0, jnp.minimum(i, docs - 1), 0, j))
    row = jax.ShapeDtypeStruct(x.shape, BF)

    def third(t):
        return pl.BlockSpec((1, parts, 1, rows, 128), lambda i, j: (t, 0, jnp.minimum(i, docs - 1), 0, j))

    return pl.pallas_call(
        functools.partial(backward_kernel, nb, ns, rank, size, tile),
        grid=(docs + 1, w // 128),
        in_specs=[pl.BlockSpec(memory_space=pltpu.SMEM), third(0), third(1), third(2), spec, spec]
        + [pl.BlockSpec((1, 1, 2, n), lambda i, j: (jnp.minimum(i, docs - 1), j, 0, 0))]
        + [any_spec] * 2 + [vmem] + [any_spec] * 5 + [vmem] * 4,
        out_specs=[any_spec, any_spec, vmem],
        out_shape=[row, row, jax.ShapeDtypeStruct((16, 8, 128), F32)],
        scratch_shapes=[pltpu.VMEM((128, n), F32), pltpu.VMEM((docs, 3, parts, rows, w), BF),
                        pltpu.VMEM(x.shape, BF), pltpu.VMEM(x.shape, F32), pltpu.VMEM((3, ns, docs, rows, w), BF)]
        + [pltpu.VMEM(wq.shape, BF)] * 3
        + [pltpu.VMEM(low.shape, BF), pltpu.VMEM(x.shape, BF)] + [pltpu.VMEM((128, d), F32)] * 3
        + [pltpu.VMEM((16, 8, 128), F32), pltpu.VMEM((16, 8, 128), F32), pltpu.VMEM((nb // 16 * ns, 8, 128), F32),
           pltpu.VMEM((16, 8, 128), F32),
           pltpu.VMEM(x.shape, BF), pltpu.VMEM((rows, d + 128), F32), pltpu.VMEM((rows, 128), BF),
           pltpu.VMEM((d, 128), BF), pltpu.VMEM((128, d), BF), pltpu.VMEM((128, d), BF),
           dma((6,)), dma((3, docs, ns, w // 128)), dma((3, docs, ns, w // 128)), dma((docs, CUTS)), dma((docs, CUTS)), dma((docs,)), dma((docs,)),
           dma((3, many)), dma((3, many))],
        compiler_params=pltpu.CompilerParams(collective_id=3, has_side_effects=True, vmem_limit_bytes=62 << 20),
        name="backward",
    )(layout, qkv, qkv, qkv, o, g, lse, top, x, gain, rg, low, wq, wk, wv, *adapters)


def local(
    nb, ns,
    tokens, cotangent, layout, attention_norm_gain, feedforward_norm_gain,
    query_weight, key_weight, value_weight, attention_output_weight, up_weight, down_weight,
    query_down_adapter, query_up_adapter, value_down_adapter, value_up_adapter,
):
    docs, rows, d = tokens.shape
    size = rows * ns // layout.shape[0]
    rank = query_up_adapter.shape[0]
    adapters = (query_down_adapter.T, query_up_adapter, value_down_adapter.T, value_up_adapter)
    gain1 = attention_norm_gain[None]
    gain2 = feedforward_norm_gain[None]

    qkv, att, mixed, lse, low, x, cot, wq, wk, wv, wo, w_up = front(
        nb, ns, layout, tokens, cotangent, query_weight, key_weight, value_weight, attention_output_weight, up_weight,
        gain1, adapters, size)
    out, rg, mix = middle(nb, ns, x, mixed, cotangent, cot, gain2, wo.reshape(d, d), w_up, down_weight)
    layer_out, input_grad, sums = backward(
        nb, ns, rank, layout, qkv, att, mix, lse, out, x, gain1, rg, low, wq, wk, wv, adapters, size)
    sums = sums.reshape(2, d // 128, 2 * rank, 128).transpose(0, 2, 1, 3).reshape(2, 2 * rank, d)
    return (layer_out, input_grad, sums[0, :rank].T, sums[1, :rank], sums[0, rank:].T, sums[1, rank:])


def solution(mesh):
    spec = P("batch", "seq", None)
    weight = P("batch", None)
    return jax.shard_map(
        functools.partial(local, mesh.shape["batch"], mesh.shape["seq"]),
        mesh=mesh,
        in_specs=(spec, spec, P(), P(), P()) + (weight,) * 6 + (P(),) * 4,
        out_specs=(spec, spec, P(), P(), P(), P()),
        check_vma=False,
    )
```

```python
import functools
import math

import jax
import jax.numpy as jnp
from jax import lax
from jax.experimental import pallas as pl
from jax.experimental.pallas import tpu as pltpu
from jax.sharding import PartitionSpec as P


EPSILON = 1e-05
ADAPTER_SCALE = 8.0
SCORE_SCALE = 0.125
NEG_FILL = -1e30
GELU_C = 0.7978845608028654
LOG2E = math.log2(math.e)
F32 = jnp.float32
BF = jnp.bfloat16
NN = (((1,), (0,)), ((), ()))
NT = (((1,), (1,)), ((), ()))
TN = (((0,), (0,)), ((), ()))


def dot(a, b, dims=NN):
    return lax.dot_general(a, b, dims, preferred_element_type=F32)


def normalise(x):
    mean = jnp.mean(x, axis=-1, keepdims=True)
    centred = x - mean
    inv = lax.rsqrt(jnp.mean(centred * centred, axis=-1, keepdims=True) + EPSILON)
    return centred * inv, inv


def norm_back(xh, inv, gain, up):
    t = up * gain
    return inv * (t - jnp.mean(t, axis=-1, keepdims=True) - xh * jnp.mean(t * xh, axis=-1, keepdims=True))


def gelu_parts(u):
    cubic = 0.044715 * u * u
    th = jnp.tanh(GELU_C * (u + cubic * u))
    half = 0.5 * (1.0 + th)
    return half * u, half + (0.5 * GELU_C) * u * (1.0 - th * th) * (1.0 + 3.0 * cubic)


MESH = pl.DeviceIdType.MESH


def flip(i, bits, width=5):
    out = 0
    for n in range(width):
        bit = 1 << n
        out = out + ((i // bit) % 2 + (bits // bit) % 2) % 2 * bit
    return out


def trade(b, s):
    return b - b % 2 + s % 2, s - s % 2 + b % 2


class Place:
    def __init__(self, nb, ns):
        self.nb, self.ns = nb, ns
        self.b, self.s = lax.axis_index("batch"), lax.axis_index("seq")
        self.lines = nb // 4
        self.line = self.b // 4
        self.partner = trade(self.b, self.s)
        self.stays = self.b % 2 == self.s % 2
        self.doc, self.part = trade(self.b, self.s)

    def peer(self, r):
        return trade(self.doc, flip(self.part, r))

    def hello(self, ways):
        bar = pltpu.get_barrier_semaphore()
        for device, cond in ways:
            def signal(device=device):
                pl.semaphore_signal(bar, inc=1, device_id=device, device_id_type=MESH)
            signal() if cond is None else pl.when(cond)(signal)

    def met(self, ways):
        count = 0
        for _, cond in ways:
            count = count + (1 if cond is None else jnp.where(cond, 1, 0))
        pl.semaphore_wait(pltpu.get_barrier_semaphore(), count)

    def greet(self, ways):
        self.hello(ways)
        self.met(ways)

    def gather_ways(self):
        b, s = self.b, self.s
        return [((b + 4, s), self.line + 1 < self.lines), ((b - 4, s), self.line > 0),
                ((flip(b, 2), s), None), ((flip(b, 1), s), None)]


class Gather:
    def __init__(self, place, own, full, send, recv):
        self.p, self.own, self.full, self.send, self.recv = place, own, full, send, recv

    def part(self, line, pair=0, core=0):
        b = self.p.b
        return line * 4 + (b // 2 + pair) % 2 * 2 + (b + core) % 2

    def copy(self, i, way, src=None):
        p = self.p
        to = [p.b + 4, p.b - 4, self.part(p.line, 1), self.part(p.line, 0, 1)][way]
        return pltpu.make_async_remote_copy(
            src_ref=self.full.at[i] if src is None else src, dst_ref=self.full.at[i],
            send_sem=self.send.at[way, i], recv_sem=self.recv.at[i],
            device_id=(to, p.s), device_id_type=MESH)

    def mine(self):
        return pltpu.make_async_copy(self.own, self.full.at[self.p.b], self.recv.at[self.p.b])

    def start(self):
        p = self.p
        pl.when(p.line + 1 < p.lines)(lambda: self.copy(p.b, 0, self.own).start())
        pl.when(p.line > 0)(lambda: self.copy(p.b, 1, self.own).start())
        self.hand_pair(p.line, self.own)
        self.copy(p.b, 3, self.own).start()
        self.mine().start()

    def hand_pair(self, line, src=None):
        self.copy(self.part(line), 2, src).start()

    def pair_sent(self, line):
        self.copy(self.part(line), 2).wait_send()

    def hop(self, k, pairs=True):
        p = self.p

        def take(way, line):
            i = self.part(line)
            self.copy(i, way).wait_recv()
            more = p.line + 1 < p.lines if way == 0 else p.line > 0
            pl.when(more)(lambda: self.copy(i, way).start())
            if pairs:
                self.hand_pair(line)
            self.copy(i, 3).start()

        below, above = p.line - k, p.line + k
        pl.when(below >= 0)(lambda: take(0, below))
        pl.when(above < p.lines)(lambda: take(1, above))

    def relay_line(self, line):
        i = self.part(line, 1)
        self.copy(i, 2).wait_recv()
        self.copy(i, 3).start()

    def relay(self, k):
        p = self.p
        if k == 0:
            self.relay_line(p.line)
        else:
            pl.when(p.line >= k)(lambda: self.relay_line(p.line - k))
            pl.when(p.line + k < p.lines)(lambda: self.relay_line(p.line + k))

    def from_core(self, line, pair):
        self.copy(self.part(line, pair, 1), 3).wait_recv()

    def finish(self):
        self.mine().wait()
        for line in range(self.p.lines):
            for pair in range(2):
                self.from_core(line, pair)

    def drain(self):
        p = self.p
        for line in range(p.lines):
            i = self.part(line)
            pl.when((p.line >= line) & (p.line + 1 < p.lines))(lambda i=i: self.copy(i, 0).wait_send())
            pl.when((p.line <= line) & (p.line > 0))(lambda i=i: self.copy(i, 1).wait_send())
            self.pair_sent(line)
            self.copy(i, 3).wait_send()
            self.copy(self.part(line, 1), 3).wait_send()

    def steps(self):
        out = [self.start]
        for k in range(1, self.p.lines):
            out.append(functools.partial(run, [functools.partial(self.hop, k), functools.partial(self.relay, k - 1)]))
        out.append(functools.partial(self.relay, self.p.lines - 1))
        out.append(self.finish)
        return out


class PlaneGather(Gather):
    def __init__(self, place, own, full, send, recv):
        super().__init__(place, own, full, send, recv)
        self.lacks = flip(place.line, 1 + place.s % 2)
        self.gives = flip(place.line, 2 - place.s % 2)

    def to_plane(self, i):
        p = self.p
        return pltpu.make_async_remote_copy(
            src_ref=self.full.at[i], dst_ref=self.full.at[i], send_sem=self.send.at[4, i], recv_sem=self.recv.at[i],
            device_id=(p.b, flip(p.s, 1)), device_id_type=MESH)

    def hand_pair(self, line, src=None):
        pl.when(line != self.lacks)(lambda: super(PlaneGather, self).hand_pair(line, src))

    def pair_sent(self, line):
        pl.when(line != self.lacks)(lambda: super(PlaneGather, self).pair_sent(line))

    def relay_line(self, line):
        @pl.when(line != self.lacks)
        def _():
            i = self.part(line, 1)
            self.copy(i, 2).wait_recv()
            pl.when(line == self.gives)(lambda: self.to_plane(i).start())
            self.copy(i, 3).start()

    def cross(self):
        i = self.part(self.lacks, 1)
        self.to_plane(i).wait_recv()
        self.copy(i, 3).start()

    def drain(self):
        super().drain()
        self.to_plane(self.part(self.gives, 1)).wait_send()

    def steps(self):
        out = super().steps()
        return out[:-1] + [self.cross] + out[-1:]


def run(calls):
    for call in calls:
        call()


def chosen(blocks, tests):
    out = blocks[0]
    for block, test in zip(blocks[1:], tests[1:]):
        out = jnp.where(test, block, out)
    return out


def picked(ref, layout, blocks, size):
    per = ref.shape[2] // size
    stored = [ref[t // per, 0, (t % per) * size:(t % per + 1) * size, :] for t in range(blocks)]
    return jnp.concatenate([chosen(stored, [layout[t] == p for t in range(blocks)]) for p in range(blocks)], axis=0)


def put_back(value, layout, blocks, size, store):
    pieces = [value[p * size:(p + 1) * size] for p in range(blocks)]
    for t in range(blocks):
        store(t, chosen(pieces, [layout[t] == p for p in range(blocks)]))


def attend(layout, qkv, out, lse_ref, doc, pair, size, tile):
    parts, rows = qkv.shape[1], qkv.shape[3]
    n = parts * rows
    blocks, per = n // size, rows // size
    lanes = pl.ds(pl.multiple_of(pair * 128, 128), 128)

    def in_order(t):
        stored = [qkv[t, b // per, doc, b % per * size:(b % per + 1) * size, lanes] for b in range(blocks)]
        return jnp.concatenate([chosen(stored, [layout[b] == p for b in range(blocks)]) for p in range(blocks)], axis=0)

    q, k, v = in_order(0), in_order(1), in_order(2)
    vt = v.T
    ones = jnp.ones((16, n), BF)
    vts = [jnp.concatenate([vt[64 * h:64 * h + 64], ones], axis=0) for h in range(2)]
    lane = lax.broadcasted_iota(jnp.int32, (1, 128), 1)
    c = SCORE_SCALE * LOG2E
    tri = lax.broadcasted_iota(jnp.int32, (tile, tile), 0) <= lax.broadcasted_iota(jnp.int32, (tile, tile), 1)
    work = [(i, h) for i in range(n // tile) for h in range(2)]
    lses = [[], []]
    mixed = {}
    waiting = []

    def scores(i, h):
        qm = jnp.where((lane < 64) == (h == 0), q[i * tile:(i + 1) * tile], jnp.zeros((), BF))
        return dot(k[:(i + 1) * tile], qm, NT)

    def settle():
        i, h, e, m = waiting.pop(0)
        o = dot(vts[h][:, :(i + 1) * tile], e)
        l = o[64:65]
        mixed[i, h] = o[:64] * (1.0 / l)
        lses[h].append(m + jnp.log2(l))

    ahead = [scores(*work[0]), scores(*work[1])]
    for t, (i, h) in enumerate(work):
        st = ahead.pop(0)
        if t + 2 < len(work):
            ahead.append(scores(*work[t + 2]))
        diag = jnp.where(tri, st[i * tile:], NEG_FILL)
        st = diag if i == 0 else jnp.concatenate([st[: i * tile], diag], axis=0)
        m = jnp.max(st, axis=0, keepdims=True) * c
        waiting.append((i, h, jnp.exp2(st * c - m).astype(BF), m))
        if t:
            settle()
    settle()
    outs = [jnp.concatenate([mixed[i, 0], mixed[i, 1]], axis=0).T.astype(BF) for i in range(n // tile)]

    def store(b, piece):
        out[b // per, doc, b % per * size:(b % per + 1) * size, lanes] = piece

    put_back(jnp.concatenate(outs, axis=0), layout, blocks, size, store)
    for h in range(2):
        lse_ref[doc, pair, h:h + 1, :] = jnp.concatenate(lses[h], axis=1)


UP_START = 1
UP_PLACES = (0, 4, 8)


def one_hot(rows, columns, first):
    at = lax.broadcasted_iota(jnp.int32, (rows, columns), 0) + first
    return (at == lax.broadcasted_iota(jnp.int32, (rows, columns), 1)).astype(BF)


def down_maps(qd, vd):
    rank = qd.shape[0]
    return (dot(qd, one_hot(rank, 128, 0), TN) + dot(vd, one_hot(rank, 128, rank), TN)).astype(BF)


def up_map(up, first):
    return (ADAPTER_SCALE * dot(one_hot(up.shape[0], 128, first), up, TN)).astype(BF)


def front_kernel(nb, ns, size, tile, layout, x_hbm, cot_hbm, wq_ref, wk_ref, wv_ref, wo_ref, up_hbm, gain_ref, qd_ref, qu_ref, vd_ref, vu_ref,
                 qkv_out, att_out, mixed_out, lse_ref, low_out, x_out, cot_out, wq_out, wk_out, wv_out, wo_out, up_out,
                 xs, n1s, stage, qkv, att, lows, ws, own, down_ref, ups_ref, send, recv, usend, urecv, xsend, xrecv, csend, crecv,
                 osend, orecv, asend, arecv, local_sem, qkv_sem, att_sem):
    docs, rows, d = x_hbm.shape
    w = d // ns
    pairs = w // 128
    p = Place(nb, ns)
    fetch = pltpu.make_async_copy(up_hbm, own, local_sem.at[docs + 5])
    fetch.start()
    p.greet(p.gather_ways() + [((p.b, flip(p.s, 1)), None), (p.partner, jnp.logical_not(p.stays))]
            + [(p.peer(r), None) for r in range(1, ns)])

    def x_remote(i):
        return pltpu.make_async_remote_copy(
            src_ref=x_hbm.at[i], dst_ref=xs.at[i], send_sem=xsend.at[i], recv_sem=xrecv.at[i],
            device_id=p.partner, device_id_type=MESH)

    def cot_remote(i):
        return pltpu.make_async_remote_copy(
            src_ref=cot_hbm.at[i], dst_ref=cot_out.at[i], send_sem=csend.at[i], recv_sem=crecv.at[i],
            device_id=p.partner, device_id_type=MESH)

    def x_local(i):
        return pltpu.make_async_copy(x_hbm.at[i], xs.at[i], xrecv.at[i])

    def x_keep(i):
        return pltpu.make_async_copy(xs.at[i], x_out.at[i], local_sem.at[i])

    for i in range(docs):
        pl.when(p.stays)(lambda i=i: x_local(i).start())
        pl.when(jnp.logical_not(p.stays))(lambda i=i: x_remote(i).start())
    for i in range(docs):
        pl.when(jnp.logical_not(p.stays))(lambda i=i: cot_remote(i).start())

    def first(i):
        pl.when(p.stays)(lambda: x_local(i).wait())
        pl.when(jnp.logical_not(p.stays))(lambda: x_remote(i).wait())
        x_keep(i).start()
        xh, _ = normalise(xs[i].astype(F32))
        n1 = (xh * gain_ref[...]).astype(BF)
        n1s[i] = n1
        lows[i] = dot(n1, down_ref[...]).astype(BF)

    def away(part, i, r):
        return pltpu.make_async_remote_copy(
            src_ref=stage.at[part, i, flip(p.part, r)], dst_ref=qkv.at[part, p.part, i],
            send_sem=osend.at[part, i, r], recv_sem=orecv.at[part, i, r],
            device_id=p.peer(r), device_id_type=MESH)

    def product(part, i):
        y = dot(n1s[i], ws[part].reshape(d, d)) + dot(lows[i], ups_ref[part])
        y = y.astype(BF)
        for g in range(ns):
            piece = y[:, g * w:(g + 1) * w]

            @pl.when(p.part == g)
            def _():
                qkv[part, p.part, i] = piece

            @pl.when(p.part != g)
            def _():
                stage[part, i, g] = piece
        for r in range(1, ns):
            away(part, i, r).start()

    gathers = [Gather(p, own_ref, ws.at[n], send.at[n], recv.at[n])
               for n, own_ref in enumerate((wq_ref, wk_ref, wv_ref, wo_ref))]
    keeps = [pltpu.make_async_copy(ws.at[n], out, local_sem.at[docs + n])
             for n, out in enumerate((wq_out, wk_out, wv_out, wo_out))]
    low_keep = pltpu.make_async_copy(lows, low_out, local_sem.at[docs + 4])
    up_gather = PlaneGather(p, own, up_out, usend, urecv)
    up_steps = up_gather.steps()

    lists = [g.steps() for g in gathers]
    delays = (0, 0, 2, 4)
    ready = [len(lists[0]) - 1 + delay for delay in delays]

    def slot(t):
        for n, steps in enumerate(lists):
            if 0 <= t - delays[n] < len(steps):
                steps[t - delays[n]]()
            if t == ready[n]:
                keeps[n].start()
        if t == UP_START + ready[0]:
            fetch.wait()
            up_steps[0]()

    slot(0)
    rank = qu_ref.shape[0]
    down_ref[...] = down_maps(qd_ref[...], vd_ref[...])
    ups_ref[0] = up_map(qu_ref[...], 0)
    ups_ref[1] = jnp.zeros((128, d), BF)
    ups_ref[2] = up_map(vu_ref[...], rank)
    for t in range(1, ready[0] + 1):
        slot(t)
    places = {2 * docs - 5 + 2 * n: t for n, t in enumerate(range(ready[0] + 1, ready[3] + 1))}

    def one_product(n, carry):
        early = n < 2 * docs
        part = jnp.where(early, n % 2, 2)
        i = jnp.where(early, n // 2, n - 2 * docs)
        pl.when(early & (part == 0))(lambda: first(i))
        product(part, i)
        for at, t in places.items():
            pl.when(n == at)(functools.partial(slot, t))
        return carry

    lax.fori_loop(0, 3 * docs, one_product, 0)
    low_keep.start()

    def qkv_keep(i):
        return pltpu.make_async_copy(qkv.at[:, :, i], qkv_out.at[:, :, i], qkv_sem.at[i])

    def att_keep(i):
        return pltpu.make_async_copy(att.at[:, i], att_out.at[:, i], att_sem.at[i, 0])

    def att_home(i):
        return pltpu.make_async_copy(att.at[p.part, i], mixed_out.at[p.part, i], att_sem.at[i, 1])

    def att_away(i, r):
        return pltpu.make_async_remote_copy(
            src_ref=att.at[flip(p.part, r), i], dst_ref=mixed_out.at[p.part, i], send_sem=asend.at[i, r],
            recv_sem=arecv.at[i, r], device_id=p.peer(r), device_id_type=MESH)

    inside = [n for n in range(1, len(up_steps)) if n <= len(UP_PLACES) and UP_PLACES[n - 1] < docs * pairs]

    def one_pair(m, carry):
        doc, pair = m // pairs, m % pairs
        for n in inside:
            pl.when(m == UP_PLACES[n - 1])(up_steps[n])

        @pl.when(pair == 0)
        def _():
            for part in range(3):
                for r in range(1, ns):
                    away(part, doc, r).wait()
            qkv_keep(doc).start()

        attend(layout, qkv, att, lse_ref, doc, pair, size, tile)

        @pl.when(pair == pairs - 1)
        def _():
            att_keep(doc).start()
            att_home(doc).start()
            for r in range(1, ns):
                att_away(doc, r).start()

        return carry

    lax.fori_loop(0, docs * pairs, one_pair, 0)
    for n in range(1, len(up_steps)):
        if n not in inside:
            up_steps[n]()
    for i in range(docs):
        x_keep(i).wait()
        pl.when(jnp.logical_not(p.stays))(lambda i=i: cot_remote(i).wait())
        qkv_keep(i).wait()
        att_keep(i).wait()
        att_home(i).wait()
        for r in range(1, ns):
            att_away(i, r).wait()
    for keep in keeps:
        keep.wait()
    low_keep.wait()
    for g in gathers + [up_gather]:
        g.drain()


def front(nb, ns, layout, x, cot, wq, wk, wv, wo, up, gain, adapters, size, tile=256):
    docs, rows, d = x.shape
    w = d // ns
    n = rows * ns
    any_spec = pl.BlockSpec(memory_space=pl.ANY)
    vmem = pl.BlockSpec(memory_space=pltpu.VMEM)
    dma = pltpu.SemaphoreType.DMA
    like = lambda *shape: jax.ShapeDtypeStruct(shape, BF)
    heads = (ns, docs, rows, w)
    outs = [like(3, *heads), like(*heads), like(*heads), jax.ShapeDtypeStruct((docs, w // 128, 2, n), F32),
            like(docs, rows, 128), like(*x.shape), like(*x.shape)] + [like(nb, *wq.shape)] * 4 + [like(nb, *up.shape)]
    return pl.pallas_call(
        functools.partial(front_kernel, nb, ns, size, tile),
        in_specs=[pl.BlockSpec(memory_space=pltpu.SMEM)] + [any_spec] * 7 + [vmem] * 5,
        out_specs=[any_spec] * 3 + [vmem] + [any_spec] * 8,
        out_shape=outs,
        scratch_shapes=[pltpu.VMEM(x.shape, BF), pltpu.VMEM(x.shape, BF), pltpu.VMEM((3, docs, ns, rows, w), BF),
                        pltpu.VMEM((3,) + heads, BF), pltpu.VMEM(heads, BF), pltpu.VMEM((docs, rows, 128), BF),
                        pltpu.VMEM((4, nb) + wq.shape, BF), pltpu.VMEM(up.shape, BF),
                        pltpu.VMEM((d, 128), BF), pltpu.VMEM((3, 128, d), BF), dma((4, 4, nb)), dma((4, nb)), dma((5, nb)), dma((nb,)), dma((docs,)), dma((docs,)),
                        dma((docs,)), dma((docs,)), dma((3, docs, ns)), dma((3, docs, ns)), dma((docs, ns)), dma((docs, ns)),
                        dma((docs + 6,)), dma((docs,)), dma((docs, 2))],
        compiler_params=pltpu.CompilerParams(collective_id=0, has_side_effects=True, vmem_limit_bytes=62 << 20),
        name="front",
    )(layout, x, cot, wq, wk, wv, wo, up, gain, *adapters)


def middle_kernel(nb, ns, x_hbm, att_hbm, kept_hbm, cot_hbm, gain_ref, wo_hbm, up_hbm, down_hbm,
                  out_hbm, rg_hbm, mix_hbm,
                  xs, atts, cots, wos, downs, ups, acc, xhs, dn, n2s, invs, us, gs,
                  send, recv, msend, mrecv, load, store):
    docs, rows, d = x_hbm.shape
    w = d // ns
    p = Place(nb, ns)
    held = down_hbm.shape[0]
    chunk = 2 * held
    loads = [pltpu.make_async_copy(wo_hbm, wos, load.at[0]), pltpu.make_async_copy(att_hbm, atts, load.at[3 + docs])]
    for i in range(docs):
        loads.append(pltpu.make_async_copy(x_hbm.at[i], xs.at[i], load.at[1 + i]))
    loads.append(pltpu.make_async_copy(up_hbm, ups, load.at[1 + docs]))
    for copy in loads:
        copy.start()

    def cot_load(source):
        return pltpu.make_async_copy(source, cots, load.at[2 + docs])

    pl.when(p.stays)(lambda: cot_load(kept_hbm).start())
    pl.when(jnp.logical_not(p.stays))(lambda: cot_load(cot_hbm).start())
    p.greet(p.gather_ways() + [(p.peer(r), None) for r in range(1, ns)])

    gather = Gather(p, down_hbm, downs, send, recv)

    gather.start()
    for copy in loads[:-1]:
        copy.wait()
    def rows_of(i):
        return pl.ds(pl.multiple_of(i * rows, rows), rows)

    def second_norm(i, carry):
        at = rows_of(i)
        res = xs[i].astype(F32)
        for g in range(ns):
            res = res + dot(atts[g, i], wos[g * w:(g + 1) * w, :])
        acc[at, :] = res
        xh, inv = normalise(res)
        xhs[at, :] = xh
        invs[at, :] = jnp.broadcast_to(inv, (rows, 128))
        n2s[at, :] = (xh * gain_ref[...]).astype(BF)
        dn[at, :] = jnp.zeros((rows, d), F32)
        return carry

    lax.fori_loop(0, docs, second_norm, 0)
    loads[-1].wait()
    cot_load(cot_hbm).wait()
    gather.mine().wait()
    pair = p.b // 2 % 2

    def weights(f):
        base = flip(p.line, f // 2) * 4 + (pair + f) % 2 * 2
        up = ups[:, :, pl.ds(pl.multiple_of(base * held, chunk), chunk)].reshape(d, chunk)
        return up, downs[pl.ds(base, 2)].reshape(chunk, d)

    def hidden(t):
        up, down = weights(t // docs)
        us[t % 2] = dot(n2s[rows_of(t % docs), :], up)
        gs[t % 2] = dot(cots[t % docs], down, NT)

    def one_tile(t, carry):
        f, i = t // docs, t % docs

        @pl.when(t + 1 < nb // 2 * docs)
        def _():
            after = (t + 1) // docs
            pl.when(i == docs - 1)(lambda: gather.from_core(flip(p.line, after // 2), after % 2))

            @pl.when((i == docs - 1) & (f % 2 == 0))
            def _():
                pl.when(f // 2 + 1 < p.lines)(lambda: gather.hop(f // 2 + 1, pairs=False))
                pl.when(f // 2 + 1 < p.lines)(lambda: gather.hand_pair(flip(p.line, f // 2 + 1)))

            pl.when((i == min(1, docs - 1)) & (f % 2 == 0))(lambda: gather.relay_line(flip(p.line, f // 2)))

        hidden(jnp.minimum(t + 1, nb // 2 * docs - 1))
        up, down = weights(f)
        act, slope = gelu_parts(us[t % 2])
        pg = (slope * gs[t % 2]).astype(BF)
        at = rows_of(i)
        acc[at, :] += dot(act.astype(BF), down)
        dn[at, :] += dot(pg, up, NT)
        return carry

    gather.from_core(p.line, 0)
    hidden(0)
    lax.fori_loop(0, nb // 2 * docs, one_tile, 0)

    def out_and_grad(i, carry):
        at = rows_of(i)
        xs[i] = acc[at, :].astype(BF)
        rg = cots[i].astype(F32) + norm_back(xhs[at, :], invs[at, :1], gain_ref[...], dn[at, :])
        xhs[at, :] = rg
        mix = dot(rg.astype(BF), wos[...], NT).astype(BF)
        for g in range(ns):
            atts[g, i] = mix[:, g * w:(g + 1) * w]
        for copy in results(i):
            copy.start()
        return carry

    def results(i):
        out = [pltpu.make_async_copy(atts.at[p.part, i], mix_hbm.at[p.part, i], store.at[2, i]),
               pltpu.make_async_copy(xs.at[i], out_hbm.at[i], store.at[0, i]),
               pltpu.make_async_copy(xhs.at[rows_of(i)], rg_hbm.at[i], store.at[1, i])]
        for r in range(1, ns):
            out.append(pltpu.make_async_remote_copy(
                src_ref=atts.at[flip(p.part, r), i], dst_ref=mix_hbm.at[p.part, i], send_sem=msend.at[i, r],
                recv_sem=mrecv.at[i, r], device_id=p.peer(r), device_id_type=MESH))
        return out

    lax.fori_loop(0, docs, out_and_grad, 0)
    for i in range(docs):
        for copy in results(i):
            copy.wait()
    gather.drain()


def middle(nb, ns, x, att, kept, cot, gain, wo, up, down):
    docs, rows, d = x.shape
    w = d // ns
    n = docs * rows
    any_spec = pl.BlockSpec(memory_space=pl.ANY)
    vmem = pl.BlockSpec(memory_space=pltpu.VMEM)
    dma = pltpu.SemaphoreType.DMA
    return pl.pallas_call(
        functools.partial(middle_kernel, nb, ns),
        in_specs=[any_spec] * 4 + [vmem] + [any_spec] * 3,
        out_specs=[any_spec] * 3,
        out_shape=[jax.ShapeDtypeStruct((docs, rows, d), BF), jax.ShapeDtypeStruct((docs, rows, d), F32),
                   jax.ShapeDtypeStruct((ns, docs, rows, w), BF)],
        scratch_shapes=[pltpu.VMEM((docs, rows, d), BF), pltpu.VMEM((ns, docs, rows, w), BF),
                        pltpu.VMEM((docs, rows, d), BF), pltpu.VMEM(wo.shape, BF), pltpu.VMEM((nb,) + down.shape, BF),
                        pltpu.VMEM(up.shape, BF), pltpu.VMEM((n, d), F32),
                        pltpu.VMEM((n, d), F32), pltpu.VMEM((n, d), F32), pltpu.VMEM((n, d), BF),
                        pltpu.VMEM((n, 128), F32), pltpu.VMEM((2, rows, 2 * down.shape[0]), F32),
                        pltpu.VMEM((2, rows, 2 * down.shape[0]), F32),
                        dma((4, nb)), dma((nb,)), dma((docs, ns)), dma((docs, ns)), dma((4 + docs,)), dma((3, docs))],
        compiler_params=pltpu.CompilerParams(collective_id=2, has_side_effects=True, vmem_limit_bytes=63 << 20),
        name="feed_forward",
    )(x, att, kept, cot, gain, wo, up, down)


class DeviceSum:
    def __init__(self, p, mine, first, second, total, sends, recvs):
        self.p, self.mine, self.first, self.second, self.total = p, mine, first, second, total
        self.sends, self.recvs = sends, recvs
        self.slot, self.block = p.b % 16, p.b - p.b % 16
        self.many = p.nb // 16 * p.ns
        self.at = (p.b // 16) * p.ns + p.s

    def copy(self, phase, j, src, dst, device):
        return pltpu.make_async_remote_copy(
            src_ref=src, dst_ref=dst, send_sem=self.sends.at[phase, j], recv_sem=self.recvs.at[phase, j],
            device_id=device, device_id_type=MESH)

    def fellow(self, j):
        return (self.block + flip(self.slot, j), self.p.s)

    def scatter(self, j):
        return self.copy(0, j, self.mine.at[flip(self.slot, j)], self.first.at[self.slot], self.fellow(j))

    def share(self, j):
        to, ns = flip(self.at, j), self.p.ns
        return self.copy(1, j, self.second.at[self.at], self.second.at[self.at], ((to // ns) * 16 + self.slot, to % ns))

    def spread(self, j):
        return self.copy(2, j, self.total.at[self.slot], self.total.at[self.slot], self.fellow(j))

    def begin(self):
        for j in range(1, 16):
            self.scatter(j).start()
        self.first[self.slot] = self.mine[self.slot]

    def middle(self):
        for j in range(1, 16):
            self.scatter(j).wait()
        self.second[self.at] = jnp.sum(self.first[...], axis=0)
        for j in range(1, self.many):
            self.share(j).start()

    def end(self):
        for j in range(1, self.many):
            self.share(j).wait()
        self.total[self.slot] = jnp.sum(self.second[...], axis=0)
        for j in range(1, 16):
            self.spread(j).start()

    def finish(self):
        for j in range(1, 16):
            self.spread(j).wait()


def sum_ways(p):
    b, s, nb, ns = p.b, p.s, p.nb, p.ns
    slot, block = b % 16, b - b % 16
    at = (b // 16) * ns + s
    ways = [((block + flip(slot, j), s), None) for j in range(1, 16)]
    for j in range(1, nb // 16 * ns):
        to = flip(at, j)
        ways.append((((to // ns) * 16 + slot, to % ns), None))
    return ways


CUTS = 2


def backward_kernel(nb, ns, rank, size, tile, layout, q_ref, k_ref, v_ref, o_ref, g_ref, lse_ref, top_hbm, x_hbm, gain_ref,
                    rg_hbm, low_hbm, wq_hbm, wk_hbm, wv_hbm, qd_ref, qu_ref, vd_ref, vu_ref, top_out, out_hbm, sum_ref,
                    dqt, stage, xs, rgs, ds, wqs, wks, wvs, lows, outs, gds, gqs, gvs, mine, first, second, summed,
                    tops, xhs, lgs, down_ref, upq_ref, upv_ref,
                    load, dsend, drecv, osend, orecv, tsend, trecv, ssend, srecv):
    docs, rows, d = x_hbm.shape
    w = d // ns
    p = Place(nb, ns)
    doc, pair = pl.program_id(0), pl.program_id(1)
    pairs = w // 128
    loads = [pltpu.make_async_copy(a, v, load.at[n]) for n, (a, v) in enumerate(
        ((wq_hbm, wqs), (wk_hbm, wks), (wv_hbm, wvs), (low_hbm, lows), (x_hbm, xs), (rg_hbm, rgs)))]

    def away(t, i, r, n):
        at = pl.ds(pl.multiple_of(n * 128, 128), 128)
        return pltpu.make_async_remote_copy(
            src_ref=stage.at[i, t, flip(p.part, r), :, at], dst_ref=ds.at[t, p.part, i, :, at], send_sem=dsend.at[t, i, r, n],
            recv_sem=drecv.at[t, i, r, n], device_id=p.peer(r), device_id_type=MESH)

    cut = rows // CUTS

    def out_away(i, n):
        at = pl.ds(pl.multiple_of(n * cut, cut), cut)
        return pltpu.make_async_remote_copy(
            src_ref=outs.at[i, at], dst_ref=out_hbm.at[i, at], send_sem=osend.at[i, n], recv_sem=orecv.at[i, n],
            device_id=p.partner, device_id_type=MESH)

    def out_home(i, n):
        at = pl.ds(pl.multiple_of(n * cut, cut), cut)
        return pltpu.make_async_copy(outs.at[i, at], out_hbm.at[i, at], orecv.at[i, n])

    def top_away(i):
        return pltpu.make_async_remote_copy(
            src_ref=top_hbm.at[i], dst_ref=top_out.at[i], send_sem=tsend.at[i], recv_sem=trecv.at[i],
            device_id=p.partner, device_id_type=MESH)

    top_in = pltpu.make_async_copy(top_hbm, tops, tsend.at[0])
    top_home = pltpu.make_async_copy(tops, top_out, trecv.at[0])
    ways = [(p.peer(r), None) for r in range(1, ns)] + [(p.partner, jnp.logical_not(p.stays))] + sum_ways(p)
    total = DeviceSum(p, mine, first, second, summed, ssend, srecv)

    @pl.when((doc == 0) & (pair == 0))
    def _():
        p.hello(ways)
        for copy in loads:
            copy.start()
        pl.when(p.stays)(lambda: top_in.start())
        down_ref[...] = down_maps(qd_ref[...], vd_ref[...])
        upq_ref[...] = up_map(qu_ref[...], 0)
        upv_ref[...] = up_map(vu_ref[...], rank)
        gds[...] = jnp.zeros_like(gds)
        gqs[...] = jnp.zeros_like(gqs)
        gvs[...] = jnp.zeros_like(gvs)

    @pl.when(doc < docs)
    def _():
        attention_gradients(layout, q_ref, k_ref, v_ref, o_ref, g_ref, lse_ref, stage, dqt, doc, pair, size, tile)

        @pl.when((doc == 0) & (pair == 0))
        def _():
            p.met(ways)
            pl.when(p.stays)(lambda: top_in.wait())
            pl.when(p.stays)(lambda: top_home.start())
            for i in range(docs):
                pl.when(jnp.logical_not(p.stays))(lambda i=i: top_away(i).start())

        for t in range(3):
            for r in range(1, ns):
                away(t, doc, r, pair).start()

    @pl.when((doc > 0) & (pair == 0))
    def _():
        i = doc - 1

        @pl.when(i == 0)
        def _():
            for copy in loads:
                copy.wait()

        for t in range(3):
            for r in range(1, ns):
                for n in range(pairs):
                    away(t, i, r, n).wait()

        xh, inv = normalise(xs[i].astype(F32))
        xhs[:, :d] = xh
        xhs[:, d:] = jnp.broadcast_to(inv, (rows, 128))
        lg = jnp.zeros((rows, 128), F32)
        for r in range(ns):
            g = flip(p.part, r)
            cols = pl.ds(pl.multiple_of(g * w, w), w)
            for t, up, grads in ((0, upq_ref, gqs), (2, upv_ref, gvs)):
                piece = ds[t, g, i] if r else stage[i, t, p.part]
                lg = lg + dot(piece, up[:, cols], NT)
                grads[:, cols] += dot(lows[i], piece, TN)
        lgs[...] = lg.astype(BF)
        gds[...] += dot(lgs[...], (xh * gain_ref[...]).astype(BF), TN)

        @pl.when(i == docs - 1)
        def _():
            upper = lax.broadcasted_iota(jnp.int32, (2 * rank, 1), 0) < rank
            both = jnp.where(upper, gqs[:2 * rank, :], gvs[:2 * rank, :]) * ADAPTER_SCALE
            for n in range(8):
                mine[n] = gds[:8, n * 128:(n + 1) * 128]
                mine[8 + n] = both[:, n * 128:(n + 1) * 128]
            total.begin()

        def some_rows(n, carry):
            at = pl.ds(pl.multiple_of(n * cut, cut), cut)
            fg = dot(lgs[at, :], down_ref[...], NT)
            for r in range(ns):
                g = flip(p.part, r)
                cols = pl.ds(pl.multiple_of(g * w, w), w)
                for t, full in enumerate((wqs, wks, wvs)):
                    piece = ds[t, g, i, at, :] if r else stage[i, t, p.part, at, :]
                    fg = fg + dot(piece, full[:, :, cols].reshape(d, w), NT)
            outs[i, at, :] = (rgs[i, at, :] + norm_back(xhs[at, :d], xhs[at, d:d + 1], gain_ref[...], fg)).astype(BF)
            pl.when(p.stays)(lambda: out_home(i, n).start())
            pl.when(jnp.logical_not(p.stays))(lambda: out_away(i, n).start())
            pl.when((i == docs - 1) & (n == 0))(total.middle)
            return carry

        lax.fori_loop(0, CUTS, some_rows, 0)
        pl.when(i == docs - 1)(total.end)

    @pl.when((doc == docs) & (pair == pairs - 1))
    def _():
        total.finish()
        sum_ref[...] = summed[...]
        pl.when(p.stays)(lambda: top_home.wait())
        for i in range(docs):
            for n in range(CUTS):
                pl.when(p.stays)(lambda i=i, n=n: out_home(i, n).wait())
                pl.when(jnp.logical_not(p.stays))(lambda i=i, n=n: out_away(i, n).wait())
            pl.when(jnp.logical_not(p.stays))(lambda i=i: top_away(i).wait())


def attention_gradients(layout, q_ref, k_ref, v_ref, o_ref, g_ref, lse_ref, stage, dqt, doc, pair, size, tile):
    parts, rows = o_ref.shape[0], o_ref.shape[2]
    n = parts * rows
    blocks, per = n // size, rows // size
    q = picked(q_ref.at[0], layout, blocks, size)
    k = picked(k_ref.at[0], layout, blocks, size)
    v = picked(v_ref.at[0], layout, blocks, size)
    o = picked(o_ref, layout, blocks, size)
    g = picked(g_ref, layout, blocks, size)
    kt = k.T
    lane = lax.broadcasted_iota(jnp.int32, (1, 128), 1)
    c = SCORE_SCALE * LOG2E
    tri = lax.broadcasted_iota(jnp.int32, (tile, tile), 0) <= lax.broadcasted_iota(jnp.int32, (tile, tile), 1)
    prod = (o.astype(F32) * g.astype(F32)).astype(BF)
    heads = (lax.broadcasted_iota(jnp.int32, (8, 128), 1) // 64 == lax.broadcasted_iota(jnp.int32, (8, 128), 0)).astype(BF)
    delta = dot(heads, prod, NT)
    zero = jnp.zeros((), BF)
    masks = [(lane < 64) == (h == 0) for h in range(2)]
    qms = [jnp.where(mk, q, zero) for mk in masks]
    gms = [jnp.where(mk, g, zero) for mk in masks]
    lse = lse_ref[0, 0]
    dks, dvs = [], []
    work = [(j, h) for j in range(n // tile) for h in range(2)]

    def products(j, h):
        lo, hi = j * tile, (j + 1) * tile
        return dot(k[lo:hi], qms[h][lo:], NT), dot(v[lo:hi], gms[h][lo:], NT)

    waiting = []
    sums = {}

    def settle():
        j, h, p, ds = waiting.pop(0)
        lo, hi = j * tile, (j + 1) * tile
        dv = dot(p, gms[h][lo:])
        dk = dot(ds, qms[h][lo:])
        dq = dot(kt[64 * h:64 * h + 64, lo:hi], ds)
        if j == 0:
            dqt[64 * h:64 * h + 64, :] = dq
        else:
            dqt[64 * h:64 * h + 64, lo:] += dq
        if h == 0:
            sums[j] = dk, dv
        else:
            dks.append(((sums[j][0] + dk) * SCORE_SCALE).astype(BF))
            dvs.append((sums[j][1] + dv).astype(BF))

    ahead = products(*work[0])
    for t, (j, h) in enumerate(work):
        st, dp = ahead
        if t + 1 < len(work):
            ahead = products(*work[t + 1])
        lo, hi = j * tile, (j + 1) * tile
        p = jnp.exp2(st * c - lse[h:h + 1, lo:])
        diag = jnp.where(tri, p[:, :tile], 0.0)
        p = diag if hi == n else jnp.concatenate([diag, p[:, tile:]], axis=1)
        waiting.append((j, h, p.astype(BF), (p * (dp - delta[h:h + 1, lo:])).astype(BF)))
        if t:
            settle()
    settle()
    lanes = pl.ds(pl.multiple_of(pair * 128, 128), 128)
    for t, value in enumerate(((dqt[...] * SCORE_SCALE).T.astype(BF), jnp.concatenate(dks, axis=0),
                               jnp.concatenate(dvs, axis=0))):
        def store(b, piece, t=t):
            stage[doc, t, b // per, b % per * size:(b % per + 1) * size, lanes] = piece
        put_back(value, layout, blocks, size, store)


def backward(nb, ns, rank, layout, qkv, o, g, lse, top, x, gain, rg, low, wq, wk, wv, adapters, size, tile=256):
    docs, rows, d = x.shape
    parts = o.shape[0]
    w = d // ns
    n = parts * rows
    any_spec = pl.BlockSpec(memory_space=pl.ANY)
    vmem = pl.BlockSpec(memory_space=pltpu.VMEM)
    dma = pltpu.SemaphoreType.DMA
    many = max(16, nb // 16 * ns)
    spec = pl.BlockSpec((parts, 1, rows, 128), lambda i, j: (0, jnp.minimum(i, docs - 1), 0, j))
    row = jax.ShapeDtypeStruct(x.shape, BF)

    def third(t):
        return pl.BlockSpec((1, parts, 1, rows, 128), lambda i, j: (t, 0, jnp.minimum(i, docs - 1), 0, j))

    return pl.pallas_call(
        functools.partial(backward_kernel, nb, ns, rank, size, tile),
        grid=(docs + 1, w // 128),
        in_specs=[pl.BlockSpec(memory_space=pltpu.SMEM), third(0), third(1), third(2), spec, spec]
        + [pl.BlockSpec((1, 1, 2, n), lambda i, j: (jnp.minimum(i, docs - 1), j, 0, 0))]
        + [any_spec] * 2 + [vmem] + [any_spec] * 5 + [vmem] * 4,
        out_specs=[any_spec, any_spec, vmem],
        out_shape=[row, row, jax.ShapeDtypeStruct((16, 8, 128), F32)],
        scratch_shapes=[pltpu.VMEM((128, n), F32), pltpu.VMEM((docs, 3, parts, rows, w), BF),
                        pltpu.VMEM(x.shape, BF), pltpu.VMEM(x.shape, F32), pltpu.VMEM((3, ns, docs, rows, w), BF)]
        + [pltpu.VMEM(wq.shape, BF)] * 3
        + [pltpu.VMEM(low.shape, BF), pltpu.VMEM(x.shape, BF)] + [pltpu.VMEM((128, d), F32)] * 3
        + [pltpu.VMEM((16, 8, 128), F32), pltpu.VMEM((16, 8, 128), F32), pltpu.VMEM((nb // 16 * ns, 8, 128), F32),
           pltpu.VMEM((16, 8, 128), F32),
           pltpu.VMEM(x.shape, BF), pltpu.VMEM((rows, d + 128), F32), pltpu.VMEM((rows, 128), BF),
           pltpu.VMEM((d, 128), BF), pltpu.VMEM((128, d), BF), pltpu.VMEM((128, d), BF),
           dma((6,)), dma((3, docs, ns, w // 128)), dma((3, docs, ns, w // 128)), dma((docs, CUTS)), dma((docs, CUTS)), dma((docs,)), dma((docs,)),
           dma((3, many)), dma((3, many))],
        compiler_params=pltpu.CompilerParams(collective_id=3, has_side_effects=True, vmem_limit_bytes=62 << 20),
        name="backward",
    )(layout, qkv, qkv, qkv, o, g, lse, top, x, gain, rg, low, wq, wk, wv, *adapters)


def local(
    nb, ns,
    tokens, cotangent, layout, attention_norm_gain, feedforward_norm_gain,
    query_weight, key_weight, value_weight, attention_output_weight, up_weight, down_weight,
    query_down_adapter, query_up_adapter, value_down_adapter, value_up_adapter,
):
    docs, rows, d = tokens.shape
    size = rows * ns // layout.shape[0]
    rank = query_up_adapter.shape[0]
    adapters = (query_down_adapter.T, query_up_adapter, value_down_adapter.T, value_up_adapter)
    gain1 = attention_norm_gain[None]
    gain2 = feedforward_norm_gain[None]

    qkv, att, mixed, lse, low, x, cot, wq, wk, wv, wo, w_up = front(
        nb, ns, layout, tokens, cotangent, query_weight, key_weight, value_weight, attention_output_weight, up_weight,
        gain1, adapters, size)
    out, rg, mix = middle(nb, ns, x, mixed, cotangent, cot, gain2, wo.reshape(d, d), w_up, down_weight)
    layer_out, input_grad, sums = backward(
        nb, ns, rank, layout, qkv, att, mix, lse, out, x, gain1, rg, low, wq, wk, wv, adapters, size)
    sums = sums.reshape(2, d // 128, 2 * rank, 128).transpose(0, 2, 1, 3).reshape(2, 2 * rank, d)
    return (layer_out, input_grad, sums[0, :rank].T, sums[1, :rank], sums[0, rank:].T, sums[1, rank:])


def solution(mesh):
    spec = P("batch", "seq", None)
    weight = P("batch", None)
    return jax.shard_map(
        functools.partial(local, mesh.shape["batch"], mesh.shape["seq"]),
        mesh=mesh,
        in_specs=(spec, spec, P(), P(), P()) + (weight,) * 6 + (P(),) * 4,
        out_specs=(spec, spec, P(), P(), P(), P()),
        check_vma=False,
    )
```

```python
import functools
import math

import jax
import jax.numpy as jnp
from jax import lax
from jax.experimental import pallas as pl
from jax.experimental.pallas import tpu as pltpu
from jax.sharding import PartitionSpec as P


EPSILON = 1e-05
ADAPTER_SCALE = 8.0
SCORE_SCALE = 0.125
NEG_FILL = -1e30
GELU_C = 0.7978845608028654
LOG2E = math.log2(math.e)
F32 = jnp.float32
BF = jnp.bfloat16
NN = (((1,), (0,)), ((), ()))
NT = (((1,), (1,)), ((), ()))
TN = (((0,), (0,)), ((), ()))


def dot(a, b, dims=NN):
    return lax.dot_general(a, b, dims, preferred_element_type=F32)


def normalise(x):
    mean = jnp.mean(x, axis=-1, keepdims=True)
    centred = x - mean
    inv = lax.rsqrt(jnp.mean(centred * centred, axis=-1, keepdims=True) + EPSILON)
    return centred * inv, inv


def norm_back(xh, inv, gain, up):
    t = up * gain
    return inv * (t - jnp.mean(t, axis=-1, keepdims=True) - xh * jnp.mean(t * xh, axis=-1, keepdims=True))


def gelu_parts(u):
    cubic = 0.044715 * u * u
    th = jnp.tanh(GELU_C * (u + cubic * u))
    half = 0.5 * (1.0 + th)
    return half * u, half + (0.5 * GELU_C) * u * (1.0 - th * th) * (1.0 + 3.0 * cubic)


MESH = pl.DeviceIdType.MESH


def flip(i, bits, width=5):
    out = 0
    for n in range(width):
        bit = 1 << n
        out = out + ((i // bit) % 2 + (bits // bit) % 2) % 2 * bit
    return out


def trade(b, s):
    return b - b % 2 + s % 2, s - s % 2 + b % 2


class Place:
    def __init__(self, nb, ns):
        self.nb, self.ns = nb, ns
        self.b, self.s = lax.axis_index("batch"), lax.axis_index("seq")
        self.lines = nb // 4
        self.line = self.b // 4
        self.partner = trade(self.b, self.s)
        self.stays = self.b % 2 == self.s % 2
        self.doc, self.part = trade(self.b, self.s)

    def peer(self, r):
        return trade(self.doc, flip(self.part, r))

    def hello(self, ways):
        bar = pltpu.get_barrier_semaphore()
        for device, cond in ways:
            def signal(device=device):
                pl.semaphore_signal(bar, inc=1, device_id=device, device_id_type=MESH)
            signal() if cond is None else pl.when(cond)(signal)

    def met(self, ways):
        count = 0
        for _, cond in ways:
            count = count + (1 if cond is None else jnp.where(cond, 1, 0))
        pl.semaphore_wait(pltpu.get_barrier_semaphore(), count)

    def greet(self, ways):
        self.hello(ways)
        self.met(ways)

    def gather_ways(self):
        b, s = self.b, self.s
        return [((b + 4, s), self.line + 1 < self.lines), ((b - 4, s), self.line > 0),
                ((flip(b, 2), s), None), ((flip(b, 1), s), None)]


class Gather:
    def __init__(self, place, own, full, send, recv):
        self.p, self.own, self.full, self.send, self.recv = place, own, full, send, recv

    def part(self, line, pair=0, core=0):
        b = self.p.b
        return line * 4 + (b // 2 + pair) % 2 * 2 + (b + core) % 2

    def copy(self, i, way, src=None):
        p = self.p
        to = [p.b + 4, p.b - 4, self.part(p.line, 1), self.part(p.line, 0, 1)][way]
        return pltpu.make_async_remote_copy(
            src_ref=self.full.at[i] if src is None else src, dst_ref=self.full.at[i],
            send_sem=self.send.at[way, i], recv_sem=self.recv.at[i],
            device_id=(to, p.s), device_id_type=MESH)

    def mine(self):
        return pltpu.make_async_copy(self.own, self.full.at[self.p.b], self.recv.at[self.p.b])

    def start(self):
        p = self.p
        pl.when(p.line + 1 < p.lines)(lambda: self.copy(p.b, 0, self.own).start())
        pl.when(p.line > 0)(lambda: self.copy(p.b, 1, self.own).start())
        self.hand_pair(p.line, self.own)
        self.copy(p.b, 3, self.own).start()
        self.mine().start()

    def hand_pair(self, line, src=None):
        self.copy(self.part(line), 2, src).start()

    def pair_sent(self, line):
        self.copy(self.part(line), 2).wait_send()

    def hop(self, k, pairs=True):
        p = self.p

        def take(way, line):
            i = self.part(line)
            self.copy(i, way).wait_recv()
            more = p.line + 1 < p.lines if way == 0 else p.line > 0
            pl.when(more)(lambda: self.copy(i, way).start())
            if pairs:
                self.hand_pair(line)
            self.copy(i, 3).start()

        below, above = p.line - k, p.line + k
        pl.when(below >= 0)(lambda: take(0, below))
        pl.when(above < p.lines)(lambda: take(1, above))

    def relay_line(self, line):
        i = self.part(line, 1)
        self.copy(i, 2).wait_recv()
        self.copy(i, 3).start()

    def relay(self, k):
        p = self.p
        if k == 0:
            self.relay_line(p.line)
        else:
            pl.when(p.line >= k)(lambda: self.relay_line(p.line - k))
            pl.when(p.line + k < p.lines)(lambda: self.relay_line(p.line + k))

    def from_core(self, line, pair):
        self.copy(self.part(line, pair, 1), 3).wait_recv()

    def finish(self):
        self.mine().wait()
        for line in range(self.p.lines):
            for pair in range(2):
                self.from_core(line, pair)

    def drain(self):
        p = self.p
        for line in range(p.lines):
            i = self.part(line)
            pl.when((p.line >= line) & (p.line + 1 < p.lines))(lambda i=i: self.copy(i, 0).wait_send())
            pl.when((p.line <= line) & (p.line > 0))(lambda i=i: self.copy(i, 1).wait_send())
            self.pair_sent(line)
            self.copy(i, 3).wait_send()
            self.copy(self.part(line, 1), 3).wait_send()

    def steps(self):
        out = [self.start]
        for k in range(1, self.p.lines):
            out.append(functools.partial(run, [functools.partial(self.hop, k), functools.partial(self.relay, k - 1)]))
        out.append(functools.partial(self.relay, self.p.lines - 1))
        out.append(self.finish)
        return out


class PlaneGather(Gather):
    def __init__(self, place, own, full, send, recv):
        super().__init__(place, own, full, send, recv)
        self.lacks = flip(place.line, 1 + place.s % 2)
        self.gives = flip(place.line, 2 - place.s % 2)

    def to_plane(self, i):
        p = self.p
        return pltpu.make_async_remote_copy(
            src_ref=self.full.at[i], dst_ref=self.full.at[i], send_sem=self.send.at[4, i], recv_sem=self.recv.at[i],
            device_id=(p.b, flip(p.s, 1)), device_id_type=MESH)

    def hand_pair(self, line, src=None):
        pl.when(line != self.lacks)(lambda: super(PlaneGather, self).hand_pair(line, src))

    def pair_sent(self, line):
        pl.when(line != self.lacks)(lambda: super(PlaneGather, self).pair_sent(line))

    def relay_line(self, line):
        @pl.when(line != self.lacks)
        def _():
            i = self.part(line, 1)
            self.copy(i, 2).wait_recv()
            pl.when(line == self.gives)(lambda: self.to_plane(i).start())
            self.copy(i, 3).start()

    def cross(self):
        i = self.part(self.lacks, 1)
        self.to_plane(i).wait_recv()
        self.copy(i, 3).start()

    def drain(self):
        super().drain()
        self.to_plane(self.part(self.gives, 1)).wait_send()

    def steps(self):
        out = super().steps()
        return out[:-1] + [self.cross] + out[-1:]


def run(calls):
    for call in calls:
        call()


def chosen(blocks, tests):
    out = blocks[0]
    for block, test in zip(blocks[1:], tests[1:]):
        out = jnp.where(test, block, out)
    return out


def picked(ref, layout, blocks, size):
    per = ref.shape[2] // size
    stored = [ref[t // per, 0, (t % per) * size:(t % per + 1) * size, :] for t in range(blocks)]
    return jnp.concatenate([chosen(stored, [layout[t] == p for t in range(blocks)]) for p in range(blocks)], axis=0)


def put_back(value, layout, blocks, size, store):
    pieces = [value[p * size:(p + 1) * size] for p in range(blocks)]
    for t in range(blocks):
        store(t, chosen(pieces, [layout[t] == p for p in range(blocks)]))


def attend(layout, qkv, out, lse_ref, doc, pair, size, tile):
    parts, rows = qkv.shape[1], qkv.shape[3]
    n = parts * rows
    blocks, per = n // size, rows // size
    lanes = pl.ds(pl.multiple_of(pair * 128, 128), 128)

    def in_order(t):
        stored = [qkv[t, b // per, doc, b % per * size:(b % per + 1) * size, lanes] for b in range(blocks)]
        return jnp.concatenate([chosen(stored, [layout[b] == p for b in range(blocks)]) for p in range(blocks)], axis=0)

    q, k, v = in_order(0), in_order(1), in_order(2)
    vt = v.T
    ones = jnp.ones((16, n), BF)
    vts = [jnp.concatenate([vt[64 * h:64 * h + 64], ones], axis=0) for h in range(2)]
    lane = lax.broadcasted_iota(jnp.int32, (1, 128), 1)
    c = SCORE_SCALE * LOG2E
    tri = lax.broadcasted_iota(jnp.int32, (tile, tile), 0) <= lax.broadcasted_iota(jnp.int32, (tile, tile), 1)
    work = [(i, h) for i in range(n // tile) for h in range(2)]
    lses = [[], []]
    mixed = {}
    waiting = []

    def scores(i, h):
        qm = jnp.where((lane < 64) == (h == 0), q[i * tile:(i + 1) * tile], jnp.zeros((), BF))
        return dot(k[:(i + 1) * tile], qm, NT)

    def settle():
        i, h, e, m = waiting.pop(0)
        o = dot(vts[h][:, :(i + 1) * tile], e)
        l = o[64:65]
        mixed[i, h] = o[:64] * (1.0 / l)
        lses[h].append(m + jnp.log2(l))

    ahead = [scores(*work[0]), scores(*work[1])]
    for t, (i, h) in enumerate(work):
        st = ahead.pop(0)
        if t + 2 < len(work):
            ahead.append(scores(*work[t + 2]))
        diag = jnp.where(tri, st[i * tile:], NEG_FILL)
        st = diag if i == 0 else jnp.concatenate([st[: i * tile], diag], axis=0)
        m = jnp.max(st, axis=0, keepdims=True) * c
        waiting.append((i, h, jnp.exp2(st * c - m).astype(BF), m))
        if t:
            settle()
    settle()
    outs = [jnp.concatenate([mixed[i, 0], mixed[i, 1]], axis=0).T.astype(BF) for i in range(n // tile)]

    def store(b, piece):
        out[b // per, doc, b % per * size:(b % per + 1) * size, lanes] = piece

    put_back(jnp.concatenate(outs, axis=0), layout, blocks, size, store)
    for h in range(2):
        lse_ref[doc, pair, h:h + 1, :] = jnp.concatenate(lses[h], axis=1)


UP_START = 1
UP_PLACES = (0, 4, 8)


def one_hot(rows, columns, first):
    at = lax.broadcasted_iota(jnp.int32, (rows, columns), 0) + first
    return (at == lax.broadcasted_iota(jnp.int32, (rows, columns), 1)).astype(BF)


def down_maps(qd, vd):
    rank = qd.shape[0]
    return (dot(qd, one_hot(rank, 128, 0), TN) + dot(vd, one_hot(rank, 128, rank), TN)).astype(BF)


def up_map(up, first):
    return (ADAPTER_SCALE * dot(one_hot(up.shape[0], 128, first), up, TN)).astype(BF)


def front_kernel(nb, ns, size, tile, layout, x_hbm, cot_hbm, wq_ref, wk_ref, wv_ref, wo_ref, up_hbm, gain_ref, qd_ref, qu_ref, vd_ref, vu_ref,
                 qkv_out, att_out, mixed_out, lse_ref, low_out, x_out, cot_out, wq_out, wk_out, wv_out, wo_out, up_out,
                 xs, n1s, stage, qkv, att, lows, ws, own, down_ref, ups_ref, send, recv, usend, urecv, xsend, xrecv, csend, crecv,
                 osend, orecv, asend, arecv, local_sem, qkv_sem, att_sem):
    docs, rows, d = x_hbm.shape
    w = d // ns
    pairs = w // 128
    p = Place(nb, ns)
    fetch = pltpu.make_async_copy(up_hbm, own, local_sem.at[docs + 5])
    fetch.start()
    p.greet(p.gather_ways() + [((p.b, flip(p.s, 1)), None), (p.partner, jnp.logical_not(p.stays))]
            + [(p.peer(r), None) for r in range(1, ns)])

    def x_remote(i):
        return pltpu.make_async_remote_copy(
            src_ref=x_hbm.at[i], dst_ref=xs.at[i], send_sem=xsend.at[i], recv_sem=xrecv.at[i],
            device_id=p.partner, device_id_type=MESH)

    def cot_remote(i):
        return pltpu.make_async_remote_copy(
            src_ref=cot_hbm.at[i], dst_ref=cot_out.at[i], send_sem=csend.at[i], recv_sem=crecv.at[i],
            device_id=p.partner, device_id_type=MESH)

    def x_local(i):
        return pltpu.make_async_copy(x_hbm.at[i], xs.at[i], xrecv.at[i])

    def x_keep(i):
        return pltpu.make_async_copy(xs.at[i], x_out.at[i], local_sem.at[i])

    for i in range(docs):
        pl.when(p.stays)(lambda i=i: x_local(i).start())
        pl.when(jnp.logical_not(p.stays))(lambda i=i: x_remote(i).start())
    for i in range(docs):
        pl.when(jnp.logical_not(p.stays))(lambda i=i: cot_remote(i).start())

    def first(i):
        pl.when(p.stays)(lambda: x_local(i).wait())
        pl.when(jnp.logical_not(p.stays))(lambda: x_remote(i).wait())
        x_keep(i).start()
        xh, _ = normalise(xs[i].astype(F32))
        n1 = (xh * gain_ref[...]).astype(BF)
        n1s[i] = n1
        lows[i] = dot(n1, down_ref[...]).astype(BF)

    def away(part, i, r):
        return pltpu.make_async_remote_copy(
            src_ref=stage.at[part, i, flip(p.part, r)], dst_ref=qkv.at[part, p.part, i],
            send_sem=osend.at[part, i, r], recv_sem=orecv.at[part, i, r],
            device_id=p.peer(r), device_id_type=MESH)

    def product(part, i):
        y = dot(n1s[i], ws[part].reshape(d, d)) + dot(lows[i], ups_ref[part])
        y = y.astype(BF)
        for g in range(ns):
            piece = y[:, g * w:(g + 1) * w]

            @pl.when(p.part == g)
            def _():
                qkv[part, p.part, i] = piece

            @pl.when(p.part != g)
            def _():
                stage[part, i, g] = piece
        for r in range(1, ns):
            away(part, i, r).start()

    gathers = [Gather(p, own_ref, ws.at[n], send.at[n], recv.at[n])
               for n, own_ref in enumerate((wq_ref, wk_ref, wv_ref, wo_ref))]
    keeps = [pltpu.make_async_copy(ws.at[n], out, local_sem.at[docs + n])
             for n, out in enumerate((wq_out, wk_out, wv_out, wo_out))]
    low_keep = pltpu.make_async_copy(lows, low_out, local_sem.at[docs + 4])
    up_gather = PlaneGather(p, own, up_out, usend, urecv)
    up_steps = up_gather.steps()

    lists = [g.steps() for g in gathers]
    delays = (0, 0, 2, 4)
    ready = [len(lists[0]) - 1 + delay for delay in delays]

    def slot(t):
        for n, steps in enumerate(lists):
            if 0 <= t - delays[n] < len(steps):
                steps[t - delays[n]]()
            if t == ready[n]:
                keeps[n].start()
        if t == UP_START + ready[0]:
            fetch.wait()
            up_steps[0]()

    slot(0)
    rank = qu_ref.shape[0]
    down_ref[...] = down_maps(qd_ref[...], vd_ref[...])
    ups_ref[0] = up_map(qu_ref[...], 0)
    ups_ref[1] = jnp.zeros((128, d), BF)
    ups_ref[2] = up_map(vu_ref[...], rank)
    for t in range(1, ready[0] + 1):
        slot(t)
    places = {2 * docs - 5 + 2 * n: t for n, t in enumerate(range(ready[0] + 1, ready[3] + 1))}

    def one_product(n, carry):
        early = n < 2 * docs
        part = jnp.where(early, n % 2, 2)
        i = jnp.where(early, n // 2, n - 2 * docs)
        pl.when(early & (part == 0))(lambda: first(i))
        product(part, i)
        for at, t in places.items():
            pl.when(n == at)(functools.partial(slot, t))
        return carry

    lax.fori_loop(0, 3 * docs, one_product, 0)
    low_keep.start()

    def qkv_keep(i):
        return pltpu.make_async_copy(qkv.at[:, :, i], qkv_out.at[:, :, i], qkv_sem.at[i])

    def att_keep(i):
        return pltpu.make_async_copy(att.at[:, i], att_out.at[:, i], att_sem.at[i, 0])

    def att_home(i):
        return pltpu.make_async_copy(att.at[p.part, i], mixed_out.at[p.part, i], att_sem.at[i, 1])

    def att_away(i, r):
        return pltpu.make_async_remote_copy(
            src_ref=att.at[flip(p.part, r), i], dst_ref=mixed_out.at[p.part, i], send_sem=asend.at[i, r],
            recv_sem=arecv.at[i, r], device_id=p.peer(r), device_id_type=MESH)

    inside = [n for n in range(1, len(up_steps)) if n <= len(UP_PLACES) and UP_PLACES[n - 1] < docs * pairs]

    def one_pair(m, carry):
        doc, pair = m // pairs, m % pairs
        for n in inside:
            pl.when(m == UP_PLACES[n - 1])(up_steps[n])

        @pl.when(pair == 0)
        def _():
            for part in range(3):
                for r in range(1, ns):
                    away(part, doc, r).wait()
            qkv_keep(doc).start()

        attend(layout, qkv, att, lse_ref, doc, pair, size, tile)

        @pl.when(pair == pairs - 1)
        def _():
            att_keep(doc).start()
            att_home(doc).start()
            for r in range(1, ns):
                att_away(doc, r).start()

        return carry

    lax.fori_loop(0, docs * pairs, one_pair, 0)
    for n in range(1, len(up_steps)):
        if n not in inside:
            up_steps[n]()
    for i in range(docs):
        x_keep(i).wait()
        pl.when(jnp.logical_not(p.stays))(lambda i=i: cot_remote(i).wait())
        qkv_keep(i).wait()
        att_keep(i).wait()
        att_home(i).wait()
        for r in range(1, ns):
            att_away(i, r).wait()
    for keep in keeps:
        keep.wait()
    low_keep.wait()
    for g in gathers + [up_gather]:
        g.drain()


def front(nb, ns, layout, x, cot, wq, wk, wv, wo, up, gain, adapters, size, tile=256):
    docs, rows, d = x.shape
    w = d // ns
    n = rows * ns
    any_spec = pl.BlockSpec(memory_space=pl.ANY)
    vmem = pl.BlockSpec(memory_space=pltpu.VMEM)
    dma = pltpu.SemaphoreType.DMA
    like = lambda *shape: jax.ShapeDtypeStruct(shape, BF)
    heads = (ns, docs, rows, w)
    outs = [like(3, *heads), like(*heads), like(*heads), jax.ShapeDtypeStruct((docs, w // 128, 2, n), F32),
            like(docs, rows, 128), like(*x.shape), like(*x.shape)] + [like(nb, *wq.shape)] * 4 + [like(nb, *up.shape)]
    return pl.pallas_call(
        functools.partial(front_kernel, nb, ns, size, tile),
        in_specs=[pl.BlockSpec(memory_space=pltpu.SMEM)] + [any_spec] * 7 + [vmem] * 5,
        out_specs=[any_spec] * 3 + [vmem] + [any_spec] * 8,
        out_shape=outs,
        scratch_shapes=[pltpu.VMEM(x.shape, BF), pltpu.VMEM(x.shape, BF), pltpu.VMEM((3, docs, ns, rows, w), BF),
                        pltpu.VMEM((3,) + heads, BF), pltpu.VMEM(heads, BF), pltpu.VMEM((docs, rows, 128), BF),
                        pltpu.VMEM((4, nb) + wq.shape, BF), pltpu.VMEM(up.shape, BF),
                        pltpu.VMEM((d, 128), BF), pltpu.VMEM((3, 128, d), BF), dma((4, 4, nb)), dma((4, nb)), dma((5, nb)), dma((nb,)), dma((docs,)), dma((docs,)),
                        dma((docs,)), dma((docs,)), dma((3, docs, ns)), dma((3, docs, ns)), dma((docs, ns)), dma((docs, ns)),
                        dma((docs + 6,)), dma((docs,)), dma((docs, 2))],
        compiler_params=pltpu.CompilerParams(collective_id=0, has_side_effects=True, vmem_limit_bytes=62 << 20),
        name="front",
    )(layout, x, cot, wq, wk, wv, wo, up, gain, *adapters)


def middle_kernel(nb, ns, x_hbm, att_hbm, kept_hbm, cot_hbm, gain_ref, wo_hbm, up_hbm, down_hbm,
                  out_hbm, rg_hbm, mix_hbm,
                  xs, atts, cots, wos, downs, ups, acc, xhs, dn, n2s, invs, us, gs,
                  send, recv, msend, mrecv, load, store):
    docs, rows, d = x_hbm.shape
    w = d // ns
    p = Place(nb, ns)
    held = down_hbm.shape[0]
    chunk = 2 * held
    loads = [pltpu.make_async_copy(wo_hbm, wos, load.at[0]), pltpu.make_async_copy(att_hbm, atts, load.at[3 + docs])]
    for i in range(docs):
        loads.append(pltpu.make_async_copy(x_hbm.at[i], xs.at[i], load.at[1 + i]))
    loads.append(pltpu.make_async_copy(up_hbm, ups, load.at[1 + docs]))
    for copy in loads:
        copy.start()

    def cot_load(source):
        return pltpu.make_async_copy(source, cots, load.at[2 + docs])

    pl.when(p.stays)(lambda: cot_load(kept_hbm).start())
    pl.when(jnp.logical_not(p.stays))(lambda: cot_load(cot_hbm).start())
    p.greet(p.gather_ways() + [(p.peer(r), None) for r in range(1, ns)])

    gather = Gather(p, down_hbm, downs, send, recv)

    gather.start()
    for copy in loads[:-1]:
        copy.wait()
    def rows_of(i):
        return pl.ds(pl.multiple_of(i * rows, rows), rows)

    def second_norm(i, carry):
        at = rows_of(i)
        res = xs[i].astype(F32)
        for g in range(ns):
            res = res + dot(atts[g, i], wos[g * w:(g + 1) * w, :])
        acc[at, :] = res
        xh, inv = normalise(res)
        xhs[at, :] = xh
        invs[at, :] = jnp.broadcast_to(inv, (rows, 128))
        n2s[at, :] = (xh * gain_ref[...]).astype(BF)
        dn[at, :] = jnp.zeros((rows, d), F32)
        return carry

    lax.fori_loop(0, docs, second_norm, 0)
    loads[-1].wait()
    cot_load(cot_hbm).wait()
    gather.mine().wait()
    pair = p.b // 2 % 2

    def weights(f):
        base = flip(p.line, f // 2) * 4 + (pair + f) % 2 * 2
        up = ups[:, :, pl.ds(pl.multiple_of(base * held, chunk), chunk)].reshape(d, chunk)
        return up, downs[pl.ds(base, 2)].reshape(chunk, d)

    tall = docs * rows // 2
    tiles = nb // 2 * 2

    def tile_of(t):
        return pl.ds(pl.multiple_of(t % 2 * tall, tall), tall)

    def hidden(t):
        up, down = weights(t // 2)
        us[t % 2] = dot(n2s[tile_of(t), :], up)
        gs[t % 2] = dot(cots[tile_of(t), :], down, NT)

    def one_tile(t, carry):
        f, i = t // 2, t % 2
        k, after = f // 2, f + 1

        @pl.when((i == 0) & (f % 2 == 0))
        def _():
            @pl.when(k + 1 < p.lines)
            def _():
                gather.hop(k + 1, pairs=False)
                gather.hand_pair(flip(p.line, k + 1))

            gather.relay_line(flip(p.line, k))

        pl.when((i == 1) & (t + 1 < tiles))(lambda: gather.from_core(flip(p.line, after // 2), after % 2))
        hidden(jnp.minimum(t + 1, tiles - 1))
        up, down = weights(f)
        act, slope = gelu_parts(us[t % 2])
        pg = (slope * gs[t % 2]).astype(BF)
        at = tile_of(t)
        acc[at, :] += dot(act.astype(BF), down)
        dn[at, :] += dot(pg, up, NT)
        return carry

    gather.from_core(p.line, 0)
    hidden(0)
    lax.fori_loop(0, tiles, one_tile, 0)

    def out_and_grad(i, carry):
        at = rows_of(i)
        xs[i] = acc[at, :].astype(BF)
        rg = cots[at, :].astype(F32) + norm_back(xhs[at, :], invs[at, :1], gain_ref[...], dn[at, :])
        xhs[at, :] = rg
        mix = dot(rg.astype(BF), wos[...], NT).astype(BF)
        for g in range(ns):
            atts[g, i] = mix[:, g * w:(g + 1) * w]
        for copy in results(i):
            copy.start()
        return carry

    def results(i):
        out = [pltpu.make_async_copy(atts.at[p.part, i], mix_hbm.at[p.part, i], store.at[2, i]),
               pltpu.make_async_copy(xs.at[i], out_hbm.at[i], store.at[0, i]),
               pltpu.make_async_copy(xhs.at[rows_of(i)], rg_hbm.at[i], store.at[1, i])]
        for r in range(1, ns):
            out.append(pltpu.make_async_remote_copy(
                src_ref=atts.at[flip(p.part, r), i], dst_ref=mix_hbm.at[p.part, i], send_sem=msend.at[i, r],
                recv_sem=mrecv.at[i, r], device_id=p.peer(r), device_id_type=MESH))
        return out

    lax.fori_loop(0, docs, out_and_grad, 0)
    for i in range(docs):
        for copy in results(i):
            copy.wait()
    gather.drain()


def middle(nb, ns, x, att, kept, cot, gain, wo, up, down):
    docs, rows, d = x.shape
    w = d // ns
    n = docs * rows
    any_spec = pl.BlockSpec(memory_space=pl.ANY)
    vmem = pl.BlockSpec(memory_space=pltpu.VMEM)
    dma = pltpu.SemaphoreType.DMA
    return pl.pallas_call(
        functools.partial(middle_kernel, nb, ns),
        in_specs=[any_spec] * 4 + [vmem] + [any_spec] * 3,
        out_specs=[any_spec] * 3,
        out_shape=[jax.ShapeDtypeStruct((docs, rows, d), BF), jax.ShapeDtypeStruct((docs, rows, d), F32),
                   jax.ShapeDtypeStruct((ns, docs, rows, w), BF)],
        scratch_shapes=[pltpu.VMEM((docs, rows, d), BF), pltpu.VMEM((ns, docs, rows, w), BF),
                        pltpu.VMEM((n, d), BF), pltpu.VMEM(wo.shape, BF), pltpu.VMEM((nb,) + down.shape, BF),
                        pltpu.VMEM(up.shape, BF), pltpu.VMEM((n, d), F32),
                        pltpu.VMEM((n, d), F32), pltpu.VMEM((n, d), F32), pltpu.VMEM((n, d), BF),
                        pltpu.VMEM((n, 128), F32), pltpu.VMEM((2, n // 2, 2 * down.shape[0]), F32),
                        pltpu.VMEM((2, n // 2, 2 * down.shape[0]), F32),
                        dma((4, nb)), dma((nb,)), dma((docs, ns)), dma((docs, ns)), dma((4 + docs,)), dma((3, docs))],
        compiler_params=pltpu.CompilerParams(collective_id=2, has_side_effects=True, vmem_limit_bytes=63 << 20),
        name="feed_forward",
    )(x, att, kept.reshape(n, d), cot.reshape(n, d), gain, wo, up, down)


class DeviceSum:
    def __init__(self, p, mine, first, second, total, sends, recvs):
        self.p, self.mine, self.first, self.second, self.total = p, mine, first, second, total
        self.sends, self.recvs = sends, recvs
        self.slot, self.block = p.b % 16, p.b - p.b % 16
        self.many = p.nb // 16 * p.ns
        self.at = (p.b // 16) * p.ns + p.s

    def copy(self, phase, j, src, dst, device):
        return pltpu.make_async_remote_copy(
            src_ref=src, dst_ref=dst, send_sem=self.sends.at[phase, j], recv_sem=self.recvs.at[phase, j],
            device_id=device, device_id_type=MESH)

    def fellow(self, j):
        return (self.block + flip(self.slot, j), self.p.s)

    def scatter(self, j):
        return self.copy(0, j, self.mine.at[flip(self.slot, j)], self.first.at[self.slot], self.fellow(j))

    def share(self, j):
        to, ns = flip(self.at, j), self.p.ns
        return self.copy(1, j, self.second.at[self.at], self.second.at[self.at], ((to // ns) * 16 + self.slot, to % ns))

    def spread(self, j):
        return self.copy(2, j, self.total.at[self.slot], self.total.at[self.slot], self.fellow(j))

    def begin(self):
        for j in range(1, 16):
            self.scatter(j).start()
        self.first[self.slot] = self.mine[self.slot]

    def middle(self):
        for j in range(1, 16):
            self.scatter(j).wait()
        self.second[self.at] = jnp.sum(self.first[...], axis=0)
        for j in range(1, self.many):
            self.share(j).start()

    def end(self):
        for j in range(1, self.many):
            self.share(j).wait()
        self.total[self.slot] = jnp.sum(self.second[...], axis=0)
        for j in range(1, 16):
            self.spread(j).start()

    def finish(self):
        for j in range(1, 16):
            self.spread(j).wait()


def sum_ways(p):
    b, s, nb, ns = p.b, p.s, p.nb, p.ns
    slot, block = b % 16, b - b % 16
    at = (b // 16) * ns + s
    ways = [((block + flip(slot, j), s), None) for j in range(1, 16)]
    for j in range(1, nb // 16 * ns):
        to = flip(at, j)
        ways.append((((to // ns) * 16 + slot, to % ns), None))
    return ways


CUTS = 2


def backward_kernel(nb, ns, rank, size, tile, layout, q_ref, k_ref, v_ref, o_ref, g_ref, lse_ref, top_hbm, x_hbm, gain_ref,
                    rg_hbm, low_hbm, wq_hbm, wk_hbm, wv_hbm, qd_ref, qu_ref, vd_ref, vu_ref, top_out, out_hbm, sum_ref,
                    dqt, stage, xs, rgs, ds, wqs, wks, wvs, lows, outs, gds, gqs, gvs, mine, first, second, summed,
                    tops, xhs, lgs, down_ref, upq_ref, upv_ref,
                    load, dsend, drecv, osend, orecv, tsend, trecv, ssend, srecv):
    docs, rows, d = x_hbm.shape
    w = d // ns
    p = Place(nb, ns)
    doc, pair = pl.program_id(0), pl.program_id(1)
    pairs = w // 128
    loads = [pltpu.make_async_copy(a, v, load.at[n]) for n, (a, v) in enumerate(
        ((wq_hbm, wqs), (wk_hbm, wks), (wv_hbm, wvs), (low_hbm, lows), (x_hbm, xs), (rg_hbm, rgs)))]

    def away(t, i, r, n):
        at = pl.ds(pl.multiple_of(n * 128, 128), 128)
        return pltpu.make_async_remote_copy(
            src_ref=stage.at[i, t, flip(p.part, r), :, at], dst_ref=ds.at[t, p.part, i, :, at], send_sem=dsend.at[t, i, r, n],
            recv_sem=drecv.at[t, i, r, n], device_id=p.peer(r), device_id_type=MESH)

    cut = rows // CUTS

    def out_away(i, n):
        at = pl.ds(pl.multiple_of(n * cut, cut), cut)
        return pltpu.make_async_remote_copy(
            src_ref=outs.at[i, at], dst_ref=out_hbm.at[i, at], send_sem=osend.at[i, n], recv_sem=orecv.at[i, n],
            device_id=p.partner, device_id_type=MESH)

    def out_home(i, n):
        at = pl.ds(pl.multiple_of(n * cut, cut), cut)
        return pltpu.make_async_copy(outs.at[i, at], out_hbm.at[i, at], orecv.at[i, n])

    def top_away(i):
        return pltpu.make_async_remote_copy(
            src_ref=top_hbm.at[i], dst_ref=top_out.at[i], send_sem=tsend.at[i], recv_sem=trecv.at[i],
            device_id=p.partner, device_id_type=MESH)

    top_in = pltpu.make_async_copy(top_hbm, tops, tsend.at[0])
    top_home = pltpu.make_async_copy(tops, top_out, trecv.at[0])
    ways = [(p.peer(r), None) for r in range(1, ns)] + [(p.partner, jnp.logical_not(p.stays))] + sum_ways(p)
    total = DeviceSum(p, mine, first, second, summed, ssend, srecv)

    @pl.when((doc == 0) & (pair == 0))
    def _():
        p.hello(ways)
        for copy in loads:
            copy.start()
        pl.when(p.stays)(lambda: top_in.start())
        down_ref[...] = down_maps(qd_ref[...], vd_ref[...])
        upq_ref[...] = up_map(qu_ref[...], 0)
        upv_ref[...] = up_map(vu_ref[...], rank)
        gds[...] = jnp.zeros_like(gds)
        gqs[...] = jnp.zeros_like(gqs)
        gvs[...] = jnp.zeros_like(gvs)

    @pl.when(doc < docs)
    def _():
        attention_gradients(layout, q_ref, k_ref, v_ref, o_ref, g_ref, lse_ref, stage, dqt, doc, pair, size, tile)

        @pl.when((doc == 0) & (pair == 0))
        def _():
            p.met(ways)
            pl.when(p.stays)(lambda: top_in.wait())
            pl.when(p.stays)(lambda: top_home.start())
            for i in range(docs):
                pl.when(jnp.logical_not(p.stays))(lambda i=i: top_away(i).start())

        for t in range(3):
            for r in range(1, ns):
                away(t, doc, r, pair).start()

    @pl.when((doc > 0) & (pair == 0))
    def _():
        i = doc - 1

        @pl.when(i == 0)
        def _():
            for copy in loads:
                copy.wait()

        for t in range(3):
            for r in range(1, ns):
                for n in range(pairs):
                    away(t, i, r, n).wait()

        xh, inv = normalise(xs[i].astype(F32))
        xhs[:, :d] = xh
        xhs[:, d:] = jnp.broadcast_to(inv, (rows, 128))
        lg = jnp.zeros((rows, 128), F32)
        for r in range(ns):
            g = flip(p.part, r)
            cols = pl.ds(pl.multiple_of(g * w, w), w)
            for t, up, grads in ((0, upq_ref, gqs), (2, upv_ref, gvs)):
                piece = ds[t, g, i] if r else stage[i, t, p.part]
                lg = lg + dot(piece, up[:, cols], NT)
                grads[:, cols] += dot(lows[i], piece, TN)
        lgs[...] = lg.astype(BF)
        gds[...] += dot(lgs[...], (xh * gain_ref[...]).astype(BF), TN)

        @pl.when(i == docs - 1)
        def _():
            upper = lax.broadcasted_iota(jnp.int32, (2 * rank, 1), 0) < rank
            both = jnp.where(upper, gqs[:2 * rank, :], gvs[:2 * rank, :]) * ADAPTER_SCALE
            for n in range(8):
                mine[n] = gds[:8, n * 128:(n + 1) * 128]
                mine[8 + n] = both[:, n * 128:(n + 1) * 128]
            total.begin()

        def some_rows(n, carry):
            at = pl.ds(pl.multiple_of(n * cut, cut), cut)
            fg = dot(lgs[at, :], down_ref[...], NT)
            for r in range(ns):
                g = flip(p.part, r)
                cols = pl.ds(pl.multiple_of(g * w, w), w)
                for t, full in enumerate((wqs, wks, wvs)):
                    piece = ds[t, g, i, at, :] if r else stage[i, t, p.part, at, :]
                    fg = fg + dot(piece, full[:, :, cols].reshape(d, w), NT)
            outs[i, at, :] = (rgs[i, at, :] + norm_back(xhs[at, :d], xhs[at, d:d + 1], gain_ref[...], fg)).astype(BF)
            pl.when(p.stays)(lambda: out_home(i, n).start())
            pl.when(jnp.logical_not(p.stays))(lambda: out_away(i, n).start())
            pl.when((i == docs - 1) & (n == 0))(total.middle)
            return carry

        lax.fori_loop(0, CUTS, some_rows, 0)
        pl.when(i == docs - 1)(total.end)

    @pl.when((doc == docs) & (pair == pairs - 1))
    def _():
        total.finish()
        sum_ref[...] = summed[...]
        pl.when(p.stays)(lambda: top_home.wait())
        for i in range(docs):
            for n in range(CUTS):
                pl.when(p.stays)(lambda i=i, n=n: out_home(i, n).wait())
                pl.when(jnp.logical_not(p.stays))(lambda i=i, n=n: out_away(i, n).wait())
            pl.when(jnp.logical_not(p.stays))(lambda i=i: top_away(i).wait())


def attention_gradients(layout, q_ref, k_ref, v_ref, o_ref, g_ref, lse_ref, stage, dqt, doc, pair, size, tile):
    parts, rows = o_ref.shape[0], o_ref.shape[2]
    n = parts * rows
    blocks, per = n // size, rows // size
    q = picked(q_ref.at[0], layout, blocks, size)
    k = picked(k_ref.at[0], layout, blocks, size)
    v = picked(v_ref.at[0], layout, blocks, size)
    o = picked(o_ref, layout, blocks, size)
    g = picked(g_ref, layout, blocks, size)
    kt = k.T
    lane = lax.broadcasted_iota(jnp.int32, (1, 128), 1)
    c = SCORE_SCALE * LOG2E
    tri = lax.broadcasted_iota(jnp.int32, (tile, tile), 0) <= lax.broadcasted_iota(jnp.int32, (tile, tile), 1)
    prod = (o.astype(F32) * g.astype(F32)).astype(BF)
    heads = (lax.broadcasted_iota(jnp.int32, (8, 128), 1) // 64 == lax.broadcasted_iota(jnp.int32, (8, 128), 0)).astype(BF)
    delta = dot(heads, prod, NT)
    zero = jnp.zeros((), BF)
    masks = [(lane < 64) == (h == 0) for h in range(2)]
    qms = [jnp.where(mk, q, zero) for mk in masks]
    gms = [jnp.where(mk, g, zero) for mk in masks]
    lse = lse_ref[0, 0]
    dks, dvs = [], []
    work = [(j, h) for j in range(n // tile) for h in range(2)]

    def products(j, h):
        lo, hi = j * tile, (j + 1) * tile
        return dot(k[lo:hi], qms[h][lo:], NT), dot(v[lo:hi], gms[h][lo:], NT)

    waiting = []
    sums = {}

    def settle():
        j, h, p, ds = waiting.pop(0)
        lo, hi = j * tile, (j + 1) * tile
        dv = dot(p, gms[h][lo:])
        dk = dot(ds, qms[h][lo:])
        dq = dot(kt[64 * h:64 * h + 64, lo:hi], ds)
        if j == 0:
            dqt[64 * h:64 * h + 64, :] = dq
        else:
            dqt[64 * h:64 * h + 64, lo:] += dq
        if h == 0:
            sums[j] = dk, dv
        else:
            dks.append(((sums[j][0] + dk) * SCORE_SCALE).astype(BF))
            dvs.append((sums[j][1] + dv).astype(BF))

    ahead = products(*work[0])
    for t, (j, h) in enumerate(work):
        st, dp = ahead
        if t + 1 < len(work):
            ahead = products(*work[t + 1])
        lo, hi = j * tile, (j + 1) * tile
        p = jnp.exp2(st * c - lse[h:h + 1, lo:])
        diag = jnp.where(tri, p[:, :tile], 0.0)
        p = diag if hi == n else jnp.concatenate([diag, p[:, tile:]], axis=1)
        waiting.append((j, h, p.astype(BF), (p * (dp - delta[h:h + 1, lo:])).astype(BF)))
        if t:
            settle()
    settle()
    lanes = pl.ds(pl.multiple_of(pair * 128, 128), 128)
    for t, value in enumerate(((dqt[...] * SCORE_SCALE).T.astype(BF), jnp.concatenate(dks, axis=0),
                               jnp.concatenate(dvs, axis=0))):
        def store(b, piece, t=t):
            stage[doc, t, b // per, b % per * size:(b % per + 1) * size, lanes] = piece
        put_back(value, layout, blocks, size, store)


def backward(nb, ns, rank, layout, qkv, o, g, lse, top, x, gain, rg, low, wq, wk, wv, adapters, size, tile=256):
    docs, rows, d = x.shape
    parts = o.shape[0]
    w = d // ns
    n = parts * rows
    any_spec = pl.BlockSpec(memory_space=pl.ANY)
    vmem = pl.BlockSpec(memory_space=pltpu.VMEM)
    dma = pltpu.SemaphoreType.DMA
    many = max(16, nb // 16 * ns)
    spec = pl.BlockSpec((parts, 1, rows, 128), lambda i, j: (0, jnp.minimum(i, docs - 1), 0, j))
    row = jax.ShapeDtypeStruct(x.shape, BF)

    def third(t):
        return pl.BlockSpec((1, parts, 1, rows, 128), lambda i, j: (t, 0, jnp.minimum(i, docs - 1), 0, j))

    return pl.pallas_call(
        functools.partial(backward_kernel, nb, ns, rank, size, tile),
        grid=(docs + 1, w // 128),
        in_specs=[pl.BlockSpec(memory_space=pltpu.SMEM), third(0), third(1), third(2), spec, spec]
        + [pl.BlockSpec((1, 1, 2, n), lambda i, j: (jnp.minimum(i, docs - 1), j, 0, 0))]
        + [any_spec] * 2 + [vmem] + [any_spec] * 5 + [vmem] * 4,
        out_specs=[any_spec, any_spec, vmem],
        out_shape=[row, row, jax.ShapeDtypeStruct((16, 8, 128), F32)],
        scratch_shapes=[pltpu.VMEM((128, n), F32), pltpu.VMEM((docs, 3, parts, rows, w), BF),
                        pltpu.VMEM(x.shape, BF), pltpu.VMEM(x.shape, F32), pltpu.VMEM((3, ns, docs, rows, w), BF)]
        + [pltpu.VMEM(wq.shape, BF)] * 3
        + [pltpu.VMEM(low.shape, BF), pltpu.VMEM(x.shape, BF)] + [pltpu.VMEM((128, d), F32)] * 3
        + [pltpu.VMEM((16, 8, 128), F32), pltpu.VMEM((16, 8, 128), F32), pltpu.VMEM((nb // 16 * ns, 8, 128), F32),
           pltpu.VMEM((16, 8, 128), F32),
           pltpu.VMEM(x.shape, BF), pltpu.VMEM((rows, d + 128), F32), pltpu.VMEM((rows, 128), BF),
           pltpu.VMEM((d, 128), BF), pltpu.VMEM((128, d), BF), pltpu.VMEM((128, d), BF),
           dma((6,)), dma((3, docs, ns, w // 128)), dma((3, docs, ns, w // 128)), dma((docs, CUTS)), dma((docs, CUTS)), dma((docs,)), dma((docs,)),
           dma((3, many)), dma((3, many))],
        compiler_params=pltpu.CompilerParams(collective_id=3, has_side_effects=True, vmem_limit_bytes=62 << 20),
        name="backward",
    )(layout, qkv, qkv, qkv, o, g, lse, top, x, gain, rg, low, wq, wk, wv, *adapters)


def local(
    nb, ns,
    tokens, cotangent, layout, attention_norm_gain, feedforward_norm_gain,
    query_weight, key_weight, value_weight, attention_output_weight, up_weight, down_weight,
    query_down_adapter, query_up_adapter, value_down_adapter, value_up_adapter,
):
    docs, rows, d = tokens.shape
    size = rows * ns // layout.shape[0]
    rank = query_up_adapter.shape[0]
    adapters = (query_down_adapter.T, query_up_adapter, value_down_adapter.T, value_up_adapter)
    gain1 = attention_norm_gain[None]
    gain2 = feedforward_norm_gain[None]

    qkv, att, mixed, lse, low, x, cot, wq, wk, wv, wo, w_up = front(
        nb, ns, layout, tokens, cotangent, query_weight, key_weight, value_weight, attention_output_weight, up_weight,
        gain1, adapters, size)
    out, rg, mix = middle(nb, ns, x, mixed, cotangent, cot, gain2, wo.reshape(d, d), w_up, down_weight)
    layer_out, input_grad, sums = backward(
        nb, ns, rank, layout, qkv, att, mix, lse, out, x, gain1, rg, low, wq, wk, wv, adapters, size)
    sums = sums.reshape(2, d // 128, 2 * rank, 128).transpose(0, 2, 1, 3).reshape(2, 2 * rank, d)
    return (layer_out, input_grad, sums[0, :rank].T, sums[1, :rank], sums[0, rank:].T, sums[1, rank:])


def solution(mesh):
    spec = P("batch", "seq", None)
    weight = P("batch", None)
    return jax.shard_map(
        functools.partial(local, mesh.shape["batch"], mesh.shape["seq"]),
        mesh=mesh,
        in_specs=(spec, spec, P(), P(), P()) + (weight,) * 6 + (P(),) * 4,
        out_specs=(spec, spec, P(), P(), P(), P()),
        check_vma=False,
    )
```

```python
import functools
import math

import jax
import jax.numpy as jnp
from jax import lax
from jax.experimental import pallas as pl
from jax.experimental.pallas import tpu as pltpu
from jax.sharding import PartitionSpec as P


EPSILON = 1e-05
ADAPTER_SCALE = 8.0
SCORE_SCALE = 0.125
NEG_FILL = -1e30
GELU_C = 0.7978845608028654
LOG2E = math.log2(math.e)
F32 = jnp.float32
BF = jnp.bfloat16
NN = (((1,), (0,)), ((), ()))
NT = (((1,), (1,)), ((), ()))
TN = (((0,), (0,)), ((), ()))


def dot(a, b, dims=NN):
    return lax.dot_general(a, b, dims, preferred_element_type=F32)


def normalise(x):
    mean = jnp.mean(x, axis=-1, keepdims=True)
    centred = x - mean
    inv = lax.rsqrt(jnp.mean(centred * centred, axis=-1, keepdims=True) + EPSILON)
    return centred * inv, inv


def norm_back(xh, inv, gain, up):
    t = up * gain
    return inv * (t - jnp.mean(t, axis=-1, keepdims=True) - xh * jnp.mean(t * xh, axis=-1, keepdims=True))


def gelu_parts(u):
    cubic = 0.044715 * u * u
    th = jnp.tanh(GELU_C * (u + cubic * u))
    half = 0.5 * (1.0 + th)
    return half * u, half + (0.5 * GELU_C) * u * (1.0 - th * th) * (1.0 + 3.0 * cubic)


MESH = pl.DeviceIdType.MESH


def flip(i, bits, width=5):
    out = 0
    for n in range(width):
        bit = 1 << n
        out = out + ((i // bit) % 2 + (bits // bit) % 2) % 2 * bit
    return out


def trade(b, s):
    return b - b % 2 + s % 2, s - s % 2 + b % 2


class Place:
    def __init__(self, nb, ns):
        self.nb, self.ns = nb, ns
        self.b, self.s = lax.axis_index("batch"), lax.axis_index("seq")
        self.lines = nb // 4
        self.line = self.b // 4
        self.partner = trade(self.b, self.s)
        self.stays = self.b % 2 == self.s % 2
        self.doc, self.part = trade(self.b, self.s)

    def peer(self, r):
        return trade(self.doc, flip(self.part, r))

    def hello(self, ways):
        bar = pltpu.get_barrier_semaphore()
        for device, cond in ways:
            def signal(device=device):
                pl.semaphore_signal(bar, inc=1, device_id=device, device_id_type=MESH)
            signal() if cond is None else pl.when(cond)(signal)

    def met(self, ways):
        count = 0
        for _, cond in ways:
            count = count + (1 if cond is None else jnp.where(cond, 1, 0))
        pl.semaphore_wait(pltpu.get_barrier_semaphore(), count)

    def greet(self, ways):
        self.hello(ways)
        self.met(ways)

    def gather_ways(self):
        b, s = self.b, self.s
        return [((b + 4, s), self.line + 1 < self.lines), ((b - 4, s), self.line > 0),
                ((flip(b, 2), s), None), ((flip(b, 1), s), None)]


class Gather:
    def __init__(self, place, own, full, send, recv):
        self.p, self.own, self.full, self.send, self.recv = place, own, full, send, recv

    def part(self, line, pair=0, core=0):
        b = self.p.b
        return line * 4 + (b // 2 + pair) % 2 * 2 + (b + core) % 2

    def copy(self, i, way, src=None):
        p = self.p
        to = [p.b + 4, p.b - 4, self.part(p.line, 1), self.part(p.line, 0, 1)][way]
        return pltpu.make_async_remote_copy(
            src_ref=self.full.at[i] if src is None else src, dst_ref=self.full.at[i],
            send_sem=self.send.at[way, i], recv_sem=self.recv.at[i],
            device_id=(to, p.s), device_id_type=MESH)

    def mine(self):
        return pltpu.make_async_copy(self.own, self.full.at[self.p.b], self.recv.at[self.p.b])

    def start(self):
        p = self.p
        pl.when(p.line + 1 < p.lines)(lambda: self.copy(p.b, 0, self.own).start())
        pl.when(p.line > 0)(lambda: self.copy(p.b, 1, self.own).start())
        self.hand_pair(p.line, self.own)
        self.copy(p.b, 3, self.own).start()
        self.mine().start()

    def hand_pair(self, line, src=None):
        self.copy(self.part(line), 2, src).start()

    def pair_sent(self, line):
        self.copy(self.part(line), 2).wait_send()

    def hop(self, k, pairs=True):
        p = self.p

        def take(way, line):
            i = self.part(line)
            self.copy(i, way).wait_recv()
            more = p.line + 1 < p.lines if way == 0 else p.line > 0
            pl.when(more)(lambda: self.copy(i, way).start())
            if pairs:
                self.hand_pair(line)
            self.copy(i, 3).start()

        below, above = p.line - k, p.line + k
        pl.when(below >= 0)(lambda: take(0, below))
        pl.when(above < p.lines)(lambda: take(1, above))

    def relay_line(self, line):
        i = self.part(line, 1)
        self.copy(i, 2).wait_recv()
        self.copy(i, 3).start()

    def relay(self, k):
        p = self.p
        if k == 0:
            self.relay_line(p.line)
        else:
            pl.when(p.line >= k)(lambda: self.relay_line(p.line - k))
            pl.when(p.line + k < p.lines)(lambda: self.relay_line(p.line + k))

    def from_core(self, line, pair):
        self.copy(self.part(line, pair, 1), 3).wait_recv()

    def finish(self):
        self.mine().wait()
        for line in range(self.p.lines):
            for pair in range(2):
                self.from_core(line, pair)

    def drain(self):
        p = self.p
        for line in range(p.lines):
            i = self.part(line)
            pl.when((p.line >= line) & (p.line + 1 < p.lines))(lambda i=i: self.copy(i, 0).wait_send())
            pl.when((p.line <= line) & (p.line > 0))(lambda i=i: self.copy(i, 1).wait_send())
            self.pair_sent(line)
            self.copy(i, 3).wait_send()
            self.copy(self.part(line, 1), 3).wait_send()

    def steps(self):
        out = [self.start]
        for k in range(1, self.p.lines):
            out.append(functools.partial(run, [functools.partial(self.hop, k), functools.partial(self.relay, k - 1)]))
        out.append(functools.partial(self.relay, self.p.lines - 1))
        out.append(self.finish)
        return out


class PlaneGather(Gather):
    def __init__(self, place, own, full, send, recv):
        super().__init__(place, own, full, send, recv)
        self.lacks = flip(place.line, 1 + place.s % 2)
        self.gives = flip(place.line, 2 - place.s % 2)

    def to_plane(self, i):
        p = self.p
        return pltpu.make_async_remote_copy(
            src_ref=self.full.at[i], dst_ref=self.full.at[i], send_sem=self.send.at[4, i], recv_sem=self.recv.at[i],
            device_id=(p.b, flip(p.s, 1)), device_id_type=MESH)

    def hand_pair(self, line, src=None):
        pl.when(line != self.lacks)(lambda: super(PlaneGather, self).hand_pair(line, src))

    def pair_sent(self, line):
        pl.when(line != self.lacks)(lambda: super(PlaneGather, self).pair_sent(line))

    def relay_line(self, line):
        @pl.when(line != self.lacks)
        def _():
            i = self.part(line, 1)
            self.copy(i, 2).wait_recv()
            pl.when(line == self.gives)(lambda: self.to_plane(i).start())
            self.copy(i, 3).start()

    def cross(self):
        i = self.part(self.lacks, 1)
        self.to_plane(i).wait_recv()
        self.copy(i, 3).start()

    def drain(self):
        super().drain()
        self.to_plane(self.part(self.gives, 1)).wait_send()

    def steps(self):
        out = super().steps()
        return out[:-1] + [self.cross] + out[-1:]


def run(calls):
    for call in calls:
        call()


def chosen(blocks, tests):
    out = blocks[0]
    for block, test in zip(blocks[1:], tests[1:]):
        out = jnp.where(test, block, out)
    return out


def picked(ref, layout, blocks, size):
    per = ref.shape[2] // size
    stored = [ref[t // per, 0, (t % per) * size:(t % per + 1) * size, :] for t in range(blocks)]
    return jnp.concatenate([chosen(stored, [layout[t] == p for t in range(blocks)]) for p in range(blocks)], axis=0)


def put_back(value, layout, blocks, size, store):
    pieces = [value[p * size:(p + 1) * size] for p in range(blocks)]
    for t in range(blocks):
        store(t, chosen(pieces, [layout[t] == p for p in range(blocks)]))


def attend(layout, qkv, out, lse_ref, doc, pair, size, tile):
    parts, rows = qkv.shape[1], qkv.shape[3]
    n = parts * rows
    blocks, per = n // size, rows // size
    lanes = pl.ds(pl.multiple_of(pair * 128, 128), 128)

    def in_order(t):
        stored = [qkv[t, b // per, doc, b % per * size:(b % per + 1) * size, lanes] for b in range(blocks)]
        return jnp.concatenate([chosen(stored, [layout[b] == p for b in range(blocks)]) for p in range(blocks)], axis=0)

    q, k, v = in_order(0), in_order(1), in_order(2)
    vt = v.T
    ones = jnp.ones((16, n), BF)
    vts = [jnp.concatenate([vt[64 * h:64 * h + 64], ones], axis=0) for h in range(2)]
    lane = lax.broadcasted_iota(jnp.int32, (1, 128), 1)
    c = SCORE_SCALE * LOG2E
    tri = lax.broadcasted_iota(jnp.int32, (tile, tile), 0) <= lax.broadcasted_iota(jnp.int32, (tile, tile), 1)
    work = [(i, h) for i in range(n // tile) for h in range(2)]
    lses = [[], []]
    mixed = {}
    waiting = []

    def scores(i, h):
        qm = jnp.where((lane < 64) == (h == 0), q[i * tile:(i + 1) * tile], jnp.zeros((), BF))
        return dot(k[:(i + 1) * tile], qm, NT)

    def settle():
        i, h, e, m = waiting.pop(0)
        o = dot(vts[h][:, :(i + 1) * tile], e)
        l = o[64:65]
        mixed[i, h] = o[:64] * (1.0 / l)
        lses[h].append(m + jnp.log2(l))

    ahead = [scores(*work[0]), scores(*work[1])]
    for t, (i, h) in enumerate(work):
        st = ahead.pop(0)
        if t + 2 < len(work):
            ahead.append(scores(*work[t + 2]))
        diag = jnp.where(tri, st[i * tile:], NEG_FILL)
        st = diag if i == 0 else jnp.concatenate([st[: i * tile], diag], axis=0)
        m = jnp.max(st, axis=0, keepdims=True) * c
        waiting.append((i, h, jnp.exp2(st * c - m).astype(BF), m))
        if t:
            settle()
    settle()
    outs = [jnp.concatenate([mixed[i, 0], mixed[i, 1]], axis=0).T.astype(BF) for i in range(n // tile)]

    def store(b, piece):
        out[b // per, doc, b % per * size:(b % per + 1) * size, lanes] = piece

    put_back(jnp.concatenate(outs, axis=0), layout, blocks, size, store)
    for h in range(2):
        lse_ref[doc, pair, h:h + 1, :] = jnp.concatenate(lses[h], axis=1)


UP_START = 1
UP_PLACES = (0, 4, 8)


def one_hot(rows, columns, first):
    at = lax.broadcasted_iota(jnp.int32, (rows, columns), 0) + first
    return (at == lax.broadcasted_iota(jnp.int32, (rows, columns), 1)).astype(BF)


def down_maps(qd, vd):
    rank = qd.shape[0]
    return (dot(qd, one_hot(rank, 128, 0), TN) + dot(vd, one_hot(rank, 128, rank), TN)).astype(BF)


def up_map(up, first):
    return (ADAPTER_SCALE * dot(one_hot(up.shape[0], 128, first), up, TN)).astype(BF)


def front_kernel(nb, ns, size, tile, layout, x_hbm, cot_hbm, wq_ref, wk_ref, wv_ref, wo_ref, up_hbm, gain_ref, qd_ref, qu_ref, vd_ref, vu_ref,
                 qkv_out, att_out, mixed_out, lse_ref, low_out, x_out, cot_out, wq_out, wk_out, wv_out, wo_out, up_out,
                 xs, n1s, stage, qkv, att, lows, ws, own, down_ref, ups_ref, send, recv, usend, urecv, xsend, xrecv, csend, crecv,
                 osend, orecv, asend, arecv, local_sem, qkv_sem, att_sem):
    docs, rows, d = x_hbm.shape
    w = d // ns
    pairs = w // 128
    p = Place(nb, ns)
    fetch = pltpu.make_async_copy(up_hbm, own, local_sem.at[docs + 5])
    fetch.start()
    p.greet(p.gather_ways() + [((p.b, flip(p.s, 1)), None), (p.partner, jnp.logical_not(p.stays))]
            + [(p.peer(r), None) for r in range(1, ns)])

    def x_remote(i):
        return pltpu.make_async_remote_copy(
            src_ref=x_hbm.at[i], dst_ref=xs.at[i], send_sem=xsend.at[i], recv_sem=xrecv.at[i],
            device_id=p.partner, device_id_type=MESH)

    def cot_remote(i):
        return pltpu.make_async_remote_copy(
            src_ref=cot_hbm.at[i], dst_ref=cot_out.at[i], send_sem=csend.at[i], recv_sem=crecv.at[i],
            device_id=p.partner, device_id_type=MESH)

    def x_local(i):
        return pltpu.make_async_copy(x_hbm.at[i], xs.at[i], xrecv.at[i])

    def x_keep(i):
        return pltpu.make_async_copy(xs.at[i], x_out.at[i], local_sem.at[i])

    for i in range(docs):
        pl.when(p.stays)(lambda i=i: x_local(i).start())
        pl.when(jnp.logical_not(p.stays))(lambda i=i: x_remote(i).start())
    for i in range(docs):
        pl.when(jnp.logical_not(p.stays))(lambda i=i: cot_remote(i).start())

    def first(i):
        pl.when(p.stays)(lambda: x_local(i).wait())
        pl.when(jnp.logical_not(p.stays))(lambda: x_remote(i).wait())
        x_keep(i).start()
        xh, _ = normalise(xs[i].astype(F32))
        n1 = (xh * gain_ref[...]).astype(BF)
        n1s[i] = n1
        lows[i] = dot(n1, down_ref[...]).astype(BF)

    def away(part, i, r):
        return pltpu.make_async_remote_copy(
            src_ref=stage.at[part, i, flip(p.part, r)], dst_ref=qkv.at[part, p.part, i],
            send_sem=osend.at[part, i, r], recv_sem=orecv.at[part, i, r],
            device_id=p.peer(r), device_id_type=MESH)

    def product(part, i):
        y = dot(n1s[i], ws[part].reshape(d, d)) + dot(lows[i], ups_ref[part])
        y = y.astype(BF)
        for g in range(ns):
            piece = y[:, g * w:(g + 1) * w]

            @pl.when(p.part == g)
            def _():
                qkv[part, p.part, i] = piece

            @pl.when(p.part != g)
            def _():
                stage[part, i, g] = piece
        for r in range(1, ns):
            away(part, i, r).start()

    gathers = [Gather(p, own_ref, ws.at[n], send.at[n], recv.at[n])
               for n, own_ref in enumerate((wq_ref, wk_ref, wv_ref, wo_ref))]
    keeps = [pltpu.make_async_copy(ws.at[n], out, local_sem.at[docs + n])
             for n, out in enumerate((wq_out, wk_out, wv_out, wo_out))]
    low_keep = pltpu.make_async_copy(lows, low_out, local_sem.at[docs + 4])
    up_gather = PlaneGather(p, own, up_out, usend, urecv)
    up_steps = up_gather.steps()

    lists = [g.steps() for g in gathers]
    delays = (0, 0, 2, 4)
    ready = [len(lists[0]) - 1 + delay for delay in delays]

    def slot(t):
        for n, steps in enumerate(lists):
            if 0 <= t - delays[n] < len(steps):
                steps[t - delays[n]]()
            if t == ready[n]:
                keeps[n].start()
        if t == UP_START + ready[0]:
            fetch.wait()
            up_steps[0]()

    slot(0)
    rank = qu_ref.shape[0]
    down_ref[...] = down_maps(qd_ref[...], vd_ref[...])
    ups_ref[0] = up_map(qu_ref[...], 0)
    ups_ref[1] = jnp.zeros((128, d), BF)
    ups_ref[2] = up_map(vu_ref[...], rank)
    for t in range(1, ready[0] + 1):
        slot(t)
    places = {2 * docs - 5 + 2 * n: t for n, t in enumerate(range(ready[0] + 1, ready[3] + 1))}

    def one_product(n, carry):
        early = n < 2 * docs
        part = jnp.where(early, n % 2, 2)
        i = jnp.where(early, n // 2, n - 2 * docs)
        pl.when(early & (part == 0))(lambda: first(i))
        product(part, i)
        for at, t in places.items():
            pl.when(n == at)(functools.partial(slot, t))
        return carry

    lax.fori_loop(0, 3 * docs, one_product, 0)
    low_keep.start()

    def qkv_keep(i):
        return pltpu.make_async_copy(qkv.at[:, :, i], qkv_out.at[:, :, i], qkv_sem.at[i])

    def att_keep(i):
        return pltpu.make_async_copy(att.at[:, i], att_out.at[:, i], att_sem.at[i, 0])

    def att_home(i):
        return pltpu.make_async_copy(att.at[p.part, i], mixed_out.at[p.part, i], att_sem.at[i, 1])

    def att_away(i, r):
        return pltpu.make_async_remote_copy(
            src_ref=att.at[flip(p.part, r), i], dst_ref=mixed_out.at[p.part, i], send_sem=asend.at[i, r],
            recv_sem=arecv.at[i, r], device_id=p.peer(r), device_id_type=MESH)

    inside = [n for n in range(1, len(up_steps)) if n <= len(UP_PLACES) and UP_PLACES[n - 1] < docs * pairs]

    def one_pair(m, carry):
        doc, pair = m // pairs, m % pairs
        for n in inside:
            pl.when(m == UP_PLACES[n - 1])(up_steps[n])

        @pl.when(pair == 0)
        def _():
            for part in range(3):
                for r in range(1, ns):
                    away(part, doc, r).wait()
            qkv_keep(doc).start()

        attend(layout, qkv, att, lse_ref, doc, pair, size, tile)

        @pl.when(pair == pairs - 1)
        def _():
            att_keep(doc).start()
            att_home(doc).start()
            for r in range(1, ns):
                att_away(doc, r).start()

        return carry

    lax.fori_loop(0, docs * pairs, one_pair, 0)
    for n in range(1, len(up_steps)):
        if n not in inside:
            up_steps[n]()
    for i in range(docs):
        x_keep(i).wait()
        pl.when(jnp.logical_not(p.stays))(lambda i=i: cot_remote(i).wait())
        qkv_keep(i).wait()
        att_keep(i).wait()
        att_home(i).wait()
        for r in range(1, ns):
            att_away(i, r).wait()
    for keep in keeps:
        keep.wait()
    low_keep.wait()
    for g in gathers + [up_gather]:
        g.drain()


def front(nb, ns, layout, x, cot, wq, wk, wv, wo, up, gain, adapters, size, tile=256):
    docs, rows, d = x.shape
    w = d // ns
    n = rows * ns
    any_spec = pl.BlockSpec(memory_space=pl.ANY)
    vmem = pl.BlockSpec(memory_space=pltpu.VMEM)
    dma = pltpu.SemaphoreType.DMA
    like = lambda *shape: jax.ShapeDtypeStruct(shape, BF)
    heads = (ns, docs, rows, w)
    outs = [like(3, *heads), like(*heads), like(*heads), jax.ShapeDtypeStruct((docs, w // 128, 2, n), F32),
            like(docs, rows, 128), like(*x.shape), like(*x.shape)] + [like(nb, *wq.shape)] * 4 + [like(nb, *up.shape)]
    return pl.pallas_call(
        functools.partial(front_kernel, nb, ns, size, tile),
        in_specs=[pl.BlockSpec(memory_space=pltpu.SMEM)] + [any_spec] * 7 + [vmem] * 5,
        out_specs=[any_spec] * 3 + [vmem] + [any_spec] * 8,
        out_shape=outs,
        scratch_shapes=[pltpu.VMEM(x.shape, BF), pltpu.VMEM(x.shape, BF), pltpu.VMEM((3, docs, ns, rows, w), BF),
                        pltpu.VMEM((3,) + heads, BF), pltpu.VMEM(heads, BF), pltpu.VMEM((docs, rows, 128), BF),
                        pltpu.VMEM((4, nb) + wq.shape, BF), pltpu.VMEM(up.shape, BF),
                        pltpu.VMEM((d, 128), BF), pltpu.VMEM((3, 128, d), BF), dma((4, 4, nb)), dma((4, nb)), dma((5, nb)), dma((nb,)), dma((docs,)), dma((docs,)),
                        dma((docs,)), dma((docs,)), dma((3, docs, ns)), dma((3, docs, ns)), dma((docs, ns)), dma((docs, ns)),
                        dma((docs + 6,)), dma((docs,)), dma((docs, 2))],
        compiler_params=pltpu.CompilerParams(collective_id=0, has_side_effects=True, vmem_limit_bytes=62 << 20),
        name="front",
    )(layout, x, cot, wq, wk, wv, wo, up, gain, *adapters)


def middle_kernel(nb, ns, x_hbm, att_hbm, kept_hbm, cot_hbm, gain_ref, wo_hbm, up_hbm, down_hbm,
                  out_hbm, rg_hbm, mix_hbm,
                  xs, atts, cots, wos, downs, ups, acc, xhs, dn, n2s, invs, us, gs,
                  send, recv, msend, mrecv, load, store):
    docs, rows, d = x_hbm.shape
    w = d // ns
    p = Place(nb, ns)
    held = down_hbm.shape[0]
    chunk = 2 * held
    loads = [pltpu.make_async_copy(wo_hbm, wos, load.at[0]), pltpu.make_async_copy(att_hbm, atts, load.at[3 + docs])]
    for i in range(docs):
        loads.append(pltpu.make_async_copy(x_hbm.at[i], xs.at[i], load.at[1 + i]))
    loads.append(pltpu.make_async_copy(up_hbm, ups, load.at[1 + docs]))
    for copy in loads:
        copy.start()

    def cot_load(source):
        return pltpu.make_async_copy(source, cots, load.at[2 + docs])

    pl.when(p.stays)(lambda: cot_load(kept_hbm).start())
    pl.when(jnp.logical_not(p.stays))(lambda: cot_load(cot_hbm).start())
    p.greet(p.gather_ways() + [(p.peer(r), None) for r in range(1, ns)])

    gather = Gather(p, down_hbm, downs, send, recv)

    gather.start()
    for copy in loads[:-1]:
        copy.wait()
    def rows_of(i):
        return pl.ds(pl.multiple_of(i * rows, rows), rows)

    def second_norm(i, carry):
        at = rows_of(i)
        res = xs[i].astype(F32)
        for g in range(ns):
            res = res + dot(atts[g, i], wos[g * w:(g + 1) * w, :])
        acc[at, :] = res
        xh, inv = normalise(res)
        xhs[at, :] = xh
        invs[at, :] = jnp.broadcast_to(inv, (rows, 128))
        n2s[at, :] = (xh * gain_ref[...]).astype(BF)
        dn[at, :] = jnp.zeros((rows, d), F32)
        return carry

    lax.fori_loop(0, docs, second_norm, 0)
    loads[-1].wait()
    cot_load(cot_hbm).wait()
    gather.mine().wait()
    pair = p.b // 2 % 2

    def weights(f):
        base = flip(p.line, f // 2) * 4 + (pair + f) % 2 * 2
        up = ups[:, :, pl.ds(pl.multiple_of(base * held, chunk), chunk)].reshape(d, chunk)
        return up, downs[pl.ds(base, 2)].reshape(chunk, d)

    tall = docs * rows // 2
    tiles = nb // 2 * 2

    def tile_of(t):
        return pl.ds(pl.multiple_of(t % 2 * tall, tall), tall)

    def hidden(t):
        up, down = weights(t // 2)
        us[t % 2] = dot(n2s[tile_of(t), :], up)
        gs[t % 2] = dot(cots[tile_of(t), :], down, NT)

    def one_tile(t, carry):
        f, i = t // 2, t % 2
        k, after = f // 2, f + 1

        @pl.when((i == 0) & (f % 2 == 0))
        def _():
            @pl.when(k + 1 < p.lines)
            def _():
                gather.hop(k + 1, pairs=False)
                gather.hand_pair(flip(p.line, k + 1))

            gather.relay_line(flip(p.line, k))

        pl.when((i == 1) & (t + 1 < tiles))(lambda: gather.from_core(flip(p.line, after // 2), after % 2))
        hidden(jnp.minimum(t + 1, tiles - 1))
        up, down = weights(f)
        act, slope = gelu_parts(us[t % 2])
        pg = (slope * gs[t % 2]).astype(BF)
        at = tile_of(t)
        acc[at, :] += dot(act.astype(BF), down)
        dn[at, :] += dot(pg, up, NT)
        return carry

    gather.from_core(p.line, 0)
    hidden(0)
    lax.fori_loop(0, tiles, one_tile, 0)

    def out_and_grad(i, carry):
        at = rows_of(i)
        xs[i] = acc[at, :].astype(BF)
        rg = cots[at, :].astype(F32) + norm_back(xhs[at, :], invs[at, :1], gain_ref[...], dn[at, :])
        xhs[at, :] = rg
        mix = dot(rg.astype(BF), wos[...], NT).astype(BF)
        for g in range(ns):
            atts[g, i] = mix[:, g * w:(g + 1) * w]
        for copy in results(i):
            copy.start()
        return carry

    def results(i):
        out = [pltpu.make_async_copy(atts.at[p.part, i], mix_hbm.at[p.part, i], store.at[2, i]),
               pltpu.make_async_copy(xs.at[i], out_hbm.at[i], store.at[0, i]),
               pltpu.make_async_copy(xhs.at[rows_of(i)], rg_hbm.at[i], store.at[1, i])]
        for r in range(1, ns):
            out.append(pltpu.make_async_remote_copy(
                src_ref=atts.at[flip(p.part, r), i], dst_ref=mix_hbm.at[p.part, i], send_sem=msend.at[i, r],
                recv_sem=mrecv.at[i, r], device_id=p.peer(r), device_id_type=MESH))
        return out

    lax.fori_loop(0, docs, out_and_grad, 0)
    for i in range(docs):
        for copy in results(i):
            copy.wait()
    gather.drain()


def middle(nb, ns, x, att, kept, cot, gain, wo, up, down):
    docs, rows, d = x.shape
    w = d // ns
    n = docs * rows
    any_spec = pl.BlockSpec(memory_space=pl.ANY)
    vmem = pl.BlockSpec(memory_space=pltpu.VMEM)
    dma = pltpu.SemaphoreType.DMA
    return pl.pallas_call(
        functools.partial(middle_kernel, nb, ns),
        in_specs=[any_spec] * 4 + [vmem] + [any_spec] * 3,
        out_specs=[any_spec] * 3,
        out_shape=[jax.ShapeDtypeStruct((docs, rows, d), BF), jax.ShapeDtypeStruct((docs, rows, d), F32),
                   jax.ShapeDtypeStruct((ns, docs, rows, w), BF)],
        scratch_shapes=[pltpu.VMEM((docs, rows, d), BF), pltpu.VMEM((ns, docs, rows, w), BF),
                        pltpu.VMEM((n, d), BF), pltpu.VMEM(wo.shape, BF), pltpu.VMEM((nb,) + down.shape, BF),
                        pltpu.VMEM(up.shape, BF), pltpu.VMEM((n, d), F32),
                        pltpu.VMEM((n, d), F32), pltpu.VMEM((n, d), F32), pltpu.VMEM((n, d), BF),
                        pltpu.VMEM((n, 128), F32), pltpu.VMEM((2, n // 2, 2 * down.shape[0]), F32),
                        pltpu.VMEM((2, n // 2, 2 * down.shape[0]), F32),
                        dma((4, nb)), dma((nb,)), dma((docs, ns)), dma((docs, ns)), dma((4 + docs,)), dma((3, docs))],
        compiler_params=pltpu.CompilerParams(collective_id=2, has_side_effects=True, vmem_limit_bytes=63 << 20),
        name="feed_forward",
    )(x, att, kept.reshape(n, d), cot.reshape(n, d), gain, wo, up, down)


class DeviceSum:
    def __init__(self, p, mine, first, second, total, sends, recvs):
        self.p, self.mine, self.first, self.second, self.total = p, mine, first, second, total
        self.sends, self.recvs = sends, recvs
        self.slot, self.block = p.b % 16, p.b - p.b % 16
        self.many = p.nb // 16 * p.ns
        self.at = (p.b // 16) * p.ns + p.s

    def copy(self, phase, j, src, dst, device):
        return pltpu.make_async_remote_copy(
            src_ref=src, dst_ref=dst, send_sem=self.sends.at[phase, j], recv_sem=self.recvs.at[phase, j],
            device_id=device, device_id_type=MESH)

    def fellow(self, j):
        return (self.block + flip(self.slot, j), self.p.s)

    def scatter(self, j):
        return self.copy(0, j, self.mine.at[flip(self.slot, j)], self.first.at[self.slot], self.fellow(j))

    def share(self, j):
        to, ns = flip(self.at, j), self.p.ns
        return self.copy(1, j, self.second.at[self.at], self.second.at[self.at], ((to // ns) * 16 + self.slot, to % ns))

    def spread(self, j):
        return self.copy(2, j, self.total.at[self.slot], self.total.at[self.slot], self.fellow(j))

    def begin(self):
        for j in range(1, 16):
            self.scatter(j).start()
        self.first[self.slot] = self.mine[self.slot]

    def middle(self):
        for j in range(1, 16):
            self.scatter(j).wait()
        self.second[self.at] = jnp.sum(self.first[...], axis=0)
        for j in range(1, self.many):
            self.share(j).start()

    def end(self):
        for j in range(1, self.many):
            self.share(j).wait()
        self.total[self.slot] = jnp.sum(self.second[...], axis=0)
        for j in range(1, 16):
            self.spread(j).start()

    def finish(self):
        for j in range(1, 16):
            self.spread(j).wait()


def sum_ways(p):
    b, s, nb, ns = p.b, p.s, p.nb, p.ns
    slot, block = b % 16, b - b % 16
    at = (b // 16) * ns + s
    ways = [((block + flip(slot, j), s), None) for j in range(1, 16)]
    for j in range(1, nb // 16 * ns):
        to = flip(at, j)
        ways.append((((to // ns) * 16 + slot, to % ns), None))
    return ways


CUTS = 2


def backward_kernel(nb, ns, rank, size, tile, layout, q_ref, k_ref, v_ref, o_ref, g_ref, lse_ref, top_hbm, x_hbm, gain_ref,
                    rg_hbm, low_hbm, wq_hbm, wk_hbm, wv_hbm, qd_ref, qu_ref, vd_ref, vu_ref, top_out, out_hbm, sum_ref,
                    dqt, stage, xs, rgs, ds, wqs, wks, wvs, lows, outs, gds, gqs, gvs, mine, first, second, summed,
                    tops, xhs, lgs, down_ref, upq_ref, upv_ref,
                    load, dsend, drecv, osend, orecv, tsend, trecv, ssend, srecv):
    docs, rows, d = x_hbm.shape
    w = d // ns
    p = Place(nb, ns)
    doc, pair = pl.program_id(0), pl.program_id(1)
    pairs = w // 128
    loads = [pltpu.make_async_copy(a, v, load.at[n]) for n, (a, v) in enumerate(
        ((wq_hbm, wqs), (wk_hbm, wks), (wv_hbm, wvs), (low_hbm, lows), (x_hbm, xs), (rg_hbm, rgs)))]

    def away(t, i, r, n):
        at = pl.ds(pl.multiple_of(n * 128, 128), 128)
        return pltpu.make_async_remote_copy(
            src_ref=stage.at[i, t, flip(p.part, r), :, at], dst_ref=ds.at[t, p.part, i, :, at], send_sem=dsend.at[t, i, r, n],
            recv_sem=drecv.at[t, i, r, n], device_id=p.peer(r), device_id_type=MESH)

    cut = rows // CUTS

    def out_away(i, n):
        at = pl.ds(pl.multiple_of(n * cut, cut), cut)
        return pltpu.make_async_remote_copy(
            src_ref=outs.at[i, at], dst_ref=out_hbm.at[i, at], send_sem=osend.at[i, n], recv_sem=orecv.at[i, n],
            device_id=p.partner, device_id_type=MESH)

    def out_home(i, n):
        at = pl.ds(pl.multiple_of(n * cut, cut), cut)
        return pltpu.make_async_copy(outs.at[i, at], out_hbm.at[i, at], orecv.at[i, n])

    def top_away(i):
        return pltpu.make_async_remote_copy(
            src_ref=top_hbm.at[i], dst_ref=top_out.at[i], send_sem=tsend.at[i], recv_sem=trecv.at[i],
            device_id=p.partner, device_id_type=MESH)

    top_in = pltpu.make_async_copy(top_hbm, tops, tsend.at[0])
    top_home = pltpu.make_async_copy(tops, top_out, trecv.at[0])
    ways = [(p.peer(r), None) for r in range(1, ns)] + [(p.partner, jnp.logical_not(p.stays))] + sum_ways(p)
    total = DeviceSum(p, mine, first, second, summed, ssend, srecv)

    @pl.when((doc == 0) & (pair == 0))
    def _():
        p.hello(ways)
        for copy in loads:
            copy.start()
        pl.when(p.stays)(lambda: top_in.start())
        down_ref[...] = down_maps(qd_ref[...], vd_ref[...])
        upq_ref[...] = up_map(qu_ref[...], 0)
        upv_ref[...] = up_map(vu_ref[...], rank)
        gds[...] = jnp.zeros_like(gds)
        gqs[...] = jnp.zeros_like(gqs)
        gvs[...] = jnp.zeros_like(gvs)

    @pl.when(doc < docs)
    def _():
        attention_gradients(layout, q_ref, k_ref, v_ref, o_ref, g_ref, lse_ref, stage, dqt, doc, pair, size, tile)

        @pl.when((doc == 0) & (pair == 0))
        def _():
            p.met(ways)
            pl.when(p.stays)(lambda: top_in.wait())
            pl.when(p.stays)(lambda: top_home.start())
            for i in range(docs):
                pl.when(jnp.logical_not(p.stays))(lambda i=i: top_away(i).start())

        for t in range(3):
            for r in range(1, ns):
                away(t, doc, r, pair).start()

    @pl.when((doc > 0) & (pair == 0))
    def _():
        i = doc - 1

        @pl.when(i == 0)
        def _():
            for copy in loads:
                copy.wait()

        for t in range(3):
            for r in range(1, ns):
                for n in range(pairs):
                    away(t, i, r, n).wait()

        xh, inv = normalise(xs[i].astype(F32))
        xhs[:, :d] = xh
        xhs[:, d:] = jnp.broadcast_to(inv, (rows, 128))
        lg = jnp.zeros((rows, 128), F32)
        for r in range(ns):
            g = flip(p.part, r)
            cols = pl.ds(pl.multiple_of(g * w, w), w)
            for t, up, grads in ((0, upq_ref, gqs), (2, upv_ref, gvs)):
                piece = ds[t, g, i] if r else stage[i, t, p.part]
                lg = lg + dot(piece, up[:, cols], NT)
                grads[:, cols] += dot(lows[i], piece, TN)
        lgs[...] = lg.astype(BF)
        gds[...] += dot(lgs[...], (xh * gain_ref[...]).astype(BF), TN)

        @pl.when(i == docs - 1)
        def _():
            upper = lax.broadcasted_iota(jnp.int32, (2 * rank, 1), 0) < rank
            both = jnp.where(upper, gqs[:2 * rank, :], gvs[:2 * rank, :]) * ADAPTER_SCALE
            for n in range(8):
                mine[n] = gds[:8, n * 128:(n + 1) * 128]
                mine[8 + n] = both[:, n * 128:(n + 1) * 128]
            total.begin()

        def some_rows(n, carry):
            at = pl.ds(pl.multiple_of(n * cut, cut), cut)
            fg = dot(lgs[at, :], down_ref[...], NT)
            for r in range(ns):
                g = flip(p.part, r)
                cols = pl.ds(pl.multiple_of(g * w, w), w)
                for t, full in enumerate((wqs, wks, wvs)):
                    piece = ds[t, g, i, at, :] if r else stage[i, t, p.part, at, :]
                    fg = fg + dot(piece, full[:, :, cols].reshape(d, w), NT)
            outs[i, at, :] = (rgs[i, at, :] + norm_back(xhs[at, :d], xhs[at, d:d + 1], gain_ref[...], fg)).astype(BF)
            pl.when(p.stays)(lambda: out_home(i, n).start())
            pl.when(jnp.logical_not(p.stays))(lambda: out_away(i, n).start())
            pl.when((i == docs - 1) & (n == 0))(total.middle)
            return carry

        lax.fori_loop(0, CUTS, some_rows, 0)
        pl.when(i == docs - 1)(total.end)

    @pl.when((doc == docs) & (pair == pairs - 1))
    def _():
        total.finish()
        sum_ref[...] = summed[...]
        pl.when(p.stays)(lambda: top_home.wait())
        for i in range(docs):
            for n in range(CUTS):
                pl.when(p.stays)(lambda i=i, n=n: out_home(i, n).wait())
                pl.when(jnp.logical_not(p.stays))(lambda i=i, n=n: out_away(i, n).wait())
            pl.when(jnp.logical_not(p.stays))(lambda i=i: top_away(i).wait())


def attention_gradients(layout, q_ref, k_ref, v_ref, o_ref, g_ref, lse_ref, stage, dqt, doc, pair, size, tile):
    parts, rows = o_ref.shape[0], o_ref.shape[2]
    n = parts * rows
    blocks, per = n // size, rows // size
    q = picked(q_ref.at[0], layout, blocks, size)
    k = picked(k_ref.at[0], layout, blocks, size)
    v = picked(v_ref.at[0], layout, blocks, size)
    o = picked(o_ref, layout, blocks, size)
    g = picked(g_ref, layout, blocks, size)
    kt = k.T
    lane = lax.broadcasted_iota(jnp.int32, (1, 128), 1)
    c = SCORE_SCALE * LOG2E
    tri = lax.broadcasted_iota(jnp.int32, (tile, tile), 0) <= lax.broadcasted_iota(jnp.int32, (tile, tile), 1)
    prod = (o.astype(F32) * g.astype(F32)).astype(BF)
    heads = (lax.broadcasted_iota(jnp.int32, (8, 128), 1) // 64 == lax.broadcasted_iota(jnp.int32, (8, 128), 0)).astype(BF)
    delta = dot(heads, prod, NT)
    zero = jnp.zeros((), BF)
    masks = [(lane < 64) == (h == 0) for h in range(2)]
    qms = [jnp.where(mk, q, zero) for mk in masks]
    gms = [jnp.where(mk, g, zero) for mk in masks]
    lse = lse_ref[0, 0]
    dks, dvs = [], []
    work = [(j, h) for j in range(n // tile) for h in range(2)]

    def products(j, h):
        lo, hi = j * tile, (j + 1) * tile
        return dot(k[lo:hi], qms[h][lo:], NT), dot(v[lo:hi], gms[h][lo:], NT)

    waiting = []
    sums = {}

    def settle():
        j, h, p, ds = waiting.pop(0)
        lo, hi = j * tile, (j + 1) * tile
        dv = dot(p, gms[h][lo:])
        dk = dot(ds, qms[h][lo:])
        dq = dot(kt[64 * h:64 * h + 64, lo:hi], ds)
        if j == 0:
            dqt[64 * h:64 * h + 64, :] = dq
        else:
            dqt[64 * h:64 * h + 64, lo:] += dq
        if h == 0:
            sums[j] = dk, dv
        else:
            dks.append(((sums[j][0] + dk) * SCORE_SCALE).astype(BF))
            dvs.append((sums[j][1] + dv).astype(BF))

    ahead = products(*work[0])
    for t, (j, h) in enumerate(work):
        st, dp = ahead
        if t + 1 < len(work):
            ahead = products(*work[t + 1])
        lo, hi = j * tile, (j + 1) * tile
        p = jnp.exp2(st * c - lse[h:h + 1, lo:])
        diag = jnp.where(tri, p[:, :tile], 0.0)
        p = diag if hi == n else jnp.concatenate([diag, p[:, tile:]], axis=1)
        waiting.append((j, h, p.astype(BF), (p * (dp - delta[h:h + 1, lo:])).astype(BF)))
        if t:
            settle()
    settle()
    lanes = pl.ds(pl.multiple_of(pair * 128, 128), 128)
    for t, value in enumerate(((dqt[...] * SCORE_SCALE).T.astype(BF), jnp.concatenate(dks, axis=0),
                               jnp.concatenate(dvs, axis=0))):
        def store(b, piece, t=t):
            stage[doc, t, b // per, b % per * size:(b % per + 1) * size, lanes] = piece
        put_back(value, layout, blocks, size, store)


def backward(nb, ns, rank, layout, qkv, o, g, lse, top, x, gain, rg, low, wq, wk, wv, adapters, size, tile=256):
    docs, rows, d = x.shape
    parts = o.shape[0]
    w = d // ns
    n = parts * rows
    any_spec = pl.BlockSpec(memory_space=pl.ANY)
    vmem = pl.BlockSpec(memory_space=pltpu.VMEM)
    dma = pltpu.SemaphoreType.DMA
    many = max(16, nb // 16 * ns)
    spec = pl.BlockSpec((parts, 1, rows, 128), lambda i, j: (0, jnp.minimum(i, docs - 1), 0, j))
    row = jax.ShapeDtypeStruct(x.shape, BF)

    def third(t):
        return pl.BlockSpec((1, parts, 1, rows, 128), lambda i, j: (t, 0, jnp.minimum(i, docs - 1), 0, j))

    return pl.pallas_call(
        functools.partial(backward_kernel, nb, ns, rank, size, tile),
        grid=(docs + 1, w // 128),
        in_specs=[pl.BlockSpec(memory_space=pltpu.SMEM), third(0), third(1), third(2), spec, spec]
        + [pl.BlockSpec((1, 1, 2, n), lambda i, j: (jnp.minimum(i, docs - 1), j, 0, 0))]
        + [any_spec] * 2 + [vmem] + [any_spec] * 5 + [vmem] * 4,
        out_specs=[any_spec, any_spec, vmem],
        out_shape=[row, row, jax.ShapeDtypeStruct((16, 8, 128), F32)],
        scratch_shapes=[pltpu.VMEM((128, n), F32), pltpu.VMEM((docs, 3, parts, rows, w), BF),
                        pltpu.VMEM(x.shape, BF), pltpu.VMEM(x.shape, F32), pltpu.VMEM((3, ns, docs, rows, w), BF)]
        + [pltpu.VMEM(wq.shape, BF)] * 3
        + [pltpu.VMEM(low.shape, BF), pltpu.VMEM(x.shape, BF)] + [pltpu.VMEM((128, d), F32)] * 3
        + [pltpu.VMEM((16, 8, 128), F32), pltpu.VMEM((16, 8, 128), F32), pltpu.VMEM((nb // 16 * ns, 8, 128), F32),
           pltpu.VMEM((16, 8, 128), F32),
           pltpu.VMEM(x.shape, BF), pltpu.VMEM((rows, d + 128), F32), pltpu.VMEM((rows, 128), BF),
           pltpu.VMEM((d, 128), BF), pltpu.VMEM((128, d), BF), pltpu.VMEM((128, d), BF),
           dma((6,)), dma((3, docs, ns, w // 128)), dma((3, docs, ns, w // 128)), dma((docs, CUTS)), dma((docs, CUTS)), dma((docs,)), dma((docs,)),
           dma((3, many)), dma((3, many))],
        compiler_params=pltpu.CompilerParams(collective_id=3, has_side_effects=True, vmem_limit_bytes=62 << 20),
        name="backward",
    )(layout, qkv, qkv, qkv, o, g, lse, top, x, gain, rg, low, wq, wk, wv, *adapters)


def hand_out_kernel(a_ref, b_ref, a_out, b_out):
    a_out[...] = a_ref[...]
    b_out[...] = b_ref[...]


def hand_out(a, b):
    docs, rows, d = a.shape
    cut = min(rows, 256)
    spec = pl.BlockSpec((1, cut, d), lambda i, j: (i, j, 0))
    return pl.pallas_call(
        hand_out_kernel,
        grid=(docs, rows // cut),
        in_specs=[spec, spec],
        out_specs=[spec, spec],
        out_shape=[jax.ShapeDtypeStruct(a.shape, a.dtype), jax.ShapeDtypeStruct(b.shape, b.dtype)],
        name="hand_out",
    )(a, b)


def local(
    nb, ns,
    tokens, cotangent, layout, attention_norm_gain, feedforward_norm_gain,
    query_weight, key_weight, value_weight, attention_output_weight, up_weight, down_weight,
    query_down_adapter, query_up_adapter, value_down_adapter, value_up_adapter,
):
    docs, rows, d = tokens.shape
    size = rows * ns // layout.shape[0]
    rank = query_up_adapter.shape[0]
    adapters = (query_down_adapter.T, query_up_adapter, value_down_adapter.T, value_up_adapter)
    gain1 = attention_norm_gain[None]
    gain2 = feedforward_norm_gain[None]

    qkv, att, mixed, lse, low, x, cot, wq, wk, wv, wo, w_up = front(
        nb, ns, layout, tokens, cotangent, query_weight, key_weight, value_weight, attention_output_weight, up_weight,
        gain1, adapters, size)
    out, rg, mix = middle(nb, ns, x, mixed, cotangent, cot, gain2, wo.reshape(d, d), w_up, down_weight)
    layer_out, input_grad, sums = backward(
        nb, ns, rank, layout, qkv, att, mix, lse, out, x, gain1, rg, low, wq, wk, wv, adapters, size)
    layer_out, input_grad = hand_out(layer_out, input_grad)
    sums = sums.reshape(2, d // 128, 2 * rank, 128).transpose(0, 2, 1, 3).reshape(2, 2 * rank, d)
    return (layer_out, input_grad, sums[0, :rank].T, sums[1, :rank], sums[0, rank:].T, sums[1, rank:])


def solution(mesh):
    spec = P("batch", "seq", None)
    weight = P("batch", None)
    return jax.shard_map(
        functools.partial(local, mesh.shape["batch"], mesh.shape["seq"]),
        mesh=mesh,
        in_specs=(spec, spec, P(), P(), P()) + (weight,) * 6 + (P(),) * 4,
        out_specs=(spec, spec, P(), P(), P(), P()),
        check_vma=False,
    )
```
